32 devices in a mesh: dp: 4 (over x, core), fsdp: 8 (over z, y).
Axes of the slice: x: 2, y: 2, z: 4, core: 2. Of those that a mesh axis runs over, the one named last changes fastest.
Arguments:
- tokens: float32 [12288, 768], P(('dp', 'fsdp')), may hold values from -6 to 6
- sensor_tag: int32 [32], P(('dp', 'fsdp')), may hold values from 0 to 6
- block_dest: int32 [12288, 1], P(('dp', 'fsdp')), may hold values from 0 to 7; in each aligned block of 384 rows (0 to 383, 384 to 767, ...) at most 96 rows name the same one
- block_order: int32 [32, 1536], P(('dp', 'fsdp')), may hold values from 0 to 1535, each once within a row
- sensor_table: float32 [7, 768], replicated, may hold values from -6 to 6
- encoder_gains: float32 [2, 768], replicated, may hold values from 0.5 to 1.5
- encoder_attend: float32 [768, 2304], P('fsdp', 'dp'), may hold values from -0.21875 to 0.21875
- encoder_merge: float32 [768, 768], P('fsdp', 'dp'), may hold values from -2.5 to 2.5
- encoder_expand: float32 [768, 3072], P('fsdp', 'dp'), may hold values from -0.21875 to 0.21875
- encoder_reduce: float32 [3072, 768], P('fsdp', 'dp'), may hold values from -0.109375 to 0.109375
- bridge: float32 [768, 512], P('fsdp', 'dp'), may hold values from -0.21875 to 0.21875
- mask_token: float32 [512], replicated, may hold values from -6 to 6
- decoder_gains: float32 [2, 512], replicated, may hold values from 0.5 to 1.5
- decoder_attend: float32 [512, 768], P('fsdp', 'dp'), may hold values from -0.25 to 0.25
- decoder_merge: float32 [256, 512], P('fsdp', 'dp'), may hold values from -6 to 6
- decoder_expand: float32 [512, 2048], P('fsdp', 'dp'), may hold values from -0.25 to 0.25
- decoder_reduce: float32 [2048, 512], P('fsdp', 'dp'), may hold values from -0.125 to 0.125
- cotangent: float32 [49152, 512], P(('dp', 'fsdp')), may hold values from -6 to 6
Outputs:
- decoded: float32 [49152, 512], P(('dp', 'fsdp'))
- tokens_grad: float32 [12288, 768], P(('dp', 'fsdp'))
- table_grad: float32 [7, 768], replicated
- encoder_gains_grad: float32 [2, 768], replicated
- encoder_attend_grad: float32 [768, 2304], P('fsdp', 'dp')
- encoder_merge_grad: float32 [768, 768], P('fsdp', 'dp')
- encoder_expand_grad: float32 [768, 3072], P('fsdp', 'dp')
- encoder_reduce_grad: float32 [3072, 768], P('fsdp', 'dp')
- bridge_grad: float32 [768, 512], P('fsdp', 'dp')
- mask_grad: float32 [512], replicated
- decoder_gains_grad: float32 [2, 512], replicated
- decoder_attend_grad: float32 [512, 768], P('fsdp', 'dp')
- decoder_merge_grad: float32 [256, 512], P('fsdp', 'dp')
- decoder_expand_grad: float32 [512, 2048], P('fsdp', 'dp')
- decoder_reduce_grad: float32 [2048, 512], P('fsdp', 'dp')
The draws below stay inside these ranges and needn't reach their ends.
Inputs may be any that keep to these rules, and one draw needn't show every extreme that they name: `block_dest`: on each device, the 384 rows name any fsdp index at most 96 times, a bound that some block reaches; every index is named somewhere. `block_order`: each row is an ordering of the positions 0 to 1535 of the spatial block of that device.
All inputs are finite; a program needn't handle non-finite values.
Results may differ from the reference program's by a relative error of at most 0.0003.
Values sent between devices are 32-bit elements; how exact they have to be, the bound alone decides.
A program may use at most 256 MiB of HBM per device.

```python
import math
from functools import partial
import jax
import jax.numpy as jnp
import numpy as np
from jax import lax

ENC = 768
HEADS_E = 12
FF_E = 3072
DEC = 512
HEADS_D = 4
FF_D = 2048
SENSORS = 7
VIS = 384
DEC_INNER = 256
BLK = 1536
CAP = 96
GROUPS = 32
VIS_ALL = 12288
BLK_ALL = 49152
N_DP = 4
N_FSDP = 8


def plant(array, key, smallest, high):
    place = [jax.random.randint(jax.random.fold_in(key, axis), (), 0, length) for axis, length in enumerate(array.shape)]
    main_axis = array.shape.index(max(array.shape))
    next_to = place[:main_axis] + [(place[main_axis] + 1) % array.shape[main_axis]] + place[main_axis + 1:]
    return array.at[tuple(place)].set(smallest).at[tuple(next_to)].set(high)


def steps_of(own_key, dims, shards, smallest, high):
    gain, own = 1.0, jax.random.fold_in(own_key, 6)
    for axis_at, parts in shards:
        draws = jnp.exp(jax.random.uniform(jax.random.fold_in(own, axis_at), (parts,), jnp.float32, smallest / len(shards), high / len(shards)))
        gain = gain * jnp.repeat(draws, dims[axis_at] // parts).reshape([-1 if axis == axis_at else 1 for axis in range(len(dims))])
    return gain


def cumulative_ranks(amount, slope):
    weights = [(1 << 20) // math.isqrt(grade ** slope) + 1 for grade in range(1, amount + 1)]
    spread = 1 + sum(weights) // (1 << 30)
    return np.cumsum(np.array([max(1, weight // spread) for weight in weights]))


def ranked_ids(rng, shape, amount, slope):
    table = cumulative_ranks(amount, slope)
    ticket = jax.random.randint(jax.random.fold_in(rng, 1), shape, 0, int(table[amount - 1]))
    rank = jnp.searchsorted(jnp.asarray(table, jnp.int32), ticket, side="right")
    return jax.random.permutation(jax.random.fold_in(rng, 2), amount)[rank].astype(jnp.int32)


def assign_block(key, own, number, rows, number_of, top, most, skew):
    sequence = jax.random.permutation(key, number_of)
    heavy_load, common = load_shares(number_of, rows * top, most, skew, True), load_shares(number_of, rows * top, most, skew, False)
    places = jnp.arange(number_of)

    def named(lengths, turn):
        used = int((lengths > 0).sum())
        fixed = max(1, used // 4)
        moved = fixed + (places - fixed + turn * (used - fixed)) % max(1, number_of - fixed)
        return jnp.zeros((number_of,), jnp.int32).at[sequence[jnp.where(places < fixed, places, moved)]].set(jnp.asarray(lengths, jnp.int32))

    lengths = jnp.where(number % 4 == 0, named(heavy_load, number // 4), named(common, number - number // 4 - 1))
    mixed = jax.random.permutation(jax.random.fold_in(own, 3), number_of)
    giver, receiver = mixed[0:number_of // 2 * 2:2], mixed[1:number_of // 2 * 2:2]
    margin = jnp.minimum(lengths[giver] - 1, most - lengths[receiver]) // 2
    margin = jnp.where((giver == sequence[0]) | (receiver == sequence[0]) | (lengths[receiver] == 0), 0, jnp.maximum(margin, 0))
    moved = jax.random.randint(jax.random.fold_in(own, 4), (number_of // 2,), 0, 1 << 20) % (margin + 1)
    lengths = lengths.at[giver].add(-moved).at[receiver].add(moved)
    labels = jnp.searchsorted(jnp.cumsum(lengths), jnp.arange(rows * top), side="right").astype(jnp.int32)
    table = labels.reshape(top, rows).T
    table = table[jax.random.permutation(jax.random.fold_in(own, 1), rows)]
    turn = jax.random.randint(jax.random.fold_in(own, 2), (rows, 1), 0, top)
    return jnp.take_along_axis(table, (jnp.arange(top)[None, :] + turn) % top, axis=1)


def load_shares(amount, total, bound, skew, full):
    portions = [(1 << 20) // math.isqrt(rank ** skew) + 1 for rank in range(1, amount + 1)]
    largest = bound if full else min(bound, max(-(-total // amount), total * portions[0] // sum(portions)))
    least = 1 if total - largest >= amount - 1 else 0
    counts, rest = [largest] + [least] * (amount - 1), total - largest - least * (amount - 1)
    while rest > 0:
        candidates = [i for i in range(1, amount) if counts[i] < largest] or [i for i in range(1, amount) if counts[i] < bound]
        whole, left = sum([portions[i] for i in candidates]), rest
        for i in candidates:
            addition = min(bound - counts[i], max(1, left * portions[i] // whole), rest)
            counts[i] = counts[i] + addition
            rest = rest - addition
    return np.array(counts)


def centred(own_key, extent, scale, reach, pieces=(), held_as=jnp.bfloat16):
    array = jax.random.normal(own_key, extent, jnp.float32) * scale
    if len(pieces) > 0:
        array = steps_of(own_key, extent, pieces, -0.22, 0.18) * array
    return jnp.clip(array, min=-reach, max=reach).astype(held_as)


def setup_inputs(seed: int = 0) -> dict:
    arg_keys = jax.random.split(jax.random.key(seed), 19)
    tokens = centred(arg_keys[0], (VIS_ALL, ENC), 1.0, 6.0, ((0, 32),), jnp.float32)
    sensor_tag = plant(ranked_ids(arg_keys[1], (GROUPS,), SENSORS, 2), jax.random.fold_in(arg_keys[1], 3), 0, SENSORS - 1).astype(jnp.int32)
    block_dest_keys = jax.random.split(jax.random.fold_in(arg_keys[2], 1), VIS_ALL // VIS)
    block_dest_turns = jax.random.permutation(jax.random.fold_in(arg_keys[2], 3), VIS_ALL // VIS)
    block_dest = jax.vmap(lambda own, number: assign_block(jax.random.fold_in(arg_keys[2], 2), own, number, VIS, N_FSDP, 1, CAP, 2))(block_dest_keys, block_dest_turns).reshape((VIS_ALL, 1))
    block_order = jax.vmap(lambda own: jax.random.permutation(own, BLK))(jax.random.split(arg_keys[3], GROUPS)).reshape((GROUPS, BLK)).astype(jnp.int32)
    sensor_table = centred(arg_keys[4], (SENSORS, ENC), 1.0, 6.0, (), jnp.float32)
    encoder_gains = jnp.clip(1.0 + 0.1 * jax.random.normal(arg_keys[5], (2, ENC), jnp.float32), 0.5, 1.5)
    encoder_attend = centred(arg_keys[6], (ENC, 3 * ENC), ENC ** -0.5, 0.21875, ((0, 8), (1, 4)), jnp.float32)
    encoder_merge = centred(arg_keys[7], (ENC, ENC), (max(ENC * 3 // VIS, 1)) ** -0.5, 2.5, ((0, 8), (1, 4)), jnp.float32)
    encoder_expand = centred(arg_keys[8], (ENC, FF_E), ENC ** -0.5, 0.21875, ((0, 8), (1, 4)), jnp.float32)
    encoder_reduce = centred(arg_keys[9], (FF_E, ENC), FF_E ** -0.5, 0.109375, ((0, 8), (1, 4)), jnp.float32)
    bridge = centred(arg_keys[10], (ENC, DEC), ENC ** -0.5, 0.21875, ((0, 8), (1, 4)), jnp.float32)
    mask_token = centred(arg_keys[11], (DEC,), 1.0, 6.0, (), jnp.float32)
    decoder_gains = jnp.clip(1.0 + 0.1 * jax.random.normal(arg_keys[12], (2, DEC), jnp.float32), 0.5, 1.5)
    decoder_attend = centred(arg_keys[13], (DEC, 3 * DEC_INNER), DEC ** -0.5, 0.25, ((0, 8), (1, 4)), jnp.float32)
    decoder_merge = centred(arg_keys[14], (DEC_INNER, DEC), (max(DEC_INNER * 3 // BLK, 1)) ** -0.5, 6.0, ((0, 8), (1, 4)), jnp.float32)
    decoder_expand = centred(arg_keys[15], (DEC, FF_D), DEC ** -0.5, 0.25, ((0, 8), (1, 4)), jnp.float32)
    decoder_reduce = centred(arg_keys[16], (FF_D, DEC), FF_D ** -0.5, 0.125, ((0, 8), (1, 4)), jnp.float32)
    cotangent = centred(arg_keys[17], (BLK_ALL, DEC), 1.0, 6.0, ((0, 32),), jnp.float32)
    return dict(tokens=tokens, sensor_tag=sensor_tag, block_dest=block_dest, block_order=block_order, sensor_table=sensor_table, encoder_gains=encoder_gains, encoder_attend=encoder_attend, encoder_merge=encoder_merge, encoder_expand=encoder_expand, encoder_reduce=encoder_reduce, bridge=bridge, mask_token=mask_token, decoder_gains=decoder_gains, decoder_attend=decoder_attend, decoder_merge=decoder_merge, decoder_expand=decoder_expand, decoder_reduce=decoder_reduce, cotangent=cotangent)


@jax.custom_vjp
def low(v):
    return lax.optimization_barrier(v.astype(jnp.bfloat16)).astype(jnp.float32)

@jax.custom_vjp
def low_back(v):
    return v

def low_keep(v):
    return (low(v), None)

def low_pass(kept, grad):
    return (grad,)

def back_keep(v):
    return (v, None)

def back_low(kept, grad):
    return (low(grad),)
low.defvjp(low_keep, low_pass)
low_back.defvjp(back_keep, back_low)
precise = lax.Precision.HIGHEST

def product(operand, factor):
    return jnp.dot(operand, factor, precision=precise, preferred_element_type=jnp.float32)

def normalize(values, gain_row):
    center = values - lax.optimization_barrier(jnp.mean(values, axis=-1, keepdims=True))
    inverse = lax.rsqrt(lax.optimization_barrier(jnp.mean(center * center, axis=-1, keepdims=True)) + 1e-06)
    return center * inverse * gain_row

def attend(packed, head_count):
    row_count = packed.shape[0]
    breadth = packed.shape[1] // 3
    head_size = breadth // head_count
    row_block = min(row_count, 512)
    queries = packed[:, :breadth].reshape(row_count // row_block, row_block, head_count, head_size)
    key_rows = packed[:, breadth:2 * breadth].reshape(row_count, head_count, head_size)
    value_rows = packed[:, 2 * breadth:].reshape(row_count, head_count, head_size)

    def one_block(block_queries):
        scores = jnp.einsum('qhd,khd->hqk', block_queries, key_rows, precision=precise) / math.sqrt(head_size)
        weights = jax.nn.softmax(scores, axis=-1)
        return jnp.einsum('hqk,khd->qhd', weights, value_rows, precision=precise)
    mixture = lax.map(jax.checkpoint(one_block), queries)
    return mixture.reshape(row_count, breadth)

def position_table(length, breadth):
    half_width = breadth // 2
    indices = jnp.arange(length, dtype=jnp.float32)[:, None]
    frequency = jnp.exp(jnp.arange(half_width, dtype=jnp.float32) * (-math.log(10000.0) / half_width))[None, :]
    angles = indices * frequency
    return jnp.concatenate([jnp.sin(angles), jnp.cos(angles)], axis=1)

def residual_block(states, gain_pair, attend_weight, merge_weight, expand_weight, reduce_weight, head_count):
    first_norm = normalize(states, gain_pair[0])
    middle = states + product(attend(product(first_norm, attend_weight), head_count), merge_weight)
    second_norm = normalize(middle, gain_pair[1])
    active = jax.nn.gelu(product(second_norm, expand_weight), approximate=False)
    return middle + product(active, reduce_weight)

def reference(tokens, sensor_tag, block_dest, block_order, sensor_table, encoder_gains, encoder_attend, encoder_merge, encoder_expand, encoder_reduce, bridge, mask_token, decoder_gains, decoder_attend, decoder_merge, decoder_expand, decoder_reduce, cotangent):
    devices = N_DP * N_FSDP
    capacity = 2 * VIS // N_FSDP
    destination = block_dest.reshape(devices, VIS).astype(jnp.int32)
    chooser = (destination[:, :, None] == jnp.arange(N_FSDP, dtype=jnp.int32)[None, None, :]).astype(jnp.int32)
    ranking = lax.optimization_barrier(jnp.sum((jnp.cumsum(chooser, axis=1) - chooser) * chooser, axis=2)).astype(jnp.int32)
    device_ids = jnp.arange(devices, dtype=jnp.int32)
    source = (device_ids % N_FSDP)[:, None]
    target = (device_ids // N_FSDP)[:, None] * N_FSDP + destination
    offset = block_order[target, source * capacity + ranking].astype(jnp.int32)
    spots = (target * BLK + offset).reshape(-1).astype(jnp.int32)
    covered = jnp.zeros((devices * BLK,), jnp.float32).at[spots].set(1.0)[:, None]
    tag_rows = (sensor_tag[:, None] == jnp.arange(SENSORS, dtype=jnp.int32)[None, :]).astype(jnp.float32)
    positions = position_table(BLK, DEC)

    def forward(tokens, sensor_table, encoder_gains, encoder_attend, encoder_merge, encoder_expand, encoder_reduce, bridge, mask_token, decoder_gains, decoder_attend, decoder_merge, decoder_expand, decoder_reduce):
        initial = tokens.reshape(devices, VIS, ENC) + product(tag_rows, sensor_table)[:, None, :]
        encoder = jax.checkpoint(partial(residual_block, gain_pair=encoder_gains, attend_weight=encoder_attend, merge_weight=encoder_merge, expand_weight=encoder_expand, reduce_weight=encoder_reduce, head_count=HEADS_E))
        encoded = lax.map(encoder, initial).reshape(devices * VIS, ENC)
        projected = product(encoded, bridge)
        scattered = jnp.zeros((devices * BLK, DEC), jnp.float32).at[spots].set(projected)
        filled = (scattered + (1.0 - covered) * mask_token).reshape(devices, BLK, DEC) + positions
        decoder = jax.checkpoint(partial(residual_block, gain_pair=decoder_gains, attend_weight=decoder_attend, merge_weight=decoder_merge, expand_weight=decoder_expand, reduce_weight=decoder_reduce, head_count=HEADS_D))
        return lax.map(decoder, filled).reshape(devices * BLK, DEC)
    decoded, backward = jax.vjp(forward, tokens, sensor_table, encoder_gains, encoder_attend, encoder_merge, encoder_expand, encoder_reduce, bridge, mask_token, decoder_gains, decoder_attend, decoder_merge, decoder_expand, decoder_reduce)
    gradients = backward(cotangent)
    return (decoded, gradients[0], gradients[1], gradients[2], gradients[3], gradients[4], gradients[5], gradients[6], gradients[7], gradients[8], gradients[9], gradients[10], gradients[11], gradients[12], gradients[13])
```

```python
from functools import partial
import math

import jax
import jax.numpy as jnp
from jax import lax
from jax.experimental import pallas as pl
from jax.experimental.pallas import tpu as pltpu
from jax.sharding import PartitionSpec as P

MESH = pl.DeviceIdType.MESH
VMEM = pltpu.VMEM
LONG = (("b", "a", "x"), ("x", "a", "b"))
SHORT = (("a", "x", "b"), ("a", "b", "x"))
TURNS = (LONG, LONG, SHORT)
AHEAD = 2


class Grid:
    def __init__(self, dp, fsdp):
        self.size = {"x": dp // 2, "a": 4, "b": fsdp // 4}
        column, row = lax.axis_index("dp"), lax.axis_index("fsdp")
        self.core = lax.rem(column, 2)
        self.at = {
            "x": lax.div(column, 2),
            "a": lax.div(row, self.size["b"]),
            "b": lax.rem(row, self.size["b"]),
        }

    def device(self, core=None, **moved):
        at = {**self.at, **moved}
        core = self.core if core is None else core
        return (at["x"] * 2 + core, at["a"] * self.size["b"] + at["b"])

    def greet(self, reach):
        barrier = pltpu.get_barrier_semaphore()
        pl.semaphore_signal(
            barrier, inc=1, device_id=self.device(1 - self.core), device_id_type=MESH
        )
        count = 1
        for axis, size in self.size.items():
            here = self.at[axis]
            for move in range(-min(reach, size - 1), min(reach, size - 1) + 1):
                if move:
                    exists = together(here + move >= 0, here + move < size)
                    count = count + jnp.where(exists, 1, 0)

                    @pl.when(exists)
                    def _(axis=axis, here=here, move=move):
                        pl.semaphore_signal(
                            barrier,
                            inc=1,
                            device_id=self.device(**{axis: here + move}),
                            device_id_type=MESH,
                        )

        pl.semaphore_wait(barrier, count)


def plan_rounds(shapes, target):
    plan, turn = [], 0
    for rows, columns in shapes:
        units = rows // 16
        pairs = max(1, min(units // 2, round(units * 8 * columns * 2 / target)))
        parts, start = [], 0
        for pair in range(pairs):
            orders = TURNS[turn % len(TURNS)]
            for place, order in enumerate(orders):
                left = 2 * (pairs - pair) - place
                take = -(-(units - start) // left)
                if take:
                    parts.append((order, start * 8, take * 8, turn))
                start += take
            turn += 1
        plan.append(parts)
    return plan


def together(*conditions):
    joined = conditions[0]
    for condition in conditions[1:]:
        joined = jnp.logical_and(joined, condition)
    return joined


class Traffic:
    def __init__(self, grid, send, receive):
        self.grid, self.send, self.receive = grid, send, receive
        self.count, self.open = 0, []

    def copy(self, source, target, device, starts, arrives):
        place = self.count
        self.count += 1

        def made():
            return pltpu.make_async_remote_copy(
                src_ref=source,
                dst_ref=target,
                send_sem=self.send.at[place],
                recv_sem=self.receive.at[place],
                device_id=device,
                device_id_type=MESH,
            )

        if starts is None:
            made().start()
        else:

            @pl.when(starts)
            def _():
                made().start()

        self.open.append((made, starts))
        return (made, arrives)

    def arrive(self, handle):
        made, arrives = handle
        if arrives is None:
            made().wait_recv()
        else:

            @pl.when(arrives)
            def _():
                made().wait_recv()

    def take(self, handle):
        handle[0]().wait_recv()

    def drain(self, handle):
        handle[0]().wait_send()
        self.open = [entry for entry in self.open if entry[0] is not handle[0]]

    def close(self):
        for made, starts in self.open:
            if starts is None:
                made().wait_send()
            else:

                @pl.when(starts)
                def _():
                    made().wait_send()


def block_of(full, chosen, offset, rows, width):
    view = []
    for axis in ("a", "b"):
        place = chosen[axis]
        view.append(slice(None) if place is None else pl.ds(place, 1))
    columns = (
        slice(None)
        if chosen["x"] is None
        else pl.ds(pl.multiple_of(chosen["x"] * width, 128), width)
    )
    return full.at[(*view, pl.ds(pl.multiple_of(offset, 8), rows), columns)]


def gather_line(traffic, axis, chosen, view, exists, arrived):
    grid = traffic.grid
    here, size = grid.at[axis], grid.size[axis]

    def both(condition):
        return condition if exists is None else together(exists, condition)

    arrived({**chosen, axis: here}, exists)
    for step in range(1, size):
        ahead, behind = {**chosen, axis: here - (step - 1)}, {**chosen, axis: here + (step - 1)}
        rightward = traffic.copy(
            view(ahead),
            view(ahead),
            grid.device(**{axis: here + 1}),
            both(together(here + 1 < size, here - (step - 1) >= 0)),
            both(here - step >= 0),
        )
        leftward = traffic.copy(
            view(behind),
            view(behind),
            grid.device(**{axis: here - 1}),
            both(together(here - 1 >= 0, here + (step - 1) < size)),
            both(here + step < size),
        )
        yield
        traffic.arrive(rightward)
        arrived({**chosen, axis: here - step}, both(here - step >= 0))
        traffic.arrive(leftward)
        arrived({**chosen, axis: here + step}, both(here + step < size))


def gather_part(traffic, order, view, spawn, share):
    first, second, third = order
    grid = traffic.grid
    own = dict(grid.at)

    def last(chosen, exists):
        def finish():
            yield from gather_line(traffic, third, chosen, view, exists, lambda *_: None)
            share(view({**chosen, third: None}), exists)

        spawn(finish())

    def begin():
        if grid.size[first] == 2:
            yield from gather_line(traffic, first, own, view, None, lambda *_: None)
            yield from gather_line(traffic, second, {**own, first: None}, view, None, last)
        else:

            def middle(chosen, exists):
                def go():
                    yield from gather_line(traffic, second, chosen, view, exists, lambda *_: None)
                    last({**chosen, second: None}, exists)

                spawn(go())

            yield from gather_line(traffic, first, own, view, None, middle)

    spawn(begin())


def run_rounds(starts):
    active = []

    def spawn(generator):
        try:
            next(generator)
            active.append(generator)
        except StopIteration:
            pass

    for start in starts:
        for begin in start:
            begin(spawn)
        advance_all(active)
    while active:
        advance_all(active)


def advance_all(active):
    for generator in list(active):
        try:
            next(generator)
        except StopIteration:
            active.remove(generator)


def gather_kernel(dp, fsdp, shapes, plan, *refs):
    number = len(shapes)
    shards, wholes = refs[:number], refs[number : 2 * number]
    raws, blocks = refs[2 * number : 3 * number], refs[3 * number : 4 * number]
    send, receive, pair_send, pair_receive, local = refs[4 * number :]
    grid = Grid(dp, fsdp)
    traffic = Traffic(grid, send, receive)
    pair = Traffic(grid, pair_send, pair_receive)
    core, other = grid.core, 1 - grid.core
    sibling = grid.device(other)
    grid.greet(1)
    handles = []
    for index, (rows, columns) in enumerate(shapes):
        half = rows // 2
        theirs = shards[index].at[pl.ds(pl.multiple_of(other * half, 8), half)]
        handles.append(pair.copy(theirs, raws[index], sibling, None, None))
    stores = []
    for index, (rows, columns) in enumerate(shapes):
        half = rows // 2
        pair.arrive(handles[index])
        mine = shards[index][pl.ds(pl.multiple_of(core * half, 8), half), :]
        came = raws[index][...]
        blocks[index][0, 0] = jnp.where(
            core == 0,
            jnp.concatenate([mine, came], axis=1),
            jnp.concatenate([came, mine], axis=1),
        )
        store = pltpu.make_async_copy(
            blocks[index],
            block_of(wholes[index], grid.at, core * half, half, 2 * columns),
            local.at[index],
        )
        store.start()
        stores.append(store)
    for store in stores:
        store.wait()
    pending = []

    def share(piece, exists):
        pending.append(pair.copy(piece, piece, sibling, exists, exists))

    starts = [[] for _ in range(1 + max(part[3] for parts in plan for part in parts))]
    for index, (rows, columns) in enumerate(shapes):
        half = rows // 2
        for order, offset, count, turn in plan[index]:

            def view(chosen, index=index, offset=offset, count=count, half=half, columns=columns):
                return block_of(wholes[index], chosen, core * half + offset, count, 2 * columns)

            starts[turn].append(
                lambda spawn, order=order, view=view: gather_part(
                    traffic, order, view, spawn, share
                )
            )
    run_rounds(starts)
    for handle in pending:
        pair.arrive(handle)
    traffic.close()
    pair.close()


def gather(weights, dp, fsdp, collective_id, target):
    shapes = [weight.shape for weight in weights]
    a, b = 4, fsdp // 4
    plan = plan_rounds(shapes, target)
    total = sum(len(parts) for parts in plan)
    out = [jax.ShapeDtypeStruct((a, b, r, dp * c), jnp.float32) for r, c in shapes]
    vmem = pl.BlockSpec(memory_space=VMEM)
    return pl.pallas_call(
        partial(gather_kernel, dp, fsdp, shapes, plan),
        out_shape=out,
        in_specs=[vmem] * len(shapes),
        out_specs=[pl.BlockSpec(memory_space=pl.ANY)] * len(shapes),
        scratch_shapes=[VMEM((r // 2, c), jnp.float32) for r, c in shapes]
        + [VMEM((1, 1, r // 2, 2 * c), jnp.float32) for r, c in shapes]
        + [
            pltpu.SemaphoreType.DMA((34 * total,)),
            pltpu.SemaphoreType.DMA((34 * total,)),
            pltpu.SemaphoreType.DMA((8 * total + len(shapes),)),
            pltpu.SemaphoreType.DMA((8 * total + len(shapes),)),
            pltpu.SemaphoreType.DMA((len(shapes),)),
        ],
        compiler_params=pltpu.CompilerParams(
            collective_id=collective_id, has_side_effects=True, vmem_limit_bytes=32 << 20
        ),
        name="gather_weights",
    )(*weights)


def landing_shapes(size, order, rows, width):
    chosen, shapes = {"x": size["x"], "a": size["a"], "b": size["b"]}, []
    for axis in reversed(order):
        chosen[axis] = 1
        slots = 1 if size[axis] == 2 else 2 * (size[axis] - 1)
        shapes.append((slots, chosen["a"], chosen["b"], rows, chosen["x"] * width))
    return shapes


def sum_line(traffic, axis, chosen, view, landing):
    grid = traffic.grid
    here, size = grid.at[axis], grid.size[axis]
    ends = size - 1

    def slot(rightward, place):
        if size == 2:
            return 0
        return place - 1 if rightward else ends + place

    def blocks(place):
        return view({**chosen, axis: place})

    def add(rightward, place):
        target = blocks(place)
        target[...] += landing[slot(rightward, place)]

    def send(rightward, place, starts, arrives):
        return traffic.copy(
            blocks(place),
            landing.at[slot(rightward, place)],
            grid.device(**{axis: here + (1 if rightward else -1)}),
            starts,
            arrives,
        )

    first = {}
    for place in range(ends, 0, -1):
        first[True, place] = send(
            True, place, here == 0, here == 1
        )
    for place in range(ends):
        first[False, place] = send(False, place, here == ends, here == ends - 1)
    later = {}
    for step in range(ends - 1):
        yield
        for come in range(1, ends):
            place = ends - step + come - 1
            if come < place <= ends:
                @pl.when(here == come)
                def _(come=come, place=place):
                    traffic.take(first[True, place] if come == 1 else later[True, come - 1, place])
                    add(True, place)

                later[True, come, place] = send(True, place, here == come, here == come + 1)
            come, place = ends - come, ends - place
            if come > place >= 0:

                @pl.when(here == come)
                def _(come=come, place=place):
                    traffic.take(
                        first[False, place] if come == ends - 1 else later[False, come + 1, place]
                    )
                    add(False, place)

                later[False, come, place] = send(False, place, here == come, here == come - 1)
    yield
    for place in range(size):

        @pl.when(here == place)
        def _(place=place):
            if place > 0:
                traffic.take(first[True, place] if place == 1 else later[True, place - 1, place])
                add(True, place)
            if place < ends:
                traffic.take(
                    first[False, place] if place == ends - 1 else later[False, place + 1, place]
                )
                add(False, place)


def sum_part(traffic, order, view, landings):
    chosen = {"x": None, "a": None, "b": None}
    for axis, landing in zip(reversed(order), landings):
        yield from sum_line(traffic, axis, chosen, view, landing)
        chosen[axis] = traffic.grid.at[axis]


def total_everywhere(traffic, pair, value, pair_landing, landings):
    grid = traffic.grid
    came = pair.copy(value, pair_landing, grid.device(1 - grid.core), None, None)
    yield
    pair.arrive(came)
    pair.drain(came)
    value[...] += pair_landing[...]
    for axis, landing in zip(("x", "b", "a"), landings):
        here, size = grid.at[axis], grid.size[axis]
        handles = []
        for move in range(1, size):
            target = lax.rem(here + move, size)
            source = lax.rem(here + size - move, size)
            handles.append(
                (
                    traffic.copy(
                        value, landing.at[here], grid.device(**{axis: target}), None, None
                    ),
                    source,
                )
            )
        landing[here] = value[...]
        yield
        for handle, _ in handles:
            traffic.arrive(handle)
            traffic.drain(handle)
        total = landing[0]
        for place in range(1, size):
            total = total + landing[place]
        value[...] = total


def scatter_kernel(dp, fsdp, shapes, pieces, has_small, *refs):
    number = len(shapes)
    refs = list(refs)

    def take(count):
        taken = refs[:count]
        del refs[:count]
        return taken

    wholes, small = take(number), (take(1)[0] if has_small else None)
    outs, small_out = take(number), (take(1)[0] if has_small else None)
    sums, others, finals = take(number), take(number), take(number)
    landings = [[take(3) for _ in parts] for parts in pieces]
    if has_small:
        small_pair, *small_landings = take(4)
    send, receive, pair_send, pair_receive, local = refs
    grid = Grid(dp, fsdp)
    traffic = Traffic(grid, send, receive)
    pair = Traffic(grid, pair_send, pair_receive)
    core, other = grid.core, 1 - grid.core
    sibling = grid.device(other)
    grid.greet(max(grid.size.values()) if small is not None else 1)
    starts = [[] for _ in range(1 + max(part[3] for parts in pieces for part in parts))]
    if has_small:
        small_out[...] = small[...]
        starts[0].append(
            lambda spawn: spawn(
                total_everywhere(traffic, pair, small_out, small_pair, small_landings)
            )
        )
    place, runs = 0, []
    for index, (rows, columns) in enumerate(shapes):
        half = rows // 2
        for part, (order, offset, count, turn) in enumerate(pieces[index]):
            window = (slice(None), slice(None), slice(offset, offset + count))
            fetched = []

            def fetch(index=index, half=half, offset=offset, count=count, window=window,
                      fetched=fetched, place=place):
                def stretch(at):
                    start = pl.multiple_of(at * half + offset, 8)
                    return wholes[index].at[:, :, pl.ds(start, count), :]

                came = pair.copy(stretch(other), others[index].at[window], sibling, None, None)
                load = pltpu.make_async_copy(
                    stretch(core), sums[index].at[window], local.at[place]
                )
                load.start()
                fetched.extend((came, load))

            ahead = max(0, turn - AHEAD)
            starts[ahead].append(lambda spawn, fetch=fetch: fetch())
            place += 1

            def run(index=index, order=order, offset=offset, count=count, window=window,
                    fetched=fetched, columns=columns, part=part):
                fetched[1].wait()
                pair.arrive(fetched[0])
                sums[index][window] += others[index][window]

                def view(chosen):
                    return block_of(sums[index], chosen, offset, count, 2 * columns)

                yield from sum_part(traffic, order, view, landings[index][part])

            runs.append((turn, lambda spawn, run=run: spawn(run())))
    for turn, run in runs:
        starts[turn].append(run)
    run_rounds(starts)
    handles = []
    for index, (rows, columns) in enumerate(shapes):
        half = rows // 2
        block = block_of(sums[index], grid.at, 0, half, 2 * columns)
        handles.append(pair.copy(block, finals[index], sibling, None, None))
    for index, (rows, columns) in enumerate(shapes):
        half = rows // 2
        block = block_of(sums[index], grid.at, 0, half, 2 * columns)[0, 0]
        pair.arrive(handles[index])
        came = finals[index][0, 0]
        for value, at in ((block, core), (came, other)):
            outs[index][pl.ds(pl.multiple_of(at * half, 8), half), :] = jnp.where(
                core == 0, value[:, :columns], value[:, columns:]
            )
    traffic.close()
    pair.close()


def scatter(wholes, small, dp, fsdp, collective_id, target):
    size = {"x": dp // 2, "a": 4, "b": fsdp // 4}
    shapes = [(whole.shape[2], whole.shape[3] // dp) for whole in wholes]
    pieces = plan_rounds(shapes, target)
    number = len(shapes)
    total = sum(len(parts) for parts in pieces)
    scratch = []
    for _ in range(2):
        scratch += [VMEM((size["a"], size["b"], r // 2, dp * c), jnp.float32) for r, c in shapes]
    scratch += [VMEM((1, 1, r // 2, 2 * c), jnp.float32) for r, c in shapes]
    for (rows, columns), parts in zip(shapes, pieces):
        for order, _, count, _ in parts:
            for shape in landing_shapes(size, order, count, 2 * columns):
                scratch.append(VMEM(shape, jnp.float32))
    smalls = [] if small is None else [small]
    for array in smalls:
        scratch.append(VMEM(array.shape, jnp.float32))
        for axis in ("x", "b", "a"):
            scratch.append(VMEM((size[axis], *array.shape), jnp.float32))
    hops = 2 * sum(size.values()) + sum((length - 1) * length for length in size.values())
    scratch += [
        pltpu.SemaphoreType.DMA((total * hops + 40,)),
        pltpu.SemaphoreType.DMA((total * hops + 40,)),
        pltpu.SemaphoreType.DMA((total + number + 1,)),
        pltpu.SemaphoreType.DMA((total + number + 1,)),
        pltpu.SemaphoreType.DMA((total,)),
    ]
    vmem = pl.BlockSpec(memory_space=VMEM)
    results = pl.pallas_call(
        partial(scatter_kernel, dp, fsdp, shapes, pieces, small is not None),
        out_shape=[jax.ShapeDtypeStruct(shape, jnp.float32) for shape in shapes]
        + [jax.ShapeDtypeStruct(array.shape, jnp.float32) for array in smalls],
        in_specs=[pl.BlockSpec(memory_space=pl.ANY)] * number + [vmem] * len(smalls),
        out_specs=[vmem] * (number + len(smalls)),
        scratch_shapes=scratch,
        compiler_params=pltpu.CompilerParams(
            collective_id=collective_id, has_side_effects=True, vmem_limit_bytes=60 << 20
        ),
        name="scatter_sums",
    )(*wholes, *smalls)
    return results[:number], (results[number] if smalls else None)


HEADS_E = 12
HEADS_D = 4
GATHER_TARGET = 60000
SCATTER_TARGET = 18000


precise = lax.Precision.HIGH
everywhere = ("dp", "fsdp")


def product(operand, factor):
    return jnp.dot(operand, factor, precision=precise, preferred_element_type=jnp.float32)


def transposed_left(operand, factor):
    return lax.dot_general(
        operand,
        factor,
        (((0,), (0,)), ((), ())),
        precision=precise,
        preferred_element_type=jnp.float32,
    )


def against(operand, factor):
    return lax.dot_general(
        operand,
        factor,
        (((1,), (1,)), ((), ())),
        precision=precise,
        preferred_element_type=jnp.float32,
    )


def normalize(values, gain_row):
    center = values - jnp.mean(values, axis=-1, keepdims=True)
    inverse = lax.rsqrt(jnp.mean(center * center, axis=-1, keepdims=True) + 1e-06)
    return center * inverse * gain_row


def attend(packed, head_count):
    row_count = packed.shape[0]
    breadth = packed.shape[1] // 3
    head_size = breadth // head_count
    row_block = min(row_count, 512)
    queries = packed[:, :breadth].reshape(row_count // row_block, row_block, head_count, head_size)
    key_rows = packed[:, breadth : 2 * breadth].reshape(row_count, head_count, head_size)
    value_rows = packed[:, 2 * breadth :].reshape(row_count, head_count, head_size)

    def one_block(block_queries):
        scores = jnp.einsum("qhd,khd->hqk", block_queries, key_rows, precision=precise) / math.sqrt(
            head_size
        )
        weights = jax.nn.softmax(scores, axis=-1)
        return jnp.einsum("hqk,khd->qhd", weights, value_rows, precision=precise)

    mixture = lax.map(jax.checkpoint(one_block), queries)
    return mixture.reshape(row_count, breadth)


def position_table(length, breadth):
    half_width = breadth // 2
    indices = jnp.arange(length, dtype=jnp.float32)[:, None]
    frequency = jnp.exp(
        jnp.arange(half_width, dtype=jnp.float32) * (-math.log(10000.0) / half_width)
    )[None, :]
    angles = indices * frequency
    return jnp.concatenate([jnp.sin(angles), jnp.cos(angles)], axis=1)


def gelu_exact(values):
    return jax.nn.gelu(values, approximate=False)


def block_forward(states, gain_pair, matrices, head_count):
    first_norm, first_back = jax.vjp(normalize, states, gain_pair[0])
    packed = product(first_norm, matrices[0])
    mixture, attend_back = jax.vjp(partial(attend, head_count=head_count), packed)
    middle = states + product(mixture, matrices[1])
    second_norm, second_back = jax.vjp(normalize, middle, gain_pair[1])
    hidden = product(second_norm, matrices[2])
    active, gelu_back = jax.vjp(gelu_exact, hidden)
    result = middle + product(active, matrices[3])
    stored = (
        first_norm,
        mixture,
        second_norm,
        active,
        first_back,
        attend_back,
        second_back,
        gelu_back,
    )
    return (result, stored)


def block_backward(upstream, matrices, stored):
    first_norm, mixture, second_norm, active, first_back, attend_back, second_back, gelu_back = (
        stored
    )
    reduce_grad = transposed_left(active, upstream)
    hidden_grad = gelu_back(against(upstream, matrices[3]))[0]
    expand_grad = transposed_left(second_norm, hidden_grad)
    middle_part, second_gain = second_back(against(hidden_grad, matrices[2]))
    middle_grad = upstream + middle_part
    merge_grad = transposed_left(mixture, middle_grad)
    packed_grad = attend_back(against(middle_grad, matrices[1]))[0]
    attend_grad = transposed_left(first_norm, packed_grad)
    states_part, first_gain = first_back(against(packed_grad, matrices[0]))
    gain_grads = jnp.stack([first_gain, second_gain])
    return (
        middle_grad + states_part,
        gain_grads,
        (attend_grad, merge_grad, expand_grad, reduce_grad),
    )


def collect(weights):
    columns, rows = lax.axis_size("dp"), lax.axis_size("fsdp")
    if all(weight.shape[0] % 16 == 0 for weight in weights):
        wholes = gather(weights, columns, rows, 1, GATHER_TARGET)
        return [whole.reshape(-1, whole.shape[3]) for whole in wholes]
    return [
        lax.all_gather(
            lax.all_gather(weight, "dp", axis=1, tiled=True), "fsdp", axis=0, tiled=True
        )
        for weight in weights
    ]


def spread(gradients, small, collective_id):
    columns, rows = lax.axis_size("dp"), lax.axis_size("fsdp")
    if all(gradient.shape[0] % (rows * 16) == 0 for gradient in gradients):
        wholes = [
            gradient.reshape(4, rows // 4, gradient.shape[0] // rows, gradient.shape[1])
            for gradient in gradients
        ]
        return scatter(wholes, small, columns, rows, collective_id, SCATTER_TARGET)
    parts = [
        lax.psum_scatter(
            lax.psum_scatter(gradient, "fsdp", scatter_dimension=0, tiled=True),
            "dp",
            scatter_dimension=1,
            tiled=True,
        )
        for gradient in gradients
    ]
    return parts, (None if small is None else lax.psum(small, everywhere))


def pack_small(arrays):
    flat = jnp.concatenate([array.reshape(-1) for array in arrays])
    size = -(-flat.shape[0] // 1024) * 1024
    return jnp.pad(flat, (0, size - flat.shape[0])).reshape(-1, 128)


def unpack_small(packed, arrays):
    flat, start, out = packed.reshape(-1), 0, []
    for array in arrays:
        out.append(flat[start : start + array.size].reshape(array.shape))
        start += array.size
    return out


def place(choice, values):
    high = lax.reduce_precision(values, 8, 7)
    low = values - high
    wide = choice.astype(jnp.bfloat16)
    return jnp.dot(
        wide, high.astype(jnp.bfloat16), preferred_element_type=jnp.float32
    ) + jnp.dot(wide, low.astype(jnp.bfloat16), preferred_element_type=jnp.float32)


def local(
    tokens,
    sensor_tag,
    block_dest,
    block_order,
    sensor_table,
    encoder_gains,
    encoder_attend,
    encoder_merge,
    encoder_expand,
    encoder_reduce,
    bridge,
    mask_token,
    decoder_gains,
    decoder_attend,
    decoder_merge,
    decoder_expand,
    decoder_reduce,
    cotangent,
):
    groups = lax.axis_size("fsdp")
    visible = tokens.shape[0]
    capacity = 2 * visible // groups
    length = block_order.shape[1]
    breadth = mask_token.shape[0]
    weights = collect(
        [
            encoder_attend,
            encoder_merge,
            encoder_expand,
            encoder_reduce,
            bridge,
            decoder_attend,
            decoder_merge,
            decoder_expand,
            decoder_reduce,
        ]
    )
    encoder_set, decoder_set = weights[:5], weights[5:]
    tag_row = (
        sensor_tag[:, None] == jnp.arange(sensor_table.shape[0], dtype=jnp.int32)[None, :]
    ).astype(jnp.float32)
    initial = tokens + product(tag_row, sensor_table)
    encoded, encoder_kept = block_forward(initial, encoder_gains, encoder_set, HEADS_E)
    projected = product(encoded, encoder_set[4])
    destination = block_dest[:, 0]
    chooser = (destination[:, None] == jnp.arange(groups, dtype=jnp.int32)[None, :]).astype(
        jnp.int32
    )
    ranking = jnp.sum((jnp.cumsum(chooser, axis=0) - chooser) * chooser, axis=1)
    slot_index = destination * capacity + ranking
    select = (
        slot_index[None, :] == jnp.arange(groups * capacity, dtype=jnp.int32)[:, None]
    ).astype(jnp.float32)
    outgoing = place(select, projected).reshape(groups, capacity, breadth)
    tallies = jnp.sum(chooser, axis=0).astype(jnp.float32)[:, None]
    arrived, arrived_tallies = (
        lax.all_to_all(outgoing, "fsdp", split_axis=0, concat_axis=0, tiled=True),
        lax.all_to_all(tallies, "fsdp", split_axis=0, concat_axis=0, tiled=True),
    )
    present = (jnp.arange(capacity, dtype=jnp.float32)[None, :] < arrived_tallies).reshape(-1)
    ordering = block_order[0, : groups * capacity]
    placing = (
        (ordering[None, :] == jnp.arange(length, dtype=jnp.int32)[:, None]) & present[None, :]
    ).astype(jnp.float32)
    covered = jnp.sum(placing, axis=1, keepdims=True)
    filled = (
        place(placing, arrived.reshape(groups * capacity, breadth))
        + (1.0 - covered) * mask_token
        + position_table(length, breadth)
    )
    decoded, decoder_kept = block_forward(filled, decoder_gains, decoder_set, HEADS_D)
    filled_grad, decoder_gain_grad, decoder_grads = block_backward(
        cotangent, decoder_set, decoder_kept
    )
    mask_grad = jnp.sum((1.0 - covered) * filled_grad, axis=0)
    arrived_grad = place(placing.T, filled_grad).reshape(groups, capacity, breadth)
    returned = lax.all_to_all(arrived_grad, "fsdp", split_axis=0, concat_axis=0, tiled=True)
    projected_grad = place(select.T, returned.reshape(groups * capacity, breadth))
    bridge_grad = transposed_left(encoded, projected_grad)
    encoded_grad = against(projected_grad, encoder_set[4])
    tokens_grad, encoder_gain_grad, encoder_grads = block_backward(
        encoded_grad, encoder_set, encoder_kept
    )
    table_grad = transposed_left(tag_row, jnp.sum(tokens_grad, axis=0, keepdims=True))
    small = (table_grad, encoder_gain_grad, mask_grad, decoder_gain_grad)
    packed_small = pack_small(small)
    decoder_spread, _ = spread(decoder_grads, None, 2)
    encoder_spread, total = spread([*encoder_grads, bridge_grad], packed_small, 3)
    summed = unpack_small(total, small)
    return (
        decoded,
        tokens_grad,
        summed[0],
        summed[1],
        encoder_spread[0],
        encoder_spread[1],
        encoder_spread[2],
        encoder_spread[3],
        encoder_spread[4],
        summed[2],
        summed[3],
        decoder_spread[0],
        decoder_spread[1],
        decoder_spread[2],
        decoder_spread[3],
    )


def solution(mesh):
    in_specs = (
        P(("dp", "fsdp"), None),
        P(("dp", "fsdp")),
        P(("dp", "fsdp"), None),
        P(("dp", "fsdp"), None),
        P(),
        P(),
        P("fsdp", "dp"),
        P("fsdp", "dp"),
        P("fsdp", "dp"),
        P("fsdp", "dp"),
        P("fsdp", "dp"),
        P(),
        P(),
        P("fsdp", "dp"),
        P("fsdp", "dp"),
        P("fsdp", "dp"),
        P("fsdp", "dp"),
        P(("dp", "fsdp"), None),
    )
    out_specs = (
        P(("dp", "fsdp"), None),
        P(("dp", "fsdp"), None),
        P(),
        P(),
        P("fsdp", "dp"),
        P("fsdp", "dp"),
        P("fsdp", "dp"),
        P("fsdp", "dp"),
        P("fsdp", "dp"),
        P(),
        P(),
        P("fsdp", "dp"),
        P("fsdp", "dp"),
        P("fsdp", "dp"),
        P("fsdp", "dp"),
    )
    return jax.shard_map(local, mesh=mesh, in_specs=in_specs, out_specs=out_specs, check_vma=False)
```

```python
from functools import partial
import math

import jax
import jax.numpy as jnp
from jax import lax
from jax.experimental import pallas as pl
from jax.experimental.pallas import tpu as pltpu
from jax.sharding import PartitionSpec as P

MESH = pl.DeviceIdType.MESH
VMEM = pltpu.VMEM
NARROW = jnp.bfloat16
LONG = (("b", "a", "x"), ("x", "a", "b"))
SHORT = (("a", "x", "b"), ("a", "b", "x"))
TURNS = (LONG, LONG, SHORT)
AHEAD = 2


class Grid:
    def __init__(self, dp, fsdp):
        self.size = {"x": dp // 2, "a": 4, "b": fsdp // 4}
        column, row = lax.axis_index("dp"), lax.axis_index("fsdp")
        self.core = lax.rem(column, 2)
        self.at = {
            "x": lax.div(column, 2),
            "a": lax.div(row, self.size["b"]),
            "b": lax.rem(row, self.size["b"]),
        }

    def device(self, core=None, **moved):
        at = {**self.at, **moved}
        core = self.core if core is None else core
        return (at["x"] * 2 + core, at["a"] * self.size["b"] + at["b"])

    def greet(self, reach):
        barrier = pltpu.get_barrier_semaphore()
        pl.semaphore_signal(
            barrier, inc=1, device_id=self.device(1 - self.core), device_id_type=MESH
        )
        count = 1
        for axis, size in self.size.items():
            here = self.at[axis]
            for move in range(-min(reach, size - 1), min(reach, size - 1) + 1):
                if move:
                    exists = together(here + move >= 0, here + move < size)
                    count = count + jnp.where(exists, 1, 0)

                    @pl.when(exists)
                    def _(axis=axis, here=here, move=move):
                        pl.semaphore_signal(
                            barrier,
                            inc=1,
                            device_id=self.device(**{axis: here + move}),
                            device_id_type=MESH,
                        )

        pl.semaphore_wait(barrier, count)


def plan_rounds(shapes, target, taper):
    plan, turn = [], 0
    for index, (rows, columns) in enumerate(shapes):
        units = rows // 16
        pairs = max(1, min(units // 2, round(units * 8 * columns * 2 / target)))
        sizes = [1] * pairs
        if taper and index == len(shapes) - 1 and units >= 2 * sum(taper):
            sizes = taper
        parts, start = [], 0
        for pair, size in enumerate(sizes):
            orders = TURNS[turn % len(TURNS)]
            for place, order in enumerate(orders):
                left = 2 * sum(sizes[pair:]) - place * size
                take = -(-(units - start) * size // left)
                if take:
                    parts.append((order, start * 8, take * 8, turn))
                start += take
            turn += 1
        plan.append(parts)
    return plan


def together(*conditions):
    joined = conditions[0]
    for condition in conditions[1:]:
        joined = jnp.logical_and(joined, condition)
    return joined


class Traffic:
    def __init__(self, grid, send, receive):
        self.grid, self.send, self.receive = grid, send, receive
        self.count, self.open = 0, []

    def copy(self, source, target, device, starts, arrives):
        place = self.count
        self.count += 1

        def made():
            return pltpu.make_async_remote_copy(
                src_ref=source,
                dst_ref=target,
                send_sem=self.send.at[place],
                recv_sem=self.receive.at[place],
                device_id=device,
                device_id_type=MESH,
            )

        if starts is None:
            made().start()
        else:

            @pl.when(starts)
            def _():
                made().start()

        self.open.append((made, starts))
        return (made, arrives)

    def arrive(self, handle):
        made, arrives = handle
        if arrives is None:
            made().wait_recv()
        else:

            @pl.when(arrives)
            def _():
                made().wait_recv()

    def take(self, handle):
        handle[0]().wait_recv()

    def drain(self, handle):
        handle[0]().wait_send()
        self.open = [entry for entry in self.open if entry[0] is not handle[0]]

    def close(self):
        for made, starts in self.open:
            if starts is None:
                made().wait_send()
            else:

                @pl.when(starts)
                def _():
                    made().wait_send()


def block_of(full, chosen, offset, rows, width):
    view = []
    for axis in ("a", "b"):
        place = chosen[axis]
        view.append(slice(None) if place is None else pl.ds(place, 1))
    columns = (
        slice(None)
        if chosen["x"] is None
        else pl.ds(pl.multiple_of(chosen["x"] * width, 128), width)
    )
    return full.at[(*view, pl.ds(pl.multiple_of(offset, 8), rows), columns)]


def gather_line(traffic, axis, chosen, view, exists, arrived):
    grid = traffic.grid
    here, size = grid.at[axis], grid.size[axis]

    def both(condition):
        return condition if exists is None else together(exists, condition)

    arrived({**chosen, axis: here}, exists)
    for step in range(1, size):
        ahead, behind = {**chosen, axis: here - (step - 1)}, {**chosen, axis: here + (step - 1)}
        rightward = traffic.copy(
            view(ahead),
            view(ahead),
            grid.device(**{axis: here + 1}),
            both(together(here + 1 < size, here - (step - 1) >= 0)),
            both(here - step >= 0),
        )
        leftward = traffic.copy(
            view(behind),
            view(behind),
            grid.device(**{axis: here - 1}),
            both(together(here - 1 >= 0, here + (step - 1) < size)),
            both(here + step < size),
        )
        yield
        traffic.arrive(rightward)
        arrived({**chosen, axis: here - step}, both(here - step >= 0))
        traffic.arrive(leftward)
        arrived({**chosen, axis: here + step}, both(here + step < size))


def gather_part(traffic, order, view, spawn, share):
    first, second, third = order
    grid = traffic.grid
    own = dict(grid.at)

    def last(chosen, exists):
        def finish():
            yield from gather_line(traffic, third, chosen, view, exists, lambda *_: None)
            share(view({**chosen, third: None}), exists)

        spawn(finish())

    def begin():
        if grid.size[first] == 2:
            yield from gather_line(traffic, first, own, view, None, lambda *_: None)
            yield from gather_line(traffic, second, {**own, first: None}, view, None, last)
        else:

            def middle(chosen, exists):
                def go():
                    yield from gather_line(traffic, second, chosen, view, exists, lambda *_: None)
                    last({**chosen, second: None}, exists)

                spawn(go())

            yield from gather_line(traffic, first, own, view, None, middle)

    spawn(begin())


def run_rounds(starts):
    active = []

    def spawn(generator):
        try:
            next(generator)
            active.append(generator)
        except StopIteration:
            pass

    for start in starts:
        for begin in start:
            begin(spawn)
        advance_all(active)
    while active:
        advance_all(active)


def advance_all(active):
    for generator in list(active):
        try:
            next(generator)
        except StopIteration:
            active.remove(generator)


def gather_kernel(dp, fsdp, shapes, plan, *refs):
    number = len(shapes)
    shards, wholes = refs[:number], refs[number : 2 * number]
    raws, blocks = refs[2 * number : 3 * number], refs[3 * number : 4 * number]
    send, receive, pair_send, pair_receive, local = refs[4 * number :]
    grid = Grid(dp, fsdp)
    traffic = Traffic(grid, send, receive)
    pair = Traffic(grid, pair_send, pair_receive)
    core, other = grid.core, 1 - grid.core
    sibling = grid.device(other)
    grid.greet(1)
    handles = []
    for index, (rows, columns) in enumerate(shapes):
        half = rows // 2
        theirs = shards[index].at[pl.ds(pl.multiple_of(other * half, 8), half)]
        handles.append(pair.copy(theirs, raws[index], sibling, None, None))
    stores = []
    for index, (rows, columns) in enumerate(shapes):
        half = rows // 2
        pair.arrive(handles[index])
        mine = shards[index][pl.ds(pl.multiple_of(core * half, 8), half), :]
        came = raws[index][...]
        blocks[index][0, 0] = jnp.where(
            core == 0,
            jnp.concatenate([mine, came], axis=1),
            jnp.concatenate([came, mine], axis=1),
        )
        store = pltpu.make_async_copy(
            blocks[index],
            block_of(wholes[index], grid.at, core * half, half, 2 * columns),
            local.at[index],
        )
        store.start()
        stores.append(store)
    for store in stores:
        store.wait()
    pending = []

    def share(piece, exists):
        pending.append(pair.copy(piece, piece, sibling, exists, exists))

    starts = [[] for _ in range(1 + max(part[3] for parts in plan for part in parts))]
    for index, (rows, columns) in enumerate(shapes):
        half = rows // 2
        for order, offset, count, turn in plan[index]:

            def view(chosen, index=index, offset=offset, count=count, half=half, columns=columns):
                return block_of(wholes[index], chosen, core * half + offset, count, 2 * columns)

            starts[turn].append(
                lambda spawn, order=order, view=view: gather_part(
                    traffic, order, view, spawn, share
                )
            )
    run_rounds(starts)
    for handle in pending:
        pair.arrive(handle)
    traffic.close()
    pair.close()


def gather(weights, dp, fsdp, collective_id, target, taper=()):
    shapes = [weight.shape for weight in weights]
    a, b = 4, fsdp // 4
    plan = plan_rounds(shapes, target, taper)
    total = sum(len(parts) for parts in plan)
    out = [jax.ShapeDtypeStruct((a, b, r, dp * c), jnp.float32) for r, c in shapes]
    vmem = pl.BlockSpec(memory_space=VMEM)
    return pl.pallas_call(
        partial(gather_kernel, dp, fsdp, shapes, plan),
        out_shape=out,
        in_specs=[vmem] * len(shapes),
        out_specs=[pl.BlockSpec(memory_space=pl.ANY)] * len(shapes),
        scratch_shapes=[VMEM((r // 2, c), jnp.float32) for r, c in shapes]
        + [VMEM((1, 1, r // 2, 2 * c), jnp.float32) for r, c in shapes]
        + [
            pltpu.SemaphoreType.DMA((34 * total,)),
            pltpu.SemaphoreType.DMA((34 * total,)),
            pltpu.SemaphoreType.DMA((8 * total + len(shapes),)),
            pltpu.SemaphoreType.DMA((8 * total + len(shapes),)),
            pltpu.SemaphoreType.DMA((len(shapes),)),
        ],
        compiler_params=pltpu.CompilerParams(
            collective_id=collective_id, has_side_effects=True, vmem_limit_bytes=32 << 20
        ),
        name="gather_weights",
    )(*weights)


def landing_shapes(size, order, rows, width):
    chosen, shapes = {"x": size["x"], "a": size["a"], "b": size["b"]}, []
    for axis in reversed(order):
        chosen[axis] = 1
        slots = 1 if size[axis] == 2 else 2 * (size[axis] - 1)
        shapes.append((slots, chosen["a"], chosen["b"], rows, chosen["x"] * width))
    return shapes


def sum_line(traffic, axis, chosen, view, landing):
    grid = traffic.grid
    here, size = grid.at[axis], grid.size[axis]
    ends = size - 1

    def slot(rightward, place):
        if size == 2:
            return 0
        return place - 1 if rightward else ends + place

    def blocks(place):
        return view({**chosen, axis: place})

    def add(rightward, place):
        target = blocks(place)
        target[...] += landing[slot(rightward, place)]

    def send(rightward, place, starts, arrives):
        return traffic.copy(
            blocks(place),
            landing.at[slot(rightward, place)],
            grid.device(**{axis: here + (1 if rightward else -1)}),
            starts,
            arrives,
        )

    first = {}
    for place in range(ends, 0, -1):
        first[True, place] = send(
            True, place, here == 0, here == 1
        )
    for place in range(ends):
        first[False, place] = send(False, place, here == ends, here == ends - 1)
    later = {}
    for step in range(ends - 1):
        yield
        for come in range(1, ends):
            place = ends - step + come - 1
            if come < place <= ends:
                @pl.when(here == come)
                def _(come=come, place=place):
                    traffic.take(first[True, place] if come == 1 else later[True, come - 1, place])
                    add(True, place)

                later[True, come, place] = send(True, place, here == come, here == come + 1)
            come, place = ends - come, ends - place
            if come > place >= 0:

                @pl.when(here == come)
                def _(come=come, place=place):
                    traffic.take(
                        first[False, place] if come == ends - 1 else later[False, come + 1, place]
                    )
                    add(False, place)

                later[False, come, place] = send(False, place, here == come, here == come - 1)
    yield
    for place in range(size):

        @pl.when(here == place)
        def _(place=place):
            if place > 0:
                traffic.take(first[True, place] if place == 1 else later[True, place - 1, place])
                add(True, place)
            if place < ends:
                traffic.take(
                    first[False, place] if place == ends - 1 else later[False, place + 1, place]
                )
                add(False, place)


def sum_part(traffic, order, view, landings):
    chosen = {"x": None, "a": None, "b": None}
    for axis, landing in zip(reversed(order), landings):
        yield from sum_line(traffic, axis, chosen, view, landing)
        chosen[axis] = traffic.grid.at[axis]


def total_everywhere(traffic, pair, value, pair_landing, landings):
    grid = traffic.grid
    came = pair.copy(value, pair_landing, grid.device(1 - grid.core), None, None)
    yield
    pair.arrive(came)
    pair.drain(came)
    value[...] += pair_landing[...]
    for axis, landing in zip(("x", "b", "a"), landings):
        here, size = grid.at[axis], grid.size[axis]
        handles = []
        for move in range(1, size):
            target = lax.rem(here + move, size)
            source = lax.rem(here + size - move, size)
            handles.append(
                (
                    traffic.copy(
                        value, landing.at[here], grid.device(**{axis: target}), None, None
                    ),
                    source,
                )
            )
        landing[here] = value[...]
        yield
        for handle, _ in handles:
            traffic.arrive(handle)
            traffic.drain(handle)
        total = landing[0]
        for place in range(1, size):
            total = total + landing[place]
        value[...] = total


def scatter_kernel(dp, fsdp, shapes, pieces, has_small, *refs):
    number = len(shapes)
    refs = list(refs)

    def take(count):
        taken = refs[:count]
        del refs[:count]
        return taken

    wholes, small = take(number), (take(1)[0] if has_small else None)
    outs, small_out = take(number), (take(1)[0] if has_small else None)
    sums, others, finals = take(number), take(number), take(number)
    landings = [[take(3) for _ in parts] for parts in pieces]
    if has_small:
        small_pair, *small_landings = take(4)
    send, receive, pair_send, pair_receive, local = refs
    grid = Grid(dp, fsdp)
    traffic = Traffic(grid, send, receive)
    pair = Traffic(grid, pair_send, pair_receive)
    core, other = grid.core, 1 - grid.core
    sibling = grid.device(other)
    grid.greet(max(grid.size.values()) if small is not None else 1)
    starts = [[] for _ in range(1 + max(part[3] for parts in pieces for part in parts))]
    if has_small:
        small_out[...] = small[...]
        starts[0].append(
            lambda spawn: spawn(
                total_everywhere(traffic, pair, small_out, small_pair, small_landings)
            )
        )
    place, runs = 0, []
    for index, (rows, columns) in enumerate(shapes):
        half = rows // 2
        for part, (order, offset, count, turn) in enumerate(pieces[index]):
            window = (slice(None), slice(None), slice(offset, offset + count))
            fetched = []

            def fetch(index=index, half=half, offset=offset, count=count, window=window,
                      fetched=fetched, place=place):
                def stretch(at):
                    start = pl.multiple_of(at * half + offset, 8)
                    return wholes[index].at[:, :, pl.ds(start, count), :]

                came = pair.copy(stretch(other), others[index].at[window], sibling, None, None)
                load = pltpu.make_async_copy(
                    stretch(core), sums[index].at[window], local.at[place]
                )
                load.start()
                fetched.extend((came, load))

            ahead = max(0, turn - AHEAD)
            starts[ahead].append(lambda spawn, fetch=fetch: fetch())
            place += 1

            def run(index=index, order=order, offset=offset, count=count, window=window,
                    fetched=fetched, columns=columns, part=part):
                fetched[1].wait()
                pair.arrive(fetched[0])
                sums[index][window] += others[index][window]

                def view(chosen):
                    return block_of(sums[index], chosen, offset, count, 2 * columns)

                yield from sum_part(traffic, order, view, landings[index][part])

            runs.append((turn, lambda spawn, run=run: spawn(run())))
    for turn, run in runs:
        starts[turn].append(run)
    run_rounds(starts)
    handles = []
    for index, (rows, columns) in enumerate(shapes):
        half = rows // 2
        block = block_of(sums[index], grid.at, 0, half, 2 * columns)
        handles.append(pair.copy(block, finals[index], sibling, None, None))
    for index, (rows, columns) in enumerate(shapes):
        half = rows // 2
        block = block_of(sums[index], grid.at, 0, half, 2 * columns)[0, 0]
        pair.arrive(handles[index])
        came = finals[index][0, 0]
        for value, at in ((block, core), (came, other)):
            outs[index][pl.ds(pl.multiple_of(at * half, 8), half), :] = jnp.where(
                core == 0, value[:, :columns], value[:, columns:]
            )
    traffic.close()
    pair.close()


def scatter(wholes, small, dp, fsdp, collective_id, target, taper=()):
    size = {"x": dp // 2, "a": 4, "b": fsdp // 4}
    shapes = [(whole.shape[2], whole.shape[3] // dp) for whole in wholes]
    pieces = plan_rounds(shapes, target, taper)
    number = len(shapes)
    total = sum(len(parts) for parts in pieces)
    scratch = []
    for _ in range(2):
        scratch += [VMEM((size["a"], size["b"], r // 2, dp * c), jnp.float32) for r, c in shapes]
    scratch += [VMEM((1, 1, r // 2, 2 * c), jnp.float32) for r, c in shapes]
    for (rows, columns), parts in zip(shapes, pieces):
        for order, _, count, _ in parts:
            for shape in landing_shapes(size, order, count, 2 * columns):
                scratch.append(VMEM(shape, jnp.float32))
    smalls = [] if small is None else [small]
    for array in smalls:
        scratch.append(VMEM(array.shape, jnp.float32))
        for axis in ("x", "b", "a"):
            scratch.append(VMEM((size[axis], *array.shape), jnp.float32))
    hops = 2 * sum(size.values()) + sum((length - 1) * length for length in size.values())
    scratch += [
        pltpu.SemaphoreType.DMA((total * hops + 40,)),
        pltpu.SemaphoreType.DMA((total * hops + 40,)),
        pltpu.SemaphoreType.DMA((total + number + 1,)),
        pltpu.SemaphoreType.DMA((total + number + 1,)),
        pltpu.SemaphoreType.DMA((total,)),
    ]
    vmem = pl.BlockSpec(memory_space=VMEM)
    results = pl.pallas_call(
        partial(scatter_kernel, dp, fsdp, shapes, pieces, small is not None),
        out_shape=[jax.ShapeDtypeStruct(shape, jnp.float32) for shape in shapes]
        + [jax.ShapeDtypeStruct(array.shape, jnp.float32) for array in smalls],
        in_specs=[pl.BlockSpec(memory_space=pl.ANY)] * number + [vmem] * len(smalls),
        out_specs=[vmem] * (number + len(smalls)),
        scratch_shapes=scratch,
        compiler_params=pltpu.CompilerParams(
            collective_id=collective_id, has_side_effects=True, vmem_limit_bytes=60 << 20
        ),
        name="scatter_sums",
    )(*wholes, *smalls)
    return results[:number], (results[number] if smalls else None)


HEAD = 64


def split(values):
    high = values.astype(NARROW)
    return high, (values - high.astype(jnp.float32)).astype(NARROW)


def tripled(values, leading):
    high, low = split(values)
    return jnp.concatenate([high, high, low] if leading else [high, low, high], axis=1)


def dot(left, right, contract=(1, 0)):
    return lax.dot_general(
        left,
        right,
        (((contract[0],), (contract[1],)), ((), ())),
        preferred_element_type=jnp.float32,
    )


def attend_kernel(chunk, q_ref, k_ref, v_ref, out_ref, lse_ref, keys, values, scores, high, low):
    rows = q_ref.shape[0]

    @pl.when(pl.program_id(1) == 0)
    def _():
        for head in range(2):
            part = slice(head * HEAD, (head + 1) * HEAD)
            keys[head] = tripled(k_ref[:, part], False)
            values[head] = jnp.concatenate(split(v_ref[:, part]), axis=1)

    outs, stats = [], []
    for head in range(2):
        part = slice(head * HEAD, (head + 1) * HEAD)
        queries = tripled(q_ref[:, part] * (1.0 / math.sqrt(HEAD)), True)
        scores[...] = dot(queries, keys[head], (1, 1))

        def body(step, _):
            at = pl.ds(pl.multiple_of(step * chunk, chunk), chunk)
            piece = scores[at, :]
            top = jnp.max(piece, axis=1, keepdims=True)
            weights = jnp.exp(piece - top)
            total = jnp.sum(weights, axis=1, keepdims=True)
            first, second = split(weights)
            high[at, :] = first
            low[at, :] = second
            lse_ref[at, head : head + 1] = top + jnp.log(total)
            lse_ref[at, 2 + head : 3 + head] = 1.0 / total
            return 0

        lax.fori_loop(0, rows // chunk, body, 0, unroll=2)
        both = dot(high[...], values[head])
        outs.append(
            (both[:, :HEAD] + both[:, HEAD:] + dot(low[...], values[head][:, :HEAD]))
            * lse_ref[:, 2 + head : 3 + head]
        )
    out_ref[...] = jnp.concatenate(outs, axis=1)


def attend_forward(packed, block=768, chunk=128):
    rows, breadth = packed.shape[0], packed.shape[1] // 3
    pairs = breadth // 128
    block = min(block, rows)
    return pl.pallas_call(
        partial(attend_kernel, chunk),
        grid=(pairs, rows // block),
        in_specs=[
            pl.BlockSpec((block, 128), lambda h, i: (i, h)),
            pl.BlockSpec((rows, 128), lambda h, i: (0, pairs + h)),
            pl.BlockSpec((rows, 128), lambda h, i: (0, 2 * pairs + h)),
        ],
        out_specs=[
            pl.BlockSpec((block, 128), lambda h, i: (i, h)),
            pl.BlockSpec((None, block, 128), lambda h, i: (h, i, 0)),
        ],
        out_shape=[
            jax.ShapeDtypeStruct((rows, breadth), jnp.float32),
            jax.ShapeDtypeStruct((pairs, rows, 128), jnp.float32),
        ],
        scratch_shapes=[
            VMEM((2, rows, 3 * HEAD), NARROW),
            VMEM((2, rows, 2 * HEAD), NARROW),
            VMEM((block, rows), jnp.float32),
            VMEM((block, rows), NARROW),
            VMEM((block, rows), NARROW),
        ],
        compiler_params=pltpu.CompilerParams(vmem_limit_bytes=48 << 20),
        cost_estimate=pl.CostEstimate(
            flops=12 * rows * rows * breadth, bytes_accessed=20 * rows * breadth, transcendentals=0
        ),
        name="attend_forward",
    )(packed, packed, packed)


def attend_back_kernel(
    chunk, q_ref, k_ref, v_ref, o_ref, g_ref, lse_ref, dq_ref, dk_ref, dv_ref,
    queries, gradients, wide_q, wide_g, row_lse, row_delta, dq, scores, other,
    p_high, p_low, s_high, s_low,
):
    rows, block = q_ref.shape[0], k_ref.shape[0]
    scale = 1.0 / math.sqrt(HEAD)

    @pl.when(pl.program_id(1) == 0)
    def _():
        for head in range(2):
            part = slice(head * HEAD, (head + 1) * HEAD)
            q = q_ref[:, part] * scale
            g = g_ref[:, part]
            queries[head] = tripled(q, True).T
            gradients[head] = tripled(g, True).T
            wide_q[head] = jnp.concatenate(split(q), axis=1)
            wide_g[head] = jnp.concatenate(split(g), axis=1)
            delta = jnp.sum(g * o_ref[:, part], axis=1, keepdims=True)
            row_delta[head] = jnp.broadcast_to(delta, (rows, 128)).T[:8]
            row_lse[head] = jnp.broadcast_to(lse_ref[:, head : head + 1], (rows, 128)).T[:8]
        dq[...] = jnp.zeros_like(dq)

    dks, dvs = [], []
    for head in range(2):
        part = slice(head * HEAD, (head + 1) * HEAD)
        k = k_ref[:, part]
        scores[...] = dot(tripled(k, False), queries[head])
        other[...] = dot(tripled(v_ref[:, part], False), gradients[head])
        lse = row_lse[head, 0:1]
        delta = row_delta[head, 0:1]

        def body(step, _):
            at = pl.ds(pl.multiple_of(step * chunk, chunk), chunk)
            weights = jnp.exp(scores[at, :] - lse)
            p_high[at, :], p_low[at, :] = split(weights)
            s_high[at, :], s_low[at, :] = split(weights * (other[at, :] - delta))
            return 0

        lax.fori_loop(0, block // chunk, body, 0, unroll=2)
        both = dot(p_high[...], wide_g[head])
        dvs.append(both[:, :HEAD] + both[:, HEAD:] + dot(p_low[...], wide_g[head][:, :HEAD]))
        both = dot(s_high[...], wide_q[head])
        dks.append(both[:, :HEAD] + both[:, HEAD:] + dot(s_low[...], wide_q[head][:, :HEAD]))
        kt = jnp.concatenate(split(k * scale), axis=1).T
        both = dot(kt, s_high[...])
        dq[head] += both[:HEAD] + both[HEAD:] + dot(kt[:HEAD], s_low[...])
    dk_ref[...] = jnp.concatenate(dks, axis=1)
    dv_ref[...] = jnp.concatenate(dvs, axis=1)

    @pl.when(pl.program_id(1) == pl.num_programs(1) - 1)
    def _():
        for head in range(2):
            dq_ref[:, head * HEAD : (head + 1) * HEAD] = dq[head].T


def attend_backward(packed, mixture, lse, upstream, block=512, chunk=128):
    rows, breadth = mixture.shape
    pairs = breadth // 128
    block = min(block, rows)
    whole = lambda h, i: (0, h)
    stretch = lambda h, i: (i, h)
    parts = pl.pallas_call(
        partial(attend_back_kernel, chunk),
        grid=(pairs, rows // block),
        in_specs=[
            pl.BlockSpec((rows, 128), whole),
            pl.BlockSpec((block, 128), lambda h, i: (i, pairs + h)),
            pl.BlockSpec((block, 128), lambda h, i: (i, 2 * pairs + h)),
            pl.BlockSpec((rows, 128), whole),
            pl.BlockSpec((rows, 128), whole),
            pl.BlockSpec((None, rows, 128), lambda h, i: (h, 0, 0)),
        ],
        out_specs=[
            pl.BlockSpec((rows, 128), whole),
            pl.BlockSpec((block, 128), stretch),
            pl.BlockSpec((block, 128), stretch),
        ],
        out_shape=[jax.ShapeDtypeStruct((rows, breadth), jnp.float32)] * 3,
        scratch_shapes=[
            VMEM((2, 3 * HEAD, rows), NARROW),
            VMEM((2, 3 * HEAD, rows), NARROW),
            VMEM((2, rows, 2 * HEAD), NARROW),
            VMEM((2, rows, 2 * HEAD), NARROW),
            VMEM((2, 8, rows), jnp.float32),
            VMEM((2, 8, rows), jnp.float32),
            VMEM((2, HEAD, rows), jnp.float32),
            VMEM((block, rows), jnp.float32),
            VMEM((block, rows), jnp.float32),
            VMEM((block, rows), NARROW),
            VMEM((block, rows), NARROW),
            VMEM((block, rows), NARROW),
            VMEM((block, rows), NARROW),
        ],
        compiler_params=pltpu.CompilerParams(vmem_limit_bytes=48 << 20),
        cost_estimate=pl.CostEstimate(
            flops=30 * rows * rows * breadth, bytes_accessed=32 * rows * breadth, transcendentals=0
        ),
        name="attend_backward",
    )(packed, packed, packed, mixture, upstream, lse)
    return jnp.concatenate(parts, axis=1)


def stacked(values):
    high, low = split(values)
    return jnp.concatenate([high, low, high], axis=0)


def normal_parts(values):
    center = values - jnp.mean(values, axis=1, keepdims=True)
    inverse = lax.rsqrt(jnp.mean(center * center, axis=1, keepdims=True) + 1e-06)
    return center * inverse, inverse


def pieces_of(rows, size, body):
    for start in range(0, rows, size):
        body(slice(start, min(start + size, rows)))


def normal_share(values):
    return 0.5 + 0.5 * lax.erf(values * math.sqrt(0.5))


def panels_spec(matrix, block):
    if matrix.ndim == 2:
        return pl.BlockSpec((matrix.shape[0], block), lambda j: (0, j))
    each = matrix.shape[2] // block
    return pl.BlockSpec(
        (None, matrix.shape[1], block), lambda j: (lax.div(j, each), 0, lax.rem(j, each))
    )


def rows_spec(matrix, block):
    if matrix.ndim == 2:
        return pl.BlockSpec((block, matrix.shape[1]), lambda j: (j, 0))
    return pl.BlockSpec((matrix.shape[0], block, matrix.shape[2]), lambda j: (0, j, 0))


def joined(ref):
    if len(ref.shape) == 2:
        return ref[...]
    return jnp.concatenate([ref[panel] for panel in range(ref.shape[0])], axis=1)


def forward_kernel(piece, m_ref, gain_ref, expand_ref, reduce_ref, out_ref, hidden_ref, wide):
    rows = m_ref.shape[0]

    @pl.when(pl.program_id(0) == 0)
    def _():
        def begin(at):
            wide[at, :] = tripled(normal_parts(m_ref[at, :])[0] * gain_ref[...], True)
            out_ref[at, :] = m_ref[at, :]

        pieces_of(rows, piece, begin)

    expand, reduce = stacked(expand_ref[...]), stacked(joined(reduce_ref))

    def go(at):
        hidden = dot(wide[at, :], expand)
        hidden_ref[at, :] = hidden
        active = hidden * normal_share(hidden)
        out_ref[at, :] = out_ref[at, :] + dot(tripled(active, True), reduce)

    pieces_of(rows, piece, go)


def feed_forward(middle, gain, expand, reduce, block=512, piece=512):
    rows, width = middle.shape
    hidden = reduce.shape[-2]
    block = min(block, expand.shape[-1])
    whole = lambda j: (0, 0)
    return pl.pallas_call(
        partial(forward_kernel, min(piece, rows)),
        grid=(hidden // block,),
        in_specs=[
            pl.BlockSpec((rows, width), whole),
            pl.BlockSpec((1, width), whole),
            panels_spec(expand, block),
            rows_spec(reduce, block),
        ],
        out_specs=[
            pl.BlockSpec((rows, width), whole),
            pl.BlockSpec((rows, block), lambda j: (0, j)),
        ],
        out_shape=[
            jax.ShapeDtypeStruct((rows, width), jnp.float32),
            jax.ShapeDtypeStruct((rows, hidden), jnp.float32),
        ],
        scratch_shapes=[VMEM((rows, 3 * width), NARROW)],
        compiler_params=pltpu.CompilerParams(vmem_limit_bytes=56 << 20),
        cost_estimate=pl.CostEstimate(
            flops=12 * rows * width * hidden, bytes_accessed=4 * rows * hidden, transcendentals=0
        ),
        name="feed_forward",
    )(middle, gain.reshape(1, width), expand, reduce)


def backward_kernel(
    piece, g_ref, m_ref, gain_ref, hidden_ref, expand_ref, reduce_ref,
    dm_ref, dgain_ref, dexpand_ref, dreduce_ref,
    wide, g_high, g_low, b_high, b_low, r_high, r_low, u_high, u_low, back,
):
    rows = g_ref.shape[0]

    @pl.when(pl.program_id(0) == 0)
    def _():
        def begin(at):
            g = g_ref[at, :]
            wide[at, :] = tripled(g, True)
            g_high[:, at], g_low[:, at] = split(g.T)
            normal = normal_parts(m_ref[at, :])[0] * gain_ref[...]
            b_high[:, at], b_low[:, at] = split(normal.T)
            back[at, :] = jnp.zeros_like(g)

        pieces_of(rows, piece, begin)

    expand, reduce = stacked(expand_ref[...].T), stacked(joined(reduce_ref).T)

    def go(at):
        hidden = hidden_ref[at, :]
        share = normal_share(hidden)
        r_high[at, :], r_low[at, :] = split(hidden * share)
        bell = jnp.exp(hidden * hidden * -0.5) * (1.0 / math.sqrt(2.0 * math.pi))
        slope = share + hidden * bell
        hidden_grad = slope * dot(wide[at, :], reduce)
        u_high[at, :], u_low[at, :] = split(hidden_grad)
        back[at, :] = back[at, :] + dot(tripled(hidden_grad, True), expand)

    pieces_of(rows, piece, go)
    grad = dot(g_high[...], r_high[...]) + dot(g_high[...], r_low[...])
    dreduce_ref[...] = (grad + dot(g_low[...], r_high[...])).T
    grad = dot(b_high[...], u_high[...]) + dot(b_high[...], u_low[...])
    dexpand_ref[...] = grad + dot(b_low[...], u_high[...])

    @pl.when(pl.program_id(0) == pl.num_programs(0) - 1)
    def _():
        dgain_ref[...] = jnp.zeros_like(dgain_ref)

        def finish(at):
            normal, inverse = normal_parts(m_ref[at, :])
            grad = back[at, :]
            dgain_ref[...] = dgain_ref[...] + jnp.sum(grad * normal, axis=0, keepdims=True)
            grad = grad * gain_ref[...]
            mean = jnp.mean(grad, axis=1, keepdims=True)
            along = jnp.mean(grad * normal, axis=1, keepdims=True)
            dm_ref[at, :] = g_ref[at, :] + inverse * (grad - mean - normal * along)

        pieces_of(rows, piece, finish)


def feed_backward(upstream, middle, gain, hidden_values, expand, reduce, block=256, piece=256):
    rows, width = middle.shape
    hidden = reduce.shape[-2]
    block = min(block, expand.shape[-1])
    whole = lambda j: (0, 0)
    once = pl.Buffered(1)
    dm, dgain, dexpand, dreduce = pl.pallas_call(
        partial(backward_kernel, min(piece, rows)),
        grid=(hidden // block,),
        in_specs=[
            pl.BlockSpec((rows, width), whole, pipeline_mode=once),
            pl.BlockSpec((rows, width), whole, pipeline_mode=once),
            pl.BlockSpec((1, width), whole),
            pl.BlockSpec((rows, block), lambda j: (0, j)),
            panels_spec(expand, block),
            rows_spec(reduce, block),
        ],
        out_specs=[
            pl.BlockSpec((rows, width), whole, pipeline_mode=once),
            pl.BlockSpec((1, width), whole),
            pl.BlockSpec((width, block), lambda j: (0, j)),
            pl.BlockSpec((block, width), lambda j: (j, 0)),
        ],
        out_shape=[
            jax.ShapeDtypeStruct((rows, width), jnp.float32),
            jax.ShapeDtypeStruct((1, width), jnp.float32),
            jax.ShapeDtypeStruct((width, hidden), jnp.float32),
            jax.ShapeDtypeStruct((hidden, width), jnp.float32),
        ],
        scratch_shapes=[
            VMEM((rows, 3 * width), NARROW),
            VMEM((width, rows), NARROW),
            VMEM((width, rows), NARROW),
            VMEM((width, rows), NARROW),
            VMEM((width, rows), NARROW),
            VMEM((rows, block), NARROW),
            VMEM((rows, block), NARROW),
            VMEM((rows, block), NARROW),
            VMEM((rows, block), NARROW),
            VMEM((rows, width), jnp.float32),
        ],
        compiler_params=pltpu.CompilerParams(vmem_limit_bytes=56 << 20),
        cost_estimate=pl.CostEstimate(
            flops=24 * rows * width * hidden, bytes_accessed=4 * rows * hidden, transcendentals=0
        ),
        name="feed_backward",
    )(upstream, middle, gain.reshape(1, width), hidden_values, expand, reduce)
    return dm, dgain[0], dexpand, dreduce


GATHER_TARGET = 60000
SCATTER_TARGET = 18000


precise = lax.Precision.HIGH
everywhere = ("dp", "fsdp")


def product(operand, factor):
    return jnp.dot(operand, factor, precision=precise, preferred_element_type=jnp.float32)


def transposed_left(operand, factor):
    return lax.dot_general(
        operand,
        factor,
        (((0,), (0,)), ((), ())),
        precision=precise,
        preferred_element_type=jnp.float32,
    )


def against(operand, factor):
    return lax.dot_general(
        operand,
        factor,
        (((1,), (1,)), ((), ())),
        precision=precise,
        preferred_element_type=jnp.float32,
    )


def normalize(values, gain_row):
    center = values - jnp.mean(values, axis=-1, keepdims=True)
    inverse = lax.rsqrt(jnp.mean(center * center, axis=-1, keepdims=True) + 1e-06)
    return center * inverse * gain_row


def position_table(length, breadth):
    half_width = breadth // 2
    indices = jnp.arange(length, dtype=jnp.float32)[:, None]
    frequency = jnp.exp(
        jnp.arange(half_width, dtype=jnp.float32) * (-math.log(10000.0) / half_width)
    )[None, :]
    angles = indices * frequency
    return jnp.concatenate([jnp.sin(angles), jnp.cos(angles)], axis=1)


def block_forward(states, gain_pair, matrices):
    first_norm, first_back = jax.vjp(normalize, states, gain_pair[0])
    packed = product(first_norm, matrices[0])
    mixture, logsum = attend_forward(packed)
    middle = states + product(mixture, matrices[1])
    result, hidden = feed_forward(middle, gain_pair[1], matrices[2], matrices[3])
    return result, (first_norm, first_back, packed, mixture, logsum, middle, hidden)


def block_backward(upstream, gain_pair, matrices, stored, beside, begins):
    first_norm, first_back, packed, mixture, logsum, middle, hidden = stored
    middle_grad, second_gain, expand_grad, reduce_grad = feed_backward(
        upstream, middle, gain_pair[1], hidden, matrices[2], matrices[3]
    )
    if begins:
        beside.begin([expand_grad, reduce_grad])
    middle_grad = beside.advance(middle_grad)
    merge_grad = transposed_left(mixture, middle_grad)
    mixture_grad = against(middle_grad, matrices[1])
    mixture_grad = beside.advance(mixture_grad)
    packed_grad = attend_backward(packed, mixture, logsum, mixture_grad)
    if begins:
        packed_grad = beside.advance(packed_grad)
    attend_grad = transposed_left(first_norm, packed_grad)
    states_part, first_gain = first_back(against(packed_grad, matrices[0]))
    gain_grads = jnp.stack([first_gain, second_gain])
    return (
        middle_grad + states_part,
        gain_grads,
        (attend_grad, merge_grad, expand_grad, reduce_grad),
    )


def collect(weights, collective_id):
    columns, rows = lax.axis_size("dp"), lax.axis_size("fsdp")
    if all(weight.shape[0] % 16 == 0 for weight in weights):
        wholes = gather(weights, columns, rows, collective_id, GATHER_TARGET)
        return [whole.reshape(-1, whole.shape[3]) for whole in wholes]
    return [
        lax.all_gather(
            lax.all_gather(weight, "dp", axis=1, tiled=True), "fsdp", axis=0, tiled=True
        )
        for weight in weights
    ]


def spread(gradients, small, collective_id):
    columns, rows = lax.axis_size("dp"), lax.axis_size("fsdp")
    if all(gradient.shape[0] % (rows * 16) == 0 for gradient in gradients):
        wholes = [
            gradient.reshape(4, rows // 4, gradient.shape[0] // rows, gradient.shape[1])
            for gradient in gradients
        ]
        return scatter(wholes, small, columns, rows, collective_id, SCATTER_TARGET)
    parts = [
        lax.psum_scatter(
            lax.psum_scatter(gradient, "fsdp", scatter_dimension=0, tiled=True),
            "dp",
            scatter_dimension=1,
            tiled=True,
        )
        for gradient in gradients
    ]
    return parts, (None if small is None else lax.psum(small, everywhere))


def exchange_steps(columns, rows, near_first):
    def bits(size):
        return [1 << place for place in reversed(range(size.bit_length() - 1))]

    across = [("dp", bit, 0) for bit in bits(columns) if bit > 1]
    far = [("fsdp", bit, 1) for bit in bits(rows) if bit >= rows // 4]
    near = [("fsdp", bit, 2) for bit in bits(rows) if bit < rows // 4]
    return near + across + far if near_first else across + near + far


class Beside:
    def __init__(self):
        self.views, self.steps = [], []

    def begin(self, gradients):
        columns, rows = lax.axis_size("dp"), lax.axis_size("fsdp")
        self.halves = []
        for place, gradient in enumerate(gradients):
            height, width = gradient.shape
            panels = [
                lax.slice_in_dim(gradient, start, start + width // columns, axis=1)
                for start in range(0, width, width // columns)
            ]
            self.halves.append((panels[::2], panels[1::2]))
            self.shape = lambda height, width: (columns // 2, 4, rows // 4, height // rows, width)
            self.steps.append([("dp", 1, None)] + exchange_steps(columns, rows, place % 2 == 0))

    def divided(self, place, upper, axis):
        if axis is not None:
            low, high = jnp.split(self.views[place], 2, axis=axis)
            return jnp.where(upper, high, low), jnp.where(upper, low, high)

        def choose(first, second):
            stack = jnp.stack([jnp.where(upper, a, b) for a, b in zip(first, second)])
            return stack.reshape(self.shape(*stack.shape[1:]))

        low, high = self.halves[place]
        return choose(high, low), choose(low, high)

    def advance(self, main):
        if not self.steps[0]:
            return main
        sent, kept, steps = [], [], [steps.pop(0) for steps in self.steps]
        for place, (name, bit, axis) in enumerate(steps):
            upper = jnp.bitwise_and(lax.axis_index(name), bit) != 0
            keep, send = self.divided(place, upper, axis)
            sent.append(send)
            kept.append(keep)
        main, sent = lax.optimization_barrier((main, sent))
        self.views = [
            keep
            + lax.ppermute(
                send, name, [(place, place ^ bit) for place in range(lax.axis_size(name))]
            )
            for send, keep, (name, bit, _) in zip(sent, kept, steps)
        ]
        return main

    def finish(self):
        while self.steps[0]:
            self.advance(jnp.zeros((), jnp.float32))
        return [view.reshape(view.shape[3:]) for view in self.views]


def collect_beside(weights):
    columns, rows = lax.axis_size("dp"), lax.axis_size("fsdp")
    attend, merge, expand, reduce = weights
    padded = jnp.pad(merge, ((0, 0), (0, attend.shape[1] - merge.shape[1])))
    both = lax.all_gather(jnp.concatenate([attend, padded], axis=0), everywhere, axis=0)

    def panels(blocks):
        return blocks.reshape(columns, rows * blocks.shape[1], blocks.shape[2])

    def whole(blocks):
        return jnp.concatenate(list(panels(blocks)), axis=1)

    height, times = expand.shape[0], expand.shape[1] // reduce.shape[1]
    beside = [reduce[start : start + height] for start in range(0, reduce.shape[0], height)]
    rest = lax.all_gather(
        jnp.concatenate([expand, jnp.concatenate(beside, axis=1)], axis=0), everywhere, axis=0
    )
    expand = panels(rest[:, :height])
    stretches = rest[:, height:].reshape(columns * rows, height, times, reduce.shape[1])
    reduce = panels(stretches.swapaxes(1, 2).reshape(columns * rows, *reduce.shape))
    if reduce.shape[2] % 128:
        expand, reduce = (jnp.concatenate(list(panel), axis=1) for panel in (expand, reduce))
    return [
        whole(both[:, : attend.shape[0]]),
        whole(both[:, attend.shape[0] :, : merge.shape[1]]),
        expand,
        reduce,
    ]


def pack_small(arrays):
    flat = jnp.concatenate([array.reshape(-1) for array in arrays])
    size = -(-flat.shape[0] // 1024) * 1024
    return jnp.pad(flat, (0, size - flat.shape[0])).reshape(-1, 128)


def unpack_small(packed, arrays):
    flat, start, out = packed.reshape(-1), 0, []
    for array in arrays:
        out.append(flat[start : start + array.size].reshape(array.shape))
        start += array.size
    return out


def place(choice, values):
    high = lax.reduce_precision(values, 8, 7)
    low = values - high
    wide = choice.astype(jnp.bfloat16)
    return jnp.dot(
        wide, high.astype(jnp.bfloat16), preferred_element_type=jnp.float32
    ) + jnp.dot(wide, low.astype(jnp.bfloat16), preferred_element_type=jnp.float32)


def local(
    tokens,
    sensor_tag,
    block_dest,
    block_order,
    sensor_table,
    encoder_gains,
    encoder_attend,
    encoder_merge,
    encoder_expand,
    encoder_reduce,
    bridge,
    mask_token,
    decoder_gains,
    decoder_attend,
    decoder_merge,
    decoder_expand,
    decoder_reduce,
    cotangent,
):
    groups = lax.axis_size("fsdp")
    visible = tokens.shape[0]
    capacity = 2 * visible // groups
    length = block_order.shape[1]
    breadth = mask_token.shape[0]
    destination = block_dest[:, 0]
    chooser = (destination[:, None] == jnp.arange(groups, dtype=jnp.int32)[None, :]).astype(
        jnp.int32
    )
    tallies = jnp.zeros((16, 128), jnp.float32)
    tallies = tallies.at[0, :groups].set(jnp.sum(chooser, axis=0).astype(jnp.float32))
    *encoder_set, all_tallies = collect(
        [encoder_attend, encoder_merge, encoder_expand, encoder_reduce, bridge, tallies], 1
    )
    mine = all_tallies.reshape(groups, 16, -1, 128)[:, 0]
    mine = lax.dynamic_index_in_dim(mine, lax.axis_index("dp"), axis=1, keepdims=False)
    arrived_tallies = lax.dynamic_slice_in_dim(mine, lax.axis_index("fsdp"), 1, axis=1)
    decoder_set = collect_beside(
        lax.optimization_barrier(
            (decoder_attend, decoder_merge, decoder_expand, decoder_reduce, encoder_set[4])
        )[:4]
    )
    tag_row = (
        sensor_tag[:, None] == jnp.arange(sensor_table.shape[0], dtype=jnp.int32)[None, :]
    ).astype(jnp.float32)
    initial = tokens + product(tag_row, sensor_table)
    encoded, encoder_kept = block_forward(initial, encoder_gains, encoder_set)
    projected = product(encoded, encoder_set[4])
    ranking = jnp.sum((jnp.cumsum(chooser, axis=0) - chooser) * chooser, axis=1)
    slot_index = destination * capacity + ranking
    select = (
        slot_index[None, :] == jnp.arange(groups * capacity, dtype=jnp.int32)[:, None]
    ).astype(jnp.float32)
    outgoing = place(select, projected).reshape(groups, capacity, breadth)
    arrived = lax.all_to_all(outgoing, "fsdp", split_axis=0, concat_axis=0, tiled=True)
    present = (jnp.arange(capacity, dtype=jnp.float32)[None, :] < arrived_tallies).reshape(-1)
    ordering = block_order[0, : groups * capacity]
    placing = (
        (ordering[None, :] == jnp.arange(length, dtype=jnp.int32)[:, None]) & present[None, :]
    ).astype(jnp.float32)
    covered = jnp.sum(placing, axis=1, keepdims=True)
    filled = (
        place(placing, arrived.reshape(groups * capacity, breadth))
        + (1.0 - covered) * mask_token
        + position_table(length, breadth)
    )
    decoded, decoder_kept = block_forward(filled, decoder_gains, decoder_set)
    beside = Beside()
    filled_grad, decoder_gain_grad, decoder_grads = block_backward(
        cotangent, decoder_gains, decoder_set, decoder_kept, beside, True
    )
    mask_grad = jnp.sum((1.0 - covered) * filled_grad, axis=0)
    arrived_grad = place(placing.T, filled_grad).reshape(groups, capacity, breadth)
    returned = lax.all_to_all(arrived_grad, "fsdp", split_axis=0, concat_axis=0, tiled=True)
    projected_grad = place(select.T, returned.reshape(groups * capacity, breadth))
    bridge_grad = transposed_left(encoded, projected_grad)
    encoded_grad = beside.advance(against(projected_grad, encoder_set[4]))
    tokens_grad, encoder_gain_grad, encoder_grads = block_backward(
        encoded_grad, encoder_gains, encoder_set, encoder_kept, beside, False
    )
    table_grad = transposed_left(tag_row, jnp.sum(tokens_grad, axis=0, keepdims=True))
    small = (table_grad, encoder_gain_grad, mask_grad, decoder_gain_grad)
    packed_small = pack_small(small)
    spreads, total = spread(
        [*encoder_grads, bridge_grad, decoder_grads[0], decoder_grads[1]], packed_small, 3
    )
    encoder_spread = spreads[:5]
    expand_sum, reduce_sum = beside.finish()
    decoder_spread = [spreads[5], spreads[6], expand_sum, reduce_sum]
    summed = unpack_small(total, small)
    return (
        decoded,
        tokens_grad,
        summed[0],
        summed[1],
        encoder_spread[0],
        encoder_spread[1],
        encoder_spread[2],
        encoder_spread[3],
        encoder_spread[4],
        summed[2],
        summed[3],
        decoder_spread[0],
        decoder_spread[1],
        decoder_spread[2],
        decoder_spread[3],
    )


def solution(mesh):
    in_specs = (
        P(("dp", "fsdp"), None),
        P(("dp", "fsdp")),
        P(("dp", "fsdp"), None),
        P(("dp", "fsdp"), None),
        P(),
        P(),
        P("fsdp", "dp"),
        P("fsdp", "dp"),
        P("fsdp", "dp"),
        P("fsdp", "dp"),
        P("fsdp", "dp"),
        P(),
        P(),
        P("fsdp", "dp"),
        P("fsdp", "dp"),
        P("fsdp", "dp"),
        P("fsdp", "dp"),
        P(("dp", "fsdp"), None),
    )
    out_specs = (
        P(("dp", "fsdp"), None),
        P(("dp", "fsdp"), None),
        P(),
        P(),
        P("fsdp", "dp"),
        P("fsdp", "dp"),
        P("fsdp", "dp"),
        P("fsdp", "dp"),
        P("fsdp", "dp"),
        P(),
        P(),
        P("fsdp", "dp"),
        P("fsdp", "dp"),
        P("fsdp", "dp"),
        P("fsdp", "dp"),
    )
    return jax.shard_map(local, mesh=mesh, in_specs=in_specs, out_specs=out_specs, check_vma=False)
```

```python
from functools import partial
import math

import jax
import jax.numpy as jnp
from jax import lax
from jax.experimental import pallas as pl
from jax.experimental.pallas import tpu as pltpu
from jax.sharding import PartitionSpec as P

MESH = pl.DeviceIdType.MESH
VMEM = pltpu.VMEM
NARROW = jnp.bfloat16
LONG = (("b", "a", "x"), ("x", "a", "b"))
SHORT = (("a", "x", "b"), ("a", "b", "x"))
GATHER_TURNS = (SHORT, LONG, LONG)
SCATTER_TURNS = (LONG, LONG, SHORT)
AHEAD = 2
SLACK = 2


class Grid:
    def __init__(self, dp, fsdp):
        self.size = {"x": dp // 2, "a": 4, "b": fsdp // 4}
        column, row = lax.axis_index("dp"), lax.axis_index("fsdp")
        self.core = lax.rem(column, 2)
        self.at = {
            "x": lax.div(column, 2),
            "a": lax.div(row, self.size["b"]),
            "b": lax.rem(row, self.size["b"]),
        }

    def device(self, core=None, **moved):
        at = {**self.at, **moved}
        core = self.core if core is None else core
        return (at["x"] * 2 + core, at["a"] * self.size["b"] + at["b"])

    def greet(self, reach):
        barrier = pltpu.get_barrier_semaphore()
        pl.semaphore_signal(
            barrier, inc=1, device_id=self.device(1 - self.core), device_id_type=MESH
        )
        count = 1
        for axis, size in self.size.items():
            here = self.at[axis]
            for move in range(-min(reach, size - 1), min(reach, size - 1) + 1):
                if move:
                    exists = together(here + move >= 0, here + move < size)
                    count = count + jnp.where(exists, 1, 0)

                    @pl.when(exists)
                    def _(axis=axis, here=here, move=move):
                        pl.semaphore_signal(
                            barrier,
                            inc=1,
                            device_id=self.device(**{axis: here + move}),
                            device_id_type=MESH,
                        )

        pl.semaphore_wait(barrier, count)


def plan_rounds(shapes, target, turns):
    plan, turn = [], 0
    for rows, columns in shapes:
        units = rows // 16
        pairs = max(1, min(units // 2, round(units * 8 * columns * 2 / target)))
        parts, start = [], 0
        for pair in range(pairs):
            orders = turns[turn % len(turns)]
            for place, order in enumerate(orders):
                take = -(-(units - start) // (2 * (pairs - pair) - place))
                if take:
                    parts.append((order, start * 8, take * 8, turn))
                start += take
            turn += 1
        plan.append(parts)
    return plan


def together(*conditions):
    joined = conditions[0]
    for condition in conditions[1:]:
        joined = jnp.logical_and(joined, condition)
    return joined


class Traffic:
    def __init__(self, grid, send, receive):
        self.grid, self.send, self.receive = grid, send, receive
        self.count, self.open = 0, []

    def copy(self, source, target, device, starts, arrives):
        place = self.count
        self.count += 1

        def made():
            return pltpu.make_async_remote_copy(
                src_ref=source,
                dst_ref=target,
                send_sem=self.send.at[place],
                recv_sem=self.receive.at[place],
                device_id=device,
                device_id_type=MESH,
            )

        if starts is None:
            made().start()
        else:

            @pl.when(starts)
            def _():
                made().start()

        self.open.append((made, starts))
        return (made, arrives)

    def arrive(self, handle):
        made, arrives = handle
        if arrives is None:
            made().wait_recv()
        else:

            @pl.when(arrives)
            def _():
                made().wait_recv()

    def take(self, handle):
        handle[0]().wait_recv()

    def drain(self, handle):
        handle[0]().wait_send()
        self.open = [entry for entry in self.open if entry[0] is not handle[0]]

    def close(self):
        for made, starts in self.open:
            if starts is None:
                made().wait_send()
            else:

                @pl.when(starts)
                def _():
                    made().wait_send()


def block_of(full, chosen, offset, rows, width):
    view = []
    for axis in ("a", "b"):
        place = chosen[axis]
        view.append(slice(None) if place is None else pl.ds(place, 1))
    columns = (
        slice(None)
        if chosen["x"] is None
        else pl.ds(pl.multiple_of(chosen["x"] * width, 128), width)
    )
    return full.at[(*view, pl.ds(pl.multiple_of(offset, 8), rows), columns)]


def pause():
    for _ in range(SLACK):
        yield


def gather_line(traffic, axis, chosen, view, exists, arrived):
    grid = traffic.grid
    here, size = grid.at[axis], grid.size[axis]

    def both(condition):
        return condition if exists is None else together(exists, condition)

    arrived({**chosen, axis: here}, exists)
    for step in range(1, size):
        ahead, behind = {**chosen, axis: here - (step - 1)}, {**chosen, axis: here + (step - 1)}
        rightward = traffic.copy(
            view(ahead),
            view(ahead),
            grid.device(**{axis: here + 1}),
            both(together(here + 1 < size, here - (step - 1) >= 0)),
            both(here - step >= 0),
        )
        leftward = traffic.copy(
            view(behind),
            view(behind),
            grid.device(**{axis: here - 1}),
            both(together(here - 1 >= 0, here + (step - 1) < size)),
            both(here + step < size),
        )
        yield from pause()
        traffic.arrive(rightward)
        arrived({**chosen, axis: here - step}, both(here - step >= 0))
        traffic.arrive(leftward)
        arrived({**chosen, axis: here + step}, both(here + step < size))


def gather_part(traffic, order, view, spawn, share):
    first, second, third = order
    grid = traffic.grid
    own = dict(grid.at)

    def last(chosen, exists):
        def finish():
            yield from gather_line(traffic, third, chosen, view, exists, lambda *_: None)
            share(view({**chosen, third: None}), exists)

        spawn(finish())

    def begin():
        if grid.size[first] == 2:
            yield from gather_line(traffic, first, own, view, None, lambda *_: None)
            yield from gather_line(traffic, second, {**own, first: None}, view, None, last)
        else:

            def middle(chosen, exists):
                def go():
                    yield from gather_line(traffic, second, chosen, view, exists, lambda *_: None)
                    last({**chosen, second: None}, exists)

                spawn(go())

            yield from gather_line(traffic, first, own, view, None, middle)

    spawn(begin())


def run_rounds(starts):
    active = []

    def spawn(generator):
        try:
            next(generator)
            active.append(generator)
        except StopIteration:
            pass

    for start in starts:
        for begin in start:
            begin(spawn)
        advance_all(active)
    while active:
        advance_all(active)


def advance_all(active):
    for generator in list(active):
        try:
            next(generator)
        except StopIteration:
            active.remove(generator)


def gather_kernel(dp, fsdp, shapes, plan, *refs):
    number = len(shapes)
    shards, wholes = refs[:number], refs[number : 2 * number]
    raws, blocks = refs[2 * number : 3 * number], refs[3 * number : 4 * number]
    send, receive, pair_send, pair_receive, local = refs[4 * number :]
    grid = Grid(dp, fsdp)
    traffic = Traffic(grid, send, receive)
    pair = Traffic(grid, pair_send, pair_receive)
    core, other = grid.core, 1 - grid.core
    sibling = grid.device(other)
    grid.greet(1)
    handles = []
    for index, (rows, columns) in enumerate(shapes):
        half = rows // 2
        theirs = shards[index].at[pl.ds(pl.multiple_of(other * half, 8), half)]
        handles.append(pair.copy(theirs, raws[index], sibling, None, None))
    stores = []
    for index, (rows, columns) in enumerate(shapes):
        half = rows // 2
        pair.arrive(handles[index])
        mine = shards[index][pl.ds(pl.multiple_of(core * half, 8), half), :]
        came = raws[index][...]
        blocks[index][0, 0] = jnp.where(
            core == 0,
            jnp.concatenate([mine, came], axis=1),
            jnp.concatenate([came, mine], axis=1),
        )
        store = pltpu.make_async_copy(
            blocks[index],
            block_of(wholes[index], grid.at, core * half, half, 2 * columns),
            local.at[index],
        )
        store.start()
        stores.append(store)
    for store in stores:
        store.wait()
    pending = []

    def share(piece, exists):
        pending.append(pair.copy(piece, piece, sibling, exists, exists))

    starts = [[] for _ in range(1 + max(part[3] for parts in plan for part in parts))]
    for index, (rows, columns) in enumerate(shapes):
        half = rows // 2
        for order, offset, count, turn in plan[index]:

            def view(chosen, index=index, offset=offset, count=count, half=half, columns=columns):
                return block_of(wholes[index], chosen, core * half + offset, count, 2 * columns)

            starts[turn].append(
                lambda spawn, order=order, view=view: gather_part(
                    traffic, order, view, spawn, share
                )
            )
    run_rounds(starts)
    for handle in pending:
        pair.arrive(handle)
    traffic.close()
    pair.close()


def gather(weights, dp, fsdp, collective_id, target):
    shapes = [weight.shape for weight in weights]
    a, b = 4, fsdp // 4
    plan = plan_rounds(shapes, target, GATHER_TURNS)
    total = sum(len(parts) for parts in plan)
    out = [jax.ShapeDtypeStruct((a, b, r, dp * c), jnp.float32) for r, c in shapes]
    vmem = pl.BlockSpec(memory_space=VMEM)
    return pl.pallas_call(
        partial(gather_kernel, dp, fsdp, shapes, plan),
        out_shape=out,
        in_specs=[vmem] * len(shapes),
        out_specs=[pl.BlockSpec(memory_space=pl.ANY)] * len(shapes),
        scratch_shapes=[VMEM((r // 2, c), jnp.float32) for r, c in shapes]
        + [VMEM((1, 1, r // 2, 2 * c), jnp.float32) for r, c in shapes]
        + [
            pltpu.SemaphoreType.DMA((34 * total,)),
            pltpu.SemaphoreType.DMA((34 * total,)),
            pltpu.SemaphoreType.DMA((8 * total + len(shapes),)),
            pltpu.SemaphoreType.DMA((8 * total + len(shapes),)),
            pltpu.SemaphoreType.DMA((len(shapes),)),
        ],
        compiler_params=pltpu.CompilerParams(
            collective_id=collective_id, has_side_effects=True, vmem_limit_bytes=32 << 20
        ),
        name="gather_weights",
    )(*weights)


def landing_shapes(size, order, rows, width):
    chosen, shapes = {"x": size["x"], "a": size["a"], "b": size["b"]}, []
    for axis in reversed(order):
        chosen[axis] = 1
        slots = 1 if size[axis] == 2 else 2 * (size[axis] - 1)
        shapes.append((slots, chosen["a"], chosen["b"], rows, chosen["x"] * width))
    return shapes


def sum_line(traffic, axis, chosen, view, landing):
    grid = traffic.grid
    here, size = grid.at[axis], grid.size[axis]
    ends = size - 1

    def slot(rightward, place):
        if size == 2:
            return 0
        return place - 1 if rightward else ends + place

    def blocks(place):
        return view({**chosen, axis: place})

    def add(rightward, place):
        target = blocks(place)
        target[...] += landing[slot(rightward, place)]

    def send(rightward, place, starts, arrives):
        return traffic.copy(
            blocks(place),
            landing.at[slot(rightward, place)],
            grid.device(**{axis: here + (1 if rightward else -1)}),
            starts,
            arrives,
        )

    first = {}
    for place in range(ends, 0, -1):
        first[True, place] = send(
            True, place, here == 0, here == 1
        )
    for place in range(ends):
        first[False, place] = send(False, place, here == ends, here == ends - 1)
    later = {}
    for step in range(ends - 1):
        yield from pause()
        for come in range(1, ends):
            place = ends - step + come - 1
            if come < place <= ends:
                @pl.when(here == come)
                def _(come=come, place=place):
                    traffic.take(first[True, place] if come == 1 else later[True, come - 1, place])
                    add(True, place)

                later[True, come, place] = send(True, place, here == come, here == come + 1)
            come, place = ends - come, ends - place
            if come > place >= 0:

                @pl.when(here == come)
                def _(come=come, place=place):
                    traffic.take(
                        first[False, place] if come == ends - 1 else later[False, come + 1, place]
                    )
                    add(False, place)

                later[False, come, place] = send(False, place, here == come, here == come - 1)
    yield from pause()
    for place in range(size):

        @pl.when(here == place)
        def _(place=place):
            if place > 0:
                traffic.take(first[True, place] if place == 1 else later[True, place - 1, place])
                add(True, place)
            if place < ends:
                traffic.take(
                    first[False, place] if place == ends - 1 else later[False, place + 1, place]
                )
                add(False, place)


def sum_part(traffic, order, view, landings):
    chosen = {"x": None, "a": None, "b": None}
    for axis, landing in zip(reversed(order), landings):
        yield from sum_line(traffic, axis, chosen, view, landing)
        chosen[axis] = traffic.grid.at[axis]


def total_everywhere(traffic, pair, value, pair_landing, landings):
    grid = traffic.grid
    came = pair.copy(value, pair_landing, grid.device(1 - grid.core), None, None)
    yield
    pair.arrive(came)
    pair.drain(came)
    value[...] += pair_landing[...]
    for axis, landing in zip(("x", "b", "a"), landings):
        here, size = grid.at[axis], grid.size[axis]
        handles = []
        for move in range(1, size):
            target = lax.rem(here + move, size)
            source = lax.rem(here + size - move, size)
            handles.append(
                (
                    traffic.copy(
                        value, landing.at[here], grid.device(**{axis: target}), None, None
                    ),
                    source,
                )
            )
        landing[here] = value[...]
        yield
        for handle, _ in handles:
            traffic.arrive(handle)
            traffic.drain(handle)
        total = landing[0]
        for place in range(1, size):
            total = total + landing[place]
        value[...] = total


def scatter_kernel(dp, fsdp, shapes, pieces, has_small, *refs):
    number = len(shapes)
    refs = list(refs)

    def take(count):
        taken = refs[:count]
        del refs[:count]
        return taken

    wholes, small = take(number), (take(1)[0] if has_small else None)
    outs, small_out = take(number), (take(1)[0] if has_small else None)
    sums, others, finals = take(number), take(number), take(number)
    landings = [[take(3) for _ in parts] for parts in pieces]
    if has_small:
        small_pair, *small_landings = take(4)
    send, receive, pair_send, pair_receive, local = refs
    grid = Grid(dp, fsdp)
    traffic = Traffic(grid, send, receive)
    pair = Traffic(grid, pair_send, pair_receive)
    core, other = grid.core, 1 - grid.core
    sibling = grid.device(other)
    grid.greet(max(grid.size.values()) if small is not None else 1)
    starts = [[] for _ in range(1 + max(part[3] for parts in pieces for part in parts))]
    if has_small:
        small_out[...] = small[...]
        starts[0].append(
            lambda spawn: spawn(
                total_everywhere(traffic, pair, small_out, small_pair, small_landings)
            )
        )
    place, runs = 0, []
    for index, (rows, columns) in enumerate(shapes):
        half = rows // 2
        for part, (order, offset, count, turn) in enumerate(pieces[index]):
            window = (slice(None), slice(None), slice(offset, offset + count))
            fetched = []

            def fetch(index=index, half=half, offset=offset, count=count, window=window,
                      fetched=fetched, place=place):
                def stretch(at):
                    start = pl.multiple_of(at * half + offset, 8)
                    return wholes[index].at[:, :, pl.ds(start, count), :]

                came = pair.copy(stretch(other), others[index].at[window], sibling, None, None)
                load = pltpu.make_async_copy(
                    stretch(core), sums[index].at[window], local.at[place]
                )
                load.start()
                fetched.extend((came, load))

            ahead = max(0, turn - AHEAD)
            starts[ahead].append(lambda spawn, fetch=fetch: fetch())
            place += 1

            def run(index=index, order=order, offset=offset, count=count, window=window,
                    fetched=fetched, columns=columns, part=part):
                fetched[1].wait()
                pair.arrive(fetched[0])
                sums[index][window] += others[index][window]

                def view(chosen):
                    return block_of(sums[index], chosen, offset, count, 2 * columns)

                yield from sum_part(traffic, order, view, landings[index][part])

            runs.append((turn, lambda spawn, run=run: spawn(run())))
    for turn, run in runs:
        starts[turn].append(run)
    run_rounds(starts)
    handles = []
    for index, (rows, columns) in enumerate(shapes):
        half = rows // 2
        block = block_of(sums[index], grid.at, 0, half, 2 * columns)
        handles.append(pair.copy(block, finals[index], sibling, None, None))
    for index, (rows, columns) in enumerate(shapes):
        half = rows // 2
        block = block_of(sums[index], grid.at, 0, half, 2 * columns)[0, 0]
        pair.arrive(handles[index])
        came = finals[index][0, 0]
        for value, at in ((block, core), (came, other)):
            outs[index][pl.ds(pl.multiple_of(at * half, 8), half), :] = jnp.where(
                core == 0, value[:, :columns], value[:, columns:]
            )
    traffic.close()
    pair.close()


def scatter(wholes, small, dp, fsdp, collective_id, target):
    size = {"x": dp // 2, "a": 4, "b": fsdp // 4}
    shapes = [(whole.shape[2], whole.shape[3] // dp) for whole in wholes]
    pieces = plan_rounds(shapes, target, SCATTER_TURNS)
    number = len(shapes)
    total = sum(len(parts) for parts in pieces)
    scratch = []
    for _ in range(2):
        scratch += [VMEM((size["a"], size["b"], r // 2, dp * c), jnp.float32) for r, c in shapes]
    scratch += [VMEM((1, 1, r // 2, 2 * c), jnp.float32) for r, c in shapes]
    for (rows, columns), parts in zip(shapes, pieces):
        for order, _, count, _ in parts:
            for shape in landing_shapes(size, order, count, 2 * columns):
                scratch.append(VMEM(shape, jnp.float32))
    smalls = [] if small is None else [small]
    for array in smalls:
        scratch.append(VMEM(array.shape, jnp.float32))
        for axis in ("x", "b", "a"):
            scratch.append(VMEM((size[axis], *array.shape), jnp.float32))
    hops = 2 * sum(size.values()) + sum((length - 1) * length for length in size.values())
    scratch += [
        pltpu.SemaphoreType.DMA((total * hops + 40,)),
        pltpu.SemaphoreType.DMA((total * hops + 40,)),
        pltpu.SemaphoreType.DMA((total + number + 1,)),
        pltpu.SemaphoreType.DMA((total + number + 1,)),
        pltpu.SemaphoreType.DMA((total,)),
    ]
    vmem = pl.BlockSpec(memory_space=VMEM)
    results = pl.pallas_call(
        partial(scatter_kernel, dp, fsdp, shapes, pieces, small is not None),
        out_shape=[jax.ShapeDtypeStruct(shape, jnp.float32) for shape in shapes]
        + [jax.ShapeDtypeStruct(array.shape, jnp.float32) for array in smalls],
        in_specs=[pl.BlockSpec(memory_space=pl.ANY)] * number + [vmem] * len(smalls),
        out_specs=[vmem] * (number + len(smalls)),
        scratch_shapes=scratch,
        compiler_params=pltpu.CompilerParams(
            collective_id=collective_id, has_side_effects=True, vmem_limit_bytes=60 << 20
        ),
        name="scatter_sums",
    )(*wholes, *smalls)
    return results[:number], (results[number] if smalls else None)


HEAD = 64


def split(values):
    high = values.astype(NARROW)
    return high, (values - high.astype(jnp.float32)).astype(NARROW)


def tripled(values, leading):
    high, low = split(values)
    return jnp.concatenate([high, high, low] if leading else [high, low, high], axis=1)


def dot(left, right, contract=(1, 0)):
    return lax.dot_general(
        left,
        right,
        (((contract[0],), (contract[1],)), ((), ())),
        preferred_element_type=jnp.float32,
    )


def attend_kernel(chunk, q_ref, k_ref, v_ref, out_ref, lse_ref, keys, values, scores, high, low):
    rows = q_ref.shape[0]

    @pl.when(pl.program_id(1) == 0)
    def _():
        for head in range(2):
            part = slice(head * HEAD, (head + 1) * HEAD)
            keys[head] = tripled(k_ref[:, part], False)
            values[head] = jnp.concatenate(split(v_ref[:, part]), axis=1)

    outs, stats = [], []
    for head in range(2):
        part = slice(head * HEAD, (head + 1) * HEAD)
        queries = tripled(q_ref[:, part] * (1.0 / math.sqrt(HEAD)), True)
        scores[...] = dot(queries, keys[head], (1, 1))

        def body(step, _):
            at = pl.ds(pl.multiple_of(step * chunk, chunk), chunk)
            piece = scores[at, :]
            top = jnp.max(piece, axis=1, keepdims=True)
            weights = jnp.exp(piece - top)
            total = jnp.sum(weights, axis=1, keepdims=True)
            first, second = split(weights)
            high[at, :] = first
            low[at, :] = second
            lse_ref[at, head : head + 1] = top + jnp.log(total)
            lse_ref[at, 2 + head : 3 + head] = 1.0 / total
            return 0

        lax.fori_loop(0, rows // chunk, body, 0, unroll=2)
        both = dot(high[...], values[head])
        outs.append(
            (both[:, :HEAD] + both[:, HEAD:] + dot(low[...], values[head][:, :HEAD]))
            * lse_ref[:, 2 + head : 3 + head]
        )
    out_ref[...] = jnp.concatenate(outs, axis=1)


def attend_forward(packed, block=768, chunk=128):
    rows, breadth = packed.shape[0], packed.shape[1] // 3
    pairs = breadth // 128
    block = min(block, rows)
    return pl.pallas_call(
        partial(attend_kernel, chunk),
        grid=(pairs, rows // block),
        in_specs=[
            pl.BlockSpec((block, 128), lambda h, i: (i, h)),
            pl.BlockSpec((rows, 128), lambda h, i: (0, pairs + h)),
            pl.BlockSpec((rows, 128), lambda h, i: (0, 2 * pairs + h)),
        ],
        out_specs=[
            pl.BlockSpec((block, 128), lambda h, i: (i, h)),
            pl.BlockSpec((None, block, 128), lambda h, i: (h, i, 0)),
        ],
        out_shape=[
            jax.ShapeDtypeStruct((rows, breadth), jnp.float32),
            jax.ShapeDtypeStruct((pairs, rows, 128), jnp.float32),
        ],
        scratch_shapes=[
            VMEM((2, rows, 3 * HEAD), NARROW),
            VMEM((2, rows, 2 * HEAD), NARROW),
            VMEM((block, rows), jnp.float32),
            VMEM((block, rows), NARROW),
            VMEM((block, rows), NARROW),
        ],
        compiler_params=pltpu.CompilerParams(vmem_limit_bytes=48 << 20),
        cost_estimate=pl.CostEstimate(
            flops=12 * rows * rows * breadth, bytes_accessed=20 * rows * breadth, transcendentals=0
        ),
        name="attend_forward",
    )(packed, packed, packed)


def attend_back_kernel(
    chunk, q_ref, k_ref, v_ref, o_ref, g_ref, lse_ref, dq_ref, dk_ref, dv_ref,
    queries, gradients, wide_q, wide_g, row_lse, row_delta, dq, scores, other,
    p_high, p_low, s_high, s_low,
):
    rows, block = q_ref.shape[0], k_ref.shape[0]
    scale = 1.0 / math.sqrt(HEAD)

    @pl.when(pl.program_id(1) == 0)
    def _():
        for head in range(2):
            part = slice(head * HEAD, (head + 1) * HEAD)
            q = q_ref[:, part] * scale
            g = g_ref[:, part]
            queries[head] = tripled(q, True).T
            gradients[head] = tripled(g, True).T
            wide_q[head] = jnp.concatenate(split(q), axis=1)
            wide_g[head] = jnp.concatenate(split(g), axis=1)
            delta = jnp.sum(g * o_ref[:, part], axis=1, keepdims=True)
            row_delta[head] = jnp.broadcast_to(delta, (rows, 128)).T[:8]
            row_lse[head] = jnp.broadcast_to(lse_ref[:, head : head + 1], (rows, 128)).T[:8]
        dq[...] = jnp.zeros_like(dq)

    dks, dvs = [], []
    for head in range(2):
        part = slice(head * HEAD, (head + 1) * HEAD)
        k = k_ref[:, part]
        scores[...] = dot(tripled(k, False), queries[head])
        other[...] = dot(tripled(v_ref[:, part], False), gradients[head])
        lse = row_lse[head, 0:1]
        delta = row_delta[head, 0:1]

        def body(step, _):
            at = pl.ds(pl.multiple_of(step * chunk, chunk), chunk)
            weights = jnp.exp(scores[at, :] - lse)
            p_high[at, :], p_low[at, :] = split(weights)
            s_high[at, :], s_low[at, :] = split(weights * (other[at, :] - delta))
            return 0

        lax.fori_loop(0, block // chunk, body, 0, unroll=2)
        both = dot(p_high[...], wide_g[head])
        dvs.append(both[:, :HEAD] + both[:, HEAD:] + dot(p_low[...], wide_g[head][:, :HEAD]))
        both = dot(s_high[...], wide_q[head])
        dks.append(both[:, :HEAD] + both[:, HEAD:] + dot(s_low[...], wide_q[head][:, :HEAD]))
        kt = jnp.concatenate(split(k * scale), axis=1).T
        both = dot(kt, s_high[...])
        dq[head] += both[:HEAD] + both[HEAD:] + dot(kt[:HEAD], s_low[...])
    dk_ref[...] = jnp.concatenate(dks, axis=1)
    dv_ref[...] = jnp.concatenate(dvs, axis=1)

    @pl.when(pl.program_id(1) == pl.num_programs(1) - 1)
    def _():
        for head in range(2):
            dq_ref[:, head * HEAD : (head + 1) * HEAD] = dq[head].T


def attend_backward(packed, mixture, lse, upstream, block=512, chunk=128):
    rows, breadth = mixture.shape
    pairs = breadth // 128
    block = min(block, rows)
    whole = lambda h, i: (0, h)
    stretch = lambda h, i: (i, h)
    parts = pl.pallas_call(
        partial(attend_back_kernel, chunk),
        grid=(pairs, rows // block),
        in_specs=[
            pl.BlockSpec((rows, 128), whole),
            pl.BlockSpec((block, 128), lambda h, i: (i, pairs + h)),
            pl.BlockSpec((block, 128), lambda h, i: (i, 2 * pairs + h)),
            pl.BlockSpec((rows, 128), whole),
            pl.BlockSpec((rows, 128), whole),
            pl.BlockSpec((None, rows, 128), lambda h, i: (h, 0, 0)),
        ],
        out_specs=[
            pl.BlockSpec((rows, 128), whole),
            pl.BlockSpec((block, 128), stretch),
            pl.BlockSpec((block, 128), stretch),
        ],
        out_shape=[jax.ShapeDtypeStruct((rows, breadth), jnp.float32)] * 3,
        scratch_shapes=[
            VMEM((2, 3 * HEAD, rows), NARROW),
            VMEM((2, 3 * HEAD, rows), NARROW),
            VMEM((2, rows, 2 * HEAD), NARROW),
            VMEM((2, rows, 2 * HEAD), NARROW),
            VMEM((2, 8, rows), jnp.float32),
            VMEM((2, 8, rows), jnp.float32),
            VMEM((2, HEAD, rows), jnp.float32),
            VMEM((block, rows), jnp.float32),
            VMEM((block, rows), jnp.float32),
            VMEM((block, rows), NARROW),
            VMEM((block, rows), NARROW),
            VMEM((block, rows), NARROW),
            VMEM((block, rows), NARROW),
        ],
        compiler_params=pltpu.CompilerParams(vmem_limit_bytes=48 << 20),
        cost_estimate=pl.CostEstimate(
            flops=30 * rows * rows * breadth, bytes_accessed=32 * rows * breadth, transcendentals=0
        ),
        name="attend_backward",
    )(packed, packed, packed, mixture, upstream, lse)
    return jnp.concatenate(parts, axis=1)


def stacked(values):
    high, low = split(values)
    return jnp.concatenate([high, low, high], axis=0)


def normal_parts(values):
    center = values - jnp.mean(values, axis=1, keepdims=True)
    inverse = lax.rsqrt(jnp.mean(center * center, axis=1, keepdims=True) + 1e-06)
    return center * inverse, inverse


def pieces_of(rows, size, body):
    for start in range(0, rows, size):
        body(slice(start, min(start + size, rows)))


def normal_share(values):
    return 0.5 + 0.5 * lax.erf(values * math.sqrt(0.5))


def weight_specs(expand, reduce, block):
    if expand.ndim == 2:
        return [
            pl.BlockSpec((expand.shape[0], block), lambda j: (0, j)),
            pl.BlockSpec((block, reduce.shape[1]), lambda j: (j, 0)),
        ]
    columns, rows, height, width = expand.shape
    each, deep = width // block, block // (columns * height // 2)
    return [
        pl.BlockSpec(
            (None, rows, height // 2, block), lambda j: (lax.div(j, each), 0, 0, lax.rem(j, each))
        ),
        pl.BlockSpec((columns, deep, height // 2, width), lambda j: (0, j, 1, 0)),
    ]


def hidden_units(expand):
    return expand.shape[1] if expand.ndim == 2 else expand.shape[0] * expand.shape[3]


def expand_of(ref):
    if len(ref.shape) == 2:
        return ref[...]
    return ref[...].reshape(ref.shape[0] * ref.shape[1], ref.shape[2])


def reduce_of(ref):
    if len(ref.shape) == 2:
        return ref[...]
    columns, deep, _, width = ref.shape
    share = width // columns
    return jnp.concatenate(
        [
            jnp.concatenate(
                [ref[column, row, :, part * share : (part + 1) * share] for column in range(columns)],
                axis=1,
            )
            for row in range(deep)
            for part in range(columns)
        ],
        axis=0,
    )


def forward_kernel(piece, m_ref, gain_ref, expand_ref, reduce_ref, out_ref, hidden_ref, wide):
    rows = m_ref.shape[0]

    @pl.when(pl.program_id(0) == 0)
    def _():
        def begin(at):
            wide[at, :] = tripled(normal_parts(m_ref[at, :])[0] * gain_ref[...], True)
            out_ref[at, :] = m_ref[at, :]

        pieces_of(rows, piece, begin)

    expand, reduce = stacked(expand_of(expand_ref)), stacked(reduce_of(reduce_ref))

    def go(at):
        hidden = dot(wide[at, :], expand)
        hidden_ref[at, :] = hidden
        active = hidden * normal_share(hidden)
        out_ref[at, :] = out_ref[at, :] + dot(tripled(active, True), reduce)

    pieces_of(rows, piece, go)


def feed_forward(middle, gain, expand, reduce, block=512, piece=512):
    rows, width = middle.shape
    hidden = hidden_units(expand)
    whole = lambda j: (0, 0)
    return pl.pallas_call(
        partial(forward_kernel, min(piece, rows)),
        grid=(hidden // block,),
        in_specs=[
            pl.BlockSpec((rows, width), whole),
            pl.BlockSpec((1, width), whole),
            *weight_specs(expand, reduce, block),
        ],
        out_specs=[
            pl.BlockSpec((rows, width), whole),
            pl.BlockSpec((rows, block), lambda j: (0, j)),
        ],
        out_shape=[
            jax.ShapeDtypeStruct((rows, width), jnp.float32),
            jax.ShapeDtypeStruct((rows, hidden), jnp.float32),
        ],
        scratch_shapes=[VMEM((rows, 3 * width), NARROW)],
        compiler_params=pltpu.CompilerParams(vmem_limit_bytes=56 << 20),
        cost_estimate=pl.CostEstimate(
            flops=12 * rows * width * hidden, bytes_accessed=4 * rows * hidden, transcendentals=0
        ),
        name="feed_forward",
    )(middle, gain.reshape(1, width), expand, reduce)


def backward_kernel(
    piece, g_ref, m_ref, gain_ref, hidden_ref, expand_ref, reduce_ref,
    dm_ref, dgain_ref, dexpand_ref, dreduce_ref,
    wide, g_high, g_low, b_high, b_low, r_high, r_low, u_high, u_low, back,
):
    rows = g_ref.shape[0]

    @pl.when(pl.program_id(0) == 0)
    def _():
        def begin(at):
            g = g_ref[at, :]
            wide[at, :] = tripled(g, True)
            g_high[:, at], g_low[:, at] = split(g.T)
            normal = normal_parts(m_ref[at, :])[0] * gain_ref[...]
            b_high[:, at], b_low[:, at] = split(normal.T)
            back[at, :] = jnp.zeros_like(g)

        pieces_of(rows, piece, begin)

    expand, reduce = stacked(expand_of(expand_ref).T), stacked(reduce_of(reduce_ref).T)

    def go(at):
        hidden = hidden_ref[at, :]
        share = normal_share(hidden)
        r_high[at, :], r_low[at, :] = split(hidden * share)
        bell = jnp.exp(hidden * hidden * -0.5) * (1.0 / math.sqrt(2.0 * math.pi))
        slope = share + hidden * bell
        hidden_grad = slope * dot(wide[at, :], reduce)
        u_high[at, :], u_low[at, :] = split(hidden_grad)
        back[at, :] = back[at, :] + dot(tripled(hidden_grad, True), expand)

    pieces_of(rows, piece, go)
    grad = dot(g_high[...], r_high[...]) + dot(g_high[...], r_low[...])
    dreduce_ref[...] = (grad + dot(g_low[...], r_high[...])).T
    grad = dot(b_high[...], u_high[...]) + dot(b_high[...], u_low[...])
    dexpand_ref[...] = grad + dot(b_low[...], u_high[...])

    @pl.when(pl.program_id(0) == pl.num_programs(0) - 1)
    def _():
        dgain_ref[...] = jnp.zeros_like(dgain_ref)

        def finish(at):
            normal, inverse = normal_parts(m_ref[at, :])
            grad = back[at, :]
            dgain_ref[...] = dgain_ref[...] + jnp.sum(grad * normal, axis=0, keepdims=True)
            grad = grad * gain_ref[...]
            mean = jnp.mean(grad, axis=1, keepdims=True)
            along = jnp.mean(grad * normal, axis=1, keepdims=True)
            dm_ref[at, :] = g_ref[at, :] + inverse * (grad - mean - normal * along)

        pieces_of(rows, piece, finish)


def feed_backward(upstream, middle, gain, hidden_values, expand, reduce):
    rows, width = middle.shape
    hidden = hidden_units(expand)
    block, piece = (512, rows) if rows <= 512 else (256, 256)
    whole = lambda j: (0, 0)
    once = pl.Buffered(1)
    dm, dgain, dexpand, dreduce = pl.pallas_call(
        partial(backward_kernel, min(piece, rows)),
        grid=(hidden // block,),
        in_specs=[
            pl.BlockSpec((rows, width), whole, pipeline_mode=once),
            pl.BlockSpec((rows, width), whole, pipeline_mode=once),
            pl.BlockSpec((1, width), whole),
            pl.BlockSpec((rows, block), lambda j: (0, j)),
            *weight_specs(expand, reduce, block),
        ],
        out_specs=[
            pl.BlockSpec((rows, width), whole, pipeline_mode=once),
            pl.BlockSpec((1, width), whole),
            pl.BlockSpec((width, block), lambda j: (0, j)),
            pl.BlockSpec((block, width), lambda j: (j, 0)),
        ],
        out_shape=[
            jax.ShapeDtypeStruct((rows, width), jnp.float32),
            jax.ShapeDtypeStruct((1, width), jnp.float32),
            jax.ShapeDtypeStruct((width, hidden), jnp.float32),
            jax.ShapeDtypeStruct((hidden, width), jnp.float32),
        ],
        scratch_shapes=[
            VMEM((rows, 3 * width), NARROW),
            VMEM((width, rows), NARROW),
            VMEM((width, rows), NARROW),
            VMEM((width, rows), NARROW),
            VMEM((width, rows), NARROW),
            VMEM((rows, block), NARROW),
            VMEM((rows, block), NARROW),
            VMEM((rows, block), NARROW),
            VMEM((rows, block), NARROW),
            VMEM((rows, width), jnp.float32),
        ],
        compiler_params=pltpu.CompilerParams(vmem_limit_bytes=56 << 20),
        cost_estimate=pl.CostEstimate(
            flops=24 * rows * width * hidden, bytes_accessed=4 * rows * hidden, transcendentals=0
        ),
        name="feed_backward",
    )(upstream, middle, gain.reshape(1, width), hidden_values, expand, reduce)
    return dm, dgain[0], dexpand, dreduce


GATHER_TARGET = 60000
SCATTER_TARGET = 26000


precise = lax.Precision.HIGH
everywhere = ("dp", "fsdp")


def product(operand, factor):
    return jnp.dot(operand, factor, precision=precise, preferred_element_type=jnp.float32)


def transposed_left(operand, factor):
    return lax.dot_general(
        operand,
        factor,
        (((0,), (0,)), ((), ())),
        precision=precise,
        preferred_element_type=jnp.float32,
    )


def against(operand, factor):
    return lax.dot_general(
        operand,
        factor,
        (((1,), (1,)), ((), ())),
        precision=precise,
        preferred_element_type=jnp.float32,
    )


def normalize(values, gain_row):
    center = values - jnp.mean(values, axis=-1, keepdims=True)
    inverse = lax.rsqrt(jnp.mean(center * center, axis=-1, keepdims=True) + 1e-06)
    return center * inverse * gain_row


def position_table(length, breadth):
    half_width = breadth // 2
    indices = jnp.arange(length, dtype=jnp.float32)[:, None]
    frequency = jnp.exp(
        jnp.arange(half_width, dtype=jnp.float32) * (-math.log(10000.0) / half_width)
    )[None, :]
    angles = indices * frequency
    return jnp.concatenate([jnp.sin(angles), jnp.cos(angles)], axis=1)


def block_forward(states, gain_pair, matrices):
    first_norm, first_back = jax.vjp(normalize, states, gain_pair[0])
    packed = product(first_norm, matrices[0])
    mixture, logsum = attend_forward(packed)
    middle = states + product(mixture, matrices[1])
    result, hidden = feed_forward(middle, gain_pair[1], matrices[2], matrices[3])
    return result, (first_norm, first_back, packed, mixture, logsum, middle, hidden)


def block_backward(upstream, gain_pair, matrices, stored, beside, begins):
    first_norm, first_back, packed, mixture, logsum, middle, hidden = stored
    middle_grad, second_gain, expand_grad, reduce_grad = feed_backward(
        upstream, middle, gain_pair[1], hidden, matrices[2], matrices[3]
    )
    if begins:
        beside.begin([expand_grad, reduce_grad])
    middle_grad = beside.advance(middle_grad)
    merge_grad = transposed_left(mixture, middle_grad)
    mixture_grad = against(middle_grad, matrices[1])
    if begins:
        mixture_grad = beside.advance(mixture_grad)
    packed_grad = attend_backward(packed, mixture, logsum, mixture_grad)
    packed_grad = beside.advance(packed_grad)
    attend_grad = transposed_left(first_norm, packed_grad)
    states_part, first_gain = first_back(against(packed_grad, matrices[0]))
    gain_grads = jnp.stack([first_gain, second_gain])
    return (
        middle_grad + states_part,
        gain_grads,
        (attend_grad, merge_grad, expand_grad, reduce_grad),
    )


def collect(weights, collective_id):
    columns, rows = lax.axis_size("dp"), lax.axis_size("fsdp")
    if all(weight.shape[0] % 16 == 0 for weight in weights):
        wholes = gather(weights, columns, rows, collective_id, GATHER_TARGET)
        return [whole.reshape(-1, whole.shape[3]) for whole in wholes]
    return [
        lax.all_gather(
            lax.all_gather(weight, "dp", axis=1, tiled=True), "fsdp", axis=0, tiled=True
        )
        for weight in weights
    ]


def spread(gradients, small, collective_id):
    columns, rows = lax.axis_size("dp"), lax.axis_size("fsdp")
    if all(gradient.shape[0] % (rows * 16) == 0 for gradient in gradients):
        wholes = [
            gradient.reshape(4, rows // 4, gradient.shape[0] // rows, gradient.shape[1])
            for gradient in gradients
        ]
        return scatter(wholes, small, columns, rows, collective_id, SCATTER_TARGET)
    parts = [
        lax.psum_scatter(
            lax.psum_scatter(gradient, "fsdp", scatter_dimension=0, tiled=True),
            "dp",
            scatter_dimension=1,
            tiled=True,
        )
        for gradient in gradients
    ]
    return parts, (None if small is None else lax.psum(small, everywhere))


def exchange_steps(columns, rows, near_first):
    def bits(size):
        return [1 << place for place in reversed(range(size.bit_length() - 1))]

    across = [("dp", bit, 0) for bit in bits(columns) if bit > 1]
    far = [("fsdp", bit, 2) for bit in bits(rows) if bit >= rows // 4]
    near = [("fsdp", bit, 3) for bit in bits(rows) if bit < rows // 4]
    return near + across + far if near_first else across + near + far


class Beside:
    def __init__(self):
        self.views, self.steps = [], []

    def begin(self, gradients):
        columns, rows = lax.axis_size("dp"), lax.axis_size("fsdp")
        for place, gradient in enumerate(gradients):
            height, width = gradient.shape
            share = width // columns
            panels = jnp.stack(
                [gradient[:, start : start + share] for start in range(0, width, share)]
            )
            self.views.append(
                panels.reshape(columns // 2, 2, 4, rows // 4, height // rows, share)
            )
            self.steps.append([("dp", 1, 1)] + exchange_steps(columns, rows, place % 2 == 0))

    def divided(self, place, upper, axis):
        view = self.views[place]
        half = view.shape[axis] // 2
        keep = lax.dynamic_slice_in_dim(view, upper * half, half, axis=axis)
        return keep, lax.dynamic_slice_in_dim(view, (1 - upper) * half, half, axis=axis)

    def advance(self, main):
        if not self.steps[0]:
            return main
        sent, kept, steps = [], [], [steps.pop(0) for steps in self.steps]
        for place, (name, bit, axis) in enumerate(steps):
            upper = jnp.bitwise_and(lax.axis_index(name) // bit, 1)
            keep, send = self.divided(place, upper, axis)
            sent.append(send)
            kept.append(keep)
        main, sent = lax.optimization_barrier((main, sent))
        self.views = [
            keep
            + lax.ppermute(
                send, name, [(place, place ^ bit) for place in range(lax.axis_size(name))]
            )
            for send, keep, (name, bit, _) in zip(sent, kept, steps)
        ]
        return main

    def finish(self):
        while self.steps[0]:
            self.advance(jnp.zeros((), jnp.float32))
        return [view.reshape(view.shape[4:]) for view in self.views]


def collect_beside(weights):
    columns, rows = lax.axis_size("dp"), lax.axis_size("fsdp")
    attend, merge, expand, reduce = weights
    padded = jnp.pad(merge, ((0, 0), (0, attend.shape[1] - merge.shape[1])))
    both = lax.all_gather(jnp.concatenate([attend, padded], axis=0), everywhere, axis=0)

    def panels(blocks):
        return blocks.reshape(columns, rows * blocks.shape[1], blocks.shape[2])

    def whole(blocks):
        return jnp.concatenate(list(panels(blocks)), axis=1)

    height = expand.shape[0]
    beside = [reduce[start : start + height] for start in range(0, reduce.shape[0], height)]
    stretches = jnp.concatenate(beside, axis=1)
    if reduce.shape[1] % 128 == 0 and stretches.shape == expand.shape and len(beside) == columns:
        rest = lax.all_gather(jnp.concatenate([expand, stretches], axis=0), everywhere, axis=0)
        expand = reduce = rest.reshape(columns, rows, 2 * height, expand.shape[1])
    else:
        expand, reduce = (
            whole(lax.all_gather(weight, everywhere, axis=0)) for weight in (expand, reduce)
        )
    return [
        whole(both[:, : attend.shape[0]]),
        whole(both[:, attend.shape[0] :, : merge.shape[1]]),
        expand,
        reduce,
    ]


def pack_small(arrays):
    flat = jnp.concatenate([array.reshape(-1) for array in arrays])
    size = -(-flat.shape[0] // 1024) * 1024
    return jnp.pad(flat, (0, size - flat.shape[0])).reshape(-1, 128)


def unpack_small(packed, arrays):
    flat, start, out = packed.reshape(-1), 0, []
    for array in arrays:
        out.append(flat[start : start + array.size].reshape(array.shape))
        start += array.size
    return out


def place(choice, values):
    high = lax.reduce_precision(values, 8, 7)
    low = values - high
    wide = choice.astype(jnp.bfloat16)
    return jnp.dot(
        wide, high.astype(jnp.bfloat16), preferred_element_type=jnp.float32
    ) + jnp.dot(wide, low.astype(jnp.bfloat16), preferred_element_type=jnp.float32)


def local(
    tokens,
    sensor_tag,
    block_dest,
    block_order,
    sensor_table,
    encoder_gains,
    encoder_attend,
    encoder_merge,
    encoder_expand,
    encoder_reduce,
    bridge,
    mask_token,
    decoder_gains,
    decoder_attend,
    decoder_merge,
    decoder_expand,
    decoder_reduce,
    cotangent,
):
    groups = lax.axis_size("fsdp")
    visible = tokens.shape[0]
    capacity = 2 * visible // groups
    length = block_order.shape[1]
    breadth = mask_token.shape[0]
    destination = block_dest[:, 0]
    chooser = (destination[:, None] == jnp.arange(groups, dtype=jnp.int32)[None, :]).astype(
        jnp.int32
    )
    tallies = jnp.zeros((16, 128), jnp.float32)
    tallies = tallies.at[0, :groups].set(jnp.sum(chooser, axis=0).astype(jnp.float32))
    expand, attend, reduce, merge, to_decoder, all_tallies = collect(
        [encoder_expand, encoder_attend, encoder_reduce, encoder_merge, bridge, tallies], 1
    )
    encoder_set = [attend, merge, expand, reduce, to_decoder]
    mine = all_tallies.reshape(groups, 16, -1, 128)[:, 0]
    mine = lax.dynamic_index_in_dim(mine, lax.axis_index("dp"), axis=1, keepdims=False)
    arrived_tallies = lax.dynamic_slice_in_dim(mine, lax.axis_index("fsdp"), 1, axis=1)
    decoder_set = collect_beside(
        lax.optimization_barrier(
            (decoder_attend, decoder_merge, decoder_expand, decoder_reduce, encoder_set[4])
        )[:4]
    )
    tag_row = (
        sensor_tag[:, None] == jnp.arange(sensor_table.shape[0], dtype=jnp.int32)[None, :]
    ).astype(jnp.float32)
    initial = tokens + product(tag_row, sensor_table)
    encoded, encoder_kept = block_forward(initial, encoder_gains, encoder_set)
    projected = product(encoded, encoder_set[4])
    ranking = jnp.sum((jnp.cumsum(chooser, axis=0) - chooser) * chooser, axis=1)
    slot_index = destination * capacity + ranking
    select = (
        slot_index[None, :] == jnp.arange(groups * capacity, dtype=jnp.int32)[:, None]
    ).astype(jnp.float32)
    outgoing = place(select, projected).reshape(groups, capacity, breadth)
    arrived = lax.all_to_all(outgoing, "fsdp", split_axis=0, concat_axis=0, tiled=True)
    present = (jnp.arange(capacity, dtype=jnp.float32)[None, :] < arrived_tallies).reshape(-1)
    ordering = block_order[0, : groups * capacity]
    placing = (
        (ordering[None, :] == jnp.arange(length, dtype=jnp.int32)[:, None]) & present[None, :]
    ).astype(jnp.float32)
    covered = jnp.sum(placing, axis=1, keepdims=True)
    filled = (
        place(placing, arrived.reshape(groups * capacity, breadth))
        + (1.0 - covered) * mask_token
        + position_table(length, breadth)
    )
    decoded, decoder_kept = block_forward(filled, decoder_gains, decoder_set)
    beside = Beside()
    filled_grad, decoder_gain_grad, decoder_grads = block_backward(
        cotangent, decoder_gains, decoder_set, decoder_kept, beside, True
    )
    mask_grad = jnp.sum((1.0 - covered) * filled_grad, axis=0)
    arrived_grad = place(placing.T, filled_grad).reshape(groups, capacity, breadth)
    returned = lax.all_to_all(arrived_grad, "fsdp", split_axis=0, concat_axis=0, tiled=True)
    projected_grad = place(select.T, returned.reshape(groups * capacity, breadth))
    bridge_grad = transposed_left(encoded, projected_grad)
    encoded_grad = against(projected_grad, encoder_set[4])
    tokens_grad, encoder_gain_grad, encoder_grads = block_backward(
        encoded_grad, encoder_gains, encoder_set, encoder_kept, beside, False
    )
    table_grad = transposed_left(tag_row, jnp.sum(tokens_grad, axis=0, keepdims=True))
    small = (table_grad, encoder_gain_grad, mask_grad, decoder_gain_grad)
    packed_small = pack_small(small)
    spreads, total = spread(
        [
            decoder_grads[1],
            encoder_grads[1],
            decoder_grads[0],
            bridge_grad,
            encoder_grads[0],
            encoder_grads[2],
            encoder_grads[3],
        ],
        packed_small,
        3,
    )
    encoder_spread = [spreads[4], spreads[1], spreads[5], spreads[6], spreads[3]]
    expand_sum, reduce_sum = beside.finish()
    decoder_spread = [spreads[2], spreads[0], expand_sum, reduce_sum]
    summed = unpack_small(total, small)
    return (
        decoded,
        tokens_grad,
        summed[0],
        summed[1],
        encoder_spread[0],
        encoder_spread[1],
        encoder_spread[2],
        encoder_spread[3],
        encoder_spread[4],
        summed[2],
        summed[3],
        decoder_spread[0],
        decoder_spread[1],
        decoder_spread[2],
        decoder_spread[3],
    )


def solution(mesh):
    in_specs = (
        P(("dp", "fsdp"), None),
        P(("dp", "fsdp")),
        P(("dp", "fsdp"), None),
        P(("dp", "fsdp"), None),
        P(),
        P(),
        P("fsdp", "dp"),
        P("fsdp", "dp"),
        P("fsdp", "dp"),
        P("fsdp", "dp"),
        P("fsdp", "dp"),
        P(),
        P(),
        P("fsdp", "dp"),
        P("fsdp", "dp"),
        P("fsdp", "dp"),
        P("fsdp", "dp"),
        P(("dp", "fsdp"), None),
    )
    out_specs = (
        P(("dp", "fsdp"), None),
        P(("dp", "fsdp"), None),
        P(),
        P(),
        P("fsdp", "dp"),
        P("fsdp", "dp"),
        P("fsdp", "dp"),
        P("fsdp", "dp"),
        P("fsdp", "dp"),
        P(),
        P(),
        P("fsdp", "dp"),
        P("fsdp", "dp"),
        P("fsdp", "dp"),
        P("fsdp", "dp"),
    )
    return jax.shard_map(local, mesh=mesh, in_specs=in_specs, out_specs=out_specs, check_vma=False)
```

```python
from functools import partial
import math

import jax
import jax.numpy as jnp
from jax import lax
from jax.experimental import pallas as pl
from jax.experimental.pallas import tpu as pltpu
from jax.sharding import PartitionSpec as P

MESH = pl.DeviceIdType.MESH
VMEM = pltpu.VMEM
NARROW = jnp.bfloat16
LONG = (("b", "a", "x"), ("x", "a", "b"))
SHORT = (("a", "x", "b"), ("a", "b", "x"))
GATHER_TURNS = (SHORT, LONG, LONG)
SCATTER_TURNS = (LONG, LONG, SHORT)
AHEAD = 2
SLACK = 2


class Grid:
    def __init__(self, dp, fsdp):
        self.size = {"x": dp // 2, "a": 4, "b": fsdp // 4}
        column, row = lax.axis_index("dp"), lax.axis_index("fsdp")
        self.core = lax.rem(column, 2)
        self.at = {
            "x": lax.div(column, 2),
            "a": lax.div(row, self.size["b"]),
            "b": lax.rem(row, self.size["b"]),
        }

    def device(self, core=None, **moved):
        at = {**self.at, **moved}
        core = self.core if core is None else core
        return (at["x"] * 2 + core, at["a"] * self.size["b"] + at["b"])

    def greet(self, reach):
        barrier = pltpu.get_barrier_semaphore()
        pl.semaphore_signal(
            barrier, inc=1, device_id=self.device(1 - self.core), device_id_type=MESH
        )
        count = 1
        for axis, size in self.size.items():
            here = self.at[axis]
            for move in range(-min(reach, size - 1), min(reach, size - 1) + 1):
                if move:
                    exists = together(here + move >= 0, here + move < size)
                    count = count + jnp.where(exists, 1, 0)

                    @pl.when(exists)
                    def _(axis=axis, here=here, move=move):
                        pl.semaphore_signal(
                            barrier,
                            inc=1,
                            device_id=self.device(**{axis: here + move}),
                            device_id_type=MESH,
                        )

        pl.semaphore_wait(barrier, count)


def plan_rounds(shapes, target, turns):
    plan, turn = [], 0
    for rows, columns in shapes:
        units = rows // 16
        pairs = max(1, min(units // 2, round(units * 8 * columns * 2 / target)))
        parts, start = [], 0
        for pair in range(pairs):
            orders = turns[turn % len(turns)]
            for place, order in enumerate(orders):
                take = -(-(units - start) // (2 * (pairs - pair) - place))
                if take:
                    parts.append((order, start * 8, take * 8, turn))
                start += take
            turn += 1
        plan.append(parts)
    return plan


def together(*conditions):
    joined = conditions[0]
    for condition in conditions[1:]:
        joined = jnp.logical_and(joined, condition)
    return joined


class Traffic:
    def __init__(self, grid, send, receive):
        self.grid, self.send, self.receive = grid, send, receive
        self.count, self.open = 0, []

    def copy(self, source, target, device, starts, arrives):
        place = self.count
        self.count += 1

        def made():
            return pltpu.make_async_remote_copy(
                src_ref=source,
                dst_ref=target,
                send_sem=self.send.at[place],
                recv_sem=self.receive.at[place],
                device_id=device,
                device_id_type=MESH,
            )

        if starts is None:
            made().start()
        else:

            @pl.when(starts)
            def _():
                made().start()

        self.open.append((made, starts))
        return (made, arrives)

    def arrive(self, handle):
        made, arrives = handle
        if arrives is None:
            made().wait_recv()
        else:

            @pl.when(arrives)
            def _():
                made().wait_recv()

    def take(self, handle):
        handle[0]().wait_recv()

    def drain(self, handle):
        handle[0]().wait_send()
        self.open = [entry for entry in self.open if entry[0] is not handle[0]]

    def close(self):
        for made, starts in self.open:
            if starts is None:
                made().wait_send()
            else:

                @pl.when(starts)
                def _():
                    made().wait_send()


def block_of(full, chosen, offset, rows, width):
    view = []
    for axis in ("a", "b"):
        place = chosen[axis]
        view.append(slice(None) if place is None else pl.ds(place, 1))
    columns = (
        slice(None)
        if chosen["x"] is None
        else pl.ds(pl.multiple_of(chosen["x"] * width, 128), width)
    )
    return full.at[(*view, pl.ds(pl.multiple_of(offset, 8), rows), columns)]


def pause():
    for _ in range(SLACK):
        yield


def gather_line(traffic, axis, chosen, view, exists, arrived):
    grid = traffic.grid
    here, size = grid.at[axis], grid.size[axis]

    def both(condition):
        return condition if exists is None else together(exists, condition)

    arrived({**chosen, axis: here}, exists)
    for step in range(1, size):
        ahead, behind = {**chosen, axis: here - (step - 1)}, {**chosen, axis: here + (step - 1)}
        rightward = traffic.copy(
            view(ahead),
            view(ahead),
            grid.device(**{axis: here + 1}),
            both(together(here + 1 < size, here - (step - 1) >= 0)),
            both(here - step >= 0),
        )
        leftward = traffic.copy(
            view(behind),
            view(behind),
            grid.device(**{axis: here - 1}),
            both(together(here - 1 >= 0, here + (step - 1) < size)),
            both(here + step < size),
        )
        yield from pause()
        traffic.arrive(rightward)
        arrived({**chosen, axis: here - step}, both(here - step >= 0))
        traffic.arrive(leftward)
        arrived({**chosen, axis: here + step}, both(here + step < size))


def gather_part(traffic, order, view, spawn, share):
    first, second, third = order
    grid = traffic.grid
    own = dict(grid.at)

    def last(chosen, exists):
        def finish():
            yield from gather_line(traffic, third, chosen, view, exists, lambda *_: None)
            share(view({**chosen, third: None}), exists)

        spawn(finish())

    def begin():
        if grid.size[first] == 2:
            yield from gather_line(traffic, first, own, view, None, lambda *_: None)
            yield from gather_line(traffic, second, {**own, first: None}, view, None, last)
        else:

            def middle(chosen, exists):
                def go():
                    yield from gather_line(traffic, second, chosen, view, exists, lambda *_: None)
                    last({**chosen, second: None}, exists)

                spawn(go())

            yield from gather_line(traffic, first, own, view, None, middle)

    spawn(begin())


def run_rounds(starts):
    active = []

    def spawn(generator):
        try:
            next(generator)
            active.append(generator)
        except StopIteration:
            pass

    for start in starts:
        for begin in start:
            begin(spawn)
        advance_all(active)
    while active:
        advance_all(active)


def advance_all(active):
    for generator in list(active):
        try:
            next(generator)
        except StopIteration:
            active.remove(generator)


def gather_kernel(dp, fsdp, shapes, plan, *refs):
    number = len(shapes)
    shards, wholes = refs[:number], refs[number : 2 * number]
    raws, blocks = refs[2 * number : 3 * number], refs[3 * number : 4 * number]
    send, receive, pair_send, pair_receive, local = refs[4 * number :]
    grid = Grid(dp, fsdp)
    traffic = Traffic(grid, send, receive)
    pair = Traffic(grid, pair_send, pair_receive)
    core, other = grid.core, 1 - grid.core
    sibling = grid.device(other)
    grid.greet(1)
    handles = []
    for index, (rows, columns) in enumerate(shapes):
        half = rows // 2
        theirs = shards[index].at[pl.ds(pl.multiple_of(other * half, 8), half)]
        handles.append(pair.copy(theirs, raws[index], sibling, None, None))
    stores = []
    for index, (rows, columns) in enumerate(shapes):
        half = rows // 2
        pair.arrive(handles[index])
        mine = shards[index][pl.ds(pl.multiple_of(core * half, 8), half), :]
        came = raws[index][...]
        blocks[index][0, 0] = jnp.where(
            core == 0,
            jnp.concatenate([mine, came], axis=1),
            jnp.concatenate([came, mine], axis=1),
        )
        store = pltpu.make_async_copy(
            blocks[index],
            block_of(wholes[index], grid.at, core * half, half, 2 * columns),
            local.at[index],
        )
        store.start()
        stores.append(store)
    for store in stores:
        store.wait()
    pending = []

    def share(piece, exists):
        pending.append(pair.copy(piece, piece, sibling, exists, exists))

    starts = [[] for _ in range(1 + max(part[3] for parts in plan for part in parts))]
    for index, (rows, columns) in enumerate(shapes):
        half = rows // 2
        for order, offset, count, turn in plan[index]:

            def view(chosen, index=index, offset=offset, count=count, half=half, columns=columns):
                return block_of(wholes[index], chosen, core * half + offset, count, 2 * columns)

            starts[turn].append(
                lambda spawn, order=order, view=view: gather_part(
                    traffic, order, view, spawn, share
                )
            )
    run_rounds(starts)
    for handle in pending:
        pair.arrive(handle)
    traffic.close()
    pair.close()


def gather(weights, dp, fsdp, collective_id, target):
    shapes = [weight.shape for weight in weights]
    a, b = 4, fsdp // 4
    plan = plan_rounds(shapes, target, GATHER_TURNS)
    total = sum(len(parts) for parts in plan)
    out = [jax.ShapeDtypeStruct((a, b, r, dp * c), jnp.float32) for r, c in shapes]
    vmem = pl.BlockSpec(memory_space=VMEM)
    return pl.pallas_call(
        partial(gather_kernel, dp, fsdp, shapes, plan),
        out_shape=out,
        in_specs=[vmem] * len(shapes),
        out_specs=[pl.BlockSpec(memory_space=pl.ANY)] * len(shapes),
        scratch_shapes=[VMEM((r // 2, c), jnp.float32) for r, c in shapes]
        + [VMEM((1, 1, r // 2, 2 * c), jnp.float32) for r, c in shapes]
        + [
            pltpu.SemaphoreType.DMA((34 * total,)),
            pltpu.SemaphoreType.DMA((34 * total,)),
            pltpu.SemaphoreType.DMA((8 * total + len(shapes),)),
            pltpu.SemaphoreType.DMA((8 * total + len(shapes),)),
            pltpu.SemaphoreType.DMA((len(shapes),)),
        ],
        compiler_params=pltpu.CompilerParams(
            collective_id=collective_id, has_side_effects=True, vmem_limit_bytes=32 << 20
        ),
        name="gather_weights",
    )(*weights)


def landing_shapes(size, order, rows, width):
    chosen, shapes = {"x": size["x"], "a": size["a"], "b": size["b"]}, []
    for axis in reversed(order):
        chosen[axis] = 1
        slots = 1 if size[axis] == 2 else 2 * (size[axis] - 1)
        shapes.append((slots, chosen["a"], chosen["b"], rows, chosen["x"] * width))
    return shapes


def sum_line(traffic, axis, chosen, view, landing):
    grid = traffic.grid
    here, size = grid.at[axis], grid.size[axis]
    ends = size - 1

    def slot(rightward, place):
        if size == 2:
            return 0
        return place - 1 if rightward else ends + place

    def blocks(place):
        return view({**chosen, axis: place})

    def add(rightward, place):
        target = blocks(place)
        target[...] += landing[slot(rightward, place)]

    def send(rightward, place, starts, arrives):
        return traffic.copy(
            blocks(place),
            landing.at[slot(rightward, place)],
            grid.device(**{axis: here + (1 if rightward else -1)}),
            starts,
            arrives,
        )

    first = {}
    for place in range(ends, 0, -1):
        first[True, place] = send(
            True, place, here == 0, here == 1
        )
    for place in range(ends):
        first[False, place] = send(False, place, here == ends, here == ends - 1)
    later = {}
    for step in range(ends - 1):
        yield from pause()
        for come in range(1, ends):
            place = ends - step + come - 1
            if come < place <= ends:
                @pl.when(here == come)
                def _(come=come, place=place):
                    traffic.take(first[True, place] if come == 1 else later[True, come - 1, place])
                    add(True, place)

                later[True, come, place] = send(True, place, here == come, here == come + 1)
            come, place = ends - come, ends - place
            if come > place >= 0:

                @pl.when(here == come)
                def _(come=come, place=place):
                    traffic.take(
                        first[False, place] if come == ends - 1 else later[False, come + 1, place]
                    )
                    add(False, place)

                later[False, come, place] = send(False, place, here == come, here == come - 1)
    yield from pause()
    for place in range(size):

        @pl.when(here == place)
        def _(place=place):
            if place > 0:
                traffic.take(first[True, place] if place == 1 else later[True, place - 1, place])
                add(True, place)
            if place < ends:
                traffic.take(
                    first[False, place] if place == ends - 1 else later[False, place + 1, place]
                )
                add(False, place)


def sum_part(traffic, order, view, landings):
    chosen = {"x": None, "a": None, "b": None}
    for axis, landing in zip(reversed(order), landings):
        yield from sum_line(traffic, axis, chosen, view, landing)
        chosen[axis] = traffic.grid.at[axis]


def total_everywhere(traffic, pair, value, pair_landing, landings):
    grid = traffic.grid
    came = pair.copy(value, pair_landing, grid.device(1 - grid.core), None, None)
    yield
    pair.arrive(came)
    pair.drain(came)
    value[...] += pair_landing[...]
    for axis, landing in zip(("x", "b", "a"), landings):
        here, size = grid.at[axis], grid.size[axis]
        handles = []
        for move in range(1, size):
            target = lax.rem(here + move, size)
            source = lax.rem(here + size - move, size)
            handles.append(
                (
                    traffic.copy(
                        value, landing.at[here], grid.device(**{axis: target}), None, None
                    ),
                    source,
                )
            )
        landing[here] = value[...]
        yield
        for handle, _ in handles:
            traffic.arrive(handle)
            traffic.drain(handle)
        total = landing[0]
        for place in range(1, size):
            total = total + landing[place]
        value[...] = total


def scatter_kernel(dp, fsdp, shapes, pieces, has_small, *refs):
    number = len(shapes)
    refs = list(refs)

    def take(count):
        taken = refs[:count]
        del refs[:count]
        return taken

    wholes, small = take(number), (take(1)[0] if has_small else None)
    outs, small_out = take(number), (take(1)[0] if has_small else None)
    sums, others, finals = take(number), take(number), take(number)
    landings = [[take(3) for _ in parts] for parts in pieces]
    if has_small:
        small_pair, *small_landings = take(4)
    send, receive, pair_send, pair_receive, local = refs
    grid = Grid(dp, fsdp)
    traffic = Traffic(grid, send, receive)
    pair = Traffic(grid, pair_send, pair_receive)
    core, other = grid.core, 1 - grid.core
    sibling = grid.device(other)
    grid.greet(max(grid.size.values()) if small is not None else 1)
    starts = [[] for _ in range(1 + max(part[3] for parts in pieces for part in parts))]
    if has_small:
        small_out[...] = small[...]
        starts[0].append(
            lambda spawn: spawn(
                total_everywhere(traffic, pair, small_out, small_pair, small_landings)
            )
        )
    place, runs = 0, []
    for index, (rows, columns) in enumerate(shapes):
        half = rows // 2
        for part, (order, offset, count, turn) in enumerate(pieces[index]):
            window = (slice(None), slice(None), slice(offset, offset + count))
            fetched = []

            def fetch(index=index, half=half, offset=offset, count=count, window=window,
                      fetched=fetched, place=place):
                def stretch(at):
                    start = pl.multiple_of(at * half + offset, 8)
                    return wholes[index].at[:, :, pl.ds(start, count), :]

                came = pair.copy(stretch(other), others[index].at[window], sibling, None, None)
                load = pltpu.make_async_copy(
                    stretch(core), sums[index].at[window], local.at[place]
                )
                load.start()
                fetched.extend((came, load))

            ahead = max(0, turn - AHEAD)
            starts[ahead].append(lambda spawn, fetch=fetch: fetch())
            place += 1

            def run(index=index, order=order, offset=offset, count=count, window=window,
                    fetched=fetched, columns=columns, part=part):
                fetched[1].wait()
                pair.arrive(fetched[0])
                sums[index][window] += others[index][window]

                def view(chosen):
                    return block_of(sums[index], chosen, offset, count, 2 * columns)

                yield from sum_part(traffic, order, view, landings[index][part])

            runs.append((turn, lambda spawn, run=run: spawn(run())))
    for turn, run in runs:
        starts[turn].append(run)
    run_rounds(starts)
    handles = []
    for index, (rows, columns) in enumerate(shapes):
        half = rows // 2
        block = block_of(sums[index], grid.at, 0, half, 2 * columns)
        handles.append(pair.copy(block, finals[index], sibling, None, None))
    for index, (rows, columns) in enumerate(shapes):
        half = rows // 2
        block = block_of(sums[index], grid.at, 0, half, 2 * columns)[0, 0]
        pair.arrive(handles[index])
        came = finals[index][0, 0]
        for value, at in ((block, core), (came, other)):
            outs[index][pl.ds(pl.multiple_of(at * half, 8), half), :] = jnp.where(
                core == 0, value[:, :columns], value[:, columns:]
            )
    traffic.close()
    pair.close()


def scatter(wholes, small, dp, fsdp, collective_id, target):
    size = {"x": dp // 2, "a": 4, "b": fsdp // 4}
    shapes = [(whole.shape[2], whole.shape[3] // dp) for whole in wholes]
    pieces = plan_rounds(shapes, target, SCATTER_TURNS)
    number = len(shapes)
    total = sum(len(parts) for parts in pieces)
    scratch = []
    for _ in range(2):
        scratch += [VMEM((size["a"], size["b"], r // 2, dp * c), jnp.float32) for r, c in shapes]
    scratch += [VMEM((1, 1, r // 2, 2 * c), jnp.float32) for r, c in shapes]
    for (rows, columns), parts in zip(shapes, pieces):
        for order, _, count, _ in parts:
            for shape in landing_shapes(size, order, count, 2 * columns):
                scratch.append(VMEM(shape, jnp.float32))
    smalls = [] if small is None else [small]
    for array in smalls:
        scratch.append(VMEM(array.shape, jnp.float32))
        for axis in ("x", "b", "a"):
            scratch.append(VMEM((size[axis], *array.shape), jnp.float32))
    hops = 2 * sum(size.values()) + sum((length - 1) * length for length in size.values())
    scratch += [
        pltpu.SemaphoreType.DMA((total * hops + 40,)),
        pltpu.SemaphoreType.DMA((total * hops + 40,)),
        pltpu.SemaphoreType.DMA((total + number + 1,)),
        pltpu.SemaphoreType.DMA((total + number + 1,)),
        pltpu.SemaphoreType.DMA((total,)),
    ]
    vmem = pl.BlockSpec(memory_space=VMEM)
    results = pl.pallas_call(
        partial(scatter_kernel, dp, fsdp, shapes, pieces, small is not None),
        out_shape=[jax.ShapeDtypeStruct(shape, jnp.float32) for shape in shapes]
        + [jax.ShapeDtypeStruct(array.shape, jnp.float32) for array in smalls],
        in_specs=[pl.BlockSpec(memory_space=pl.ANY)] * number + [vmem] * len(smalls),
        out_specs=[vmem] * (number + len(smalls)),
        scratch_shapes=scratch,
        compiler_params=pltpu.CompilerParams(
            collective_id=collective_id, has_side_effects=True, vmem_limit_bytes=60 << 20
        ),
        name="scatter_sums",
    )(*wholes, *smalls)
    return results[:number], (results[number] if smalls else None)


HEAD = 64


def split(values):
    high = values.astype(NARROW)
    return high, (values - high.astype(jnp.float32)).astype(NARROW)


def tripled(values, leading):
    high, low = split(values)
    return jnp.concatenate([high, high, low] if leading else [high, low, high], axis=1)


def dot(left, right, contract=(1, 0)):
    return lax.dot_general(
        left,
        right,
        (((contract[0],), (contract[1],)), ((), ())),
        preferred_element_type=jnp.float32,
    )


def attend_kernel(chunk, q_ref, k_ref, v_ref, out_ref, lse_ref, keys, values):
    rows = q_ref.shape[0]

    @pl.when(pl.program_id(1) == 0)
    def _():
        for head in range(2):
            part = slice(head * HEAD, (head + 1) * HEAD)
            keys[head] = tripled(k_ref[:, part], False)
            values[head] = jnp.concatenate(split(v_ref[:, part]), axis=1)

    for start in range(0, rows, chunk):
        at = slice(start, start + chunk)
        outs = []
        for head in range(2):
            part = slice(head * HEAD, (head + 1) * HEAD)
            queries = tripled(q_ref[at, part] * (1.0 / math.sqrt(HEAD)), True)
            scores = dot(queries, keys[head], (1, 1))
            top = jnp.max(scores, axis=1, keepdims=True)
            weights = jnp.exp(scores - top)
            total = jnp.sum(weights, axis=1, keepdims=True)
            first, second = split(weights)
            both = dot(first, values[head])
            mixed = both[:, :HEAD] + both[:, HEAD:] + dot(second, values[head][:, :HEAD])
            outs.append(mixed * (1.0 / total))
            lse_ref[at, head : head + 1] = top + jnp.log(total)
        out_ref[at, :] = jnp.concatenate(outs, axis=1)


def attend_forward(packed, block=768, chunk=768):
    rows, breadth = packed.shape[0], packed.shape[1] // 3
    pairs = breadth // 128
    block = min(block, rows)
    chunk = min(chunk, block)
    return pl.pallas_call(
        partial(attend_kernel, chunk),
        grid=(pairs, rows // block),
        in_specs=[
            pl.BlockSpec((block, 128), lambda h, i: (i, h)),
            pl.BlockSpec((rows, 128), lambda h, i: (0, pairs + h)),
            pl.BlockSpec((rows, 128), lambda h, i: (0, 2 * pairs + h)),
        ],
        out_specs=[
            pl.BlockSpec((block, 128), lambda h, i: (i, h)),
            pl.BlockSpec((None, block, 128), lambda h, i: (h, i, 0)),
        ],
        out_shape=[
            jax.ShapeDtypeStruct((rows, breadth), jnp.float32),
            jax.ShapeDtypeStruct((pairs, rows, 128), jnp.float32),
        ],
        scratch_shapes=[
            VMEM((2, rows, 3 * HEAD), NARROW),
            VMEM((2, rows, 2 * HEAD), NARROW),
        ],
        compiler_params=pltpu.CompilerParams(vmem_limit_bytes=48 << 20),
        cost_estimate=pl.CostEstimate(
            flops=12 * rows * rows * breadth, bytes_accessed=20 * rows * breadth, transcendentals=0
        ),
        name="attend_forward",
    )(packed, packed, packed)


def attend_back_kernel(
    chunk, q_ref, k_ref, v_ref, o_ref, g_ref, lse_ref, dq_ref, dk_ref, dv_ref,
    queries, gradients, wide_q, wide_g, row_lse, row_delta, dq,
):
    rows, block = q_ref.shape[0], k_ref.shape[0]
    scale = 1.0 / math.sqrt(HEAD)

    @pl.when(pl.program_id(1) == 0)
    def _():
        for head in range(2):
            part = slice(head * HEAD, (head + 1) * HEAD)
            q = q_ref[:, part] * scale
            g = g_ref[:, part]
            queries[head] = tripled(q, True).T
            gradients[head] = tripled(g, True).T
            wide_q[head] = jnp.concatenate(split(q), axis=1)
            wide_g[head] = jnp.concatenate(split(g), axis=1)
            delta = jnp.sum(g * o_ref[:, part], axis=1, keepdims=True)
            row_delta[head] = jnp.broadcast_to(delta, (rows, 128)).T[:8]
            row_lse[head] = jnp.broadcast_to(lse_ref[:, head : head + 1], (rows, 128)).T[:8]
        dq[...] = jnp.zeros_like(dq)

    for start in range(0, block, chunk):
        at = slice(start, start + chunk)
        dks, dvs = [], []
        for head in range(2):
            part = slice(head * HEAD, (head + 1) * HEAD)
            k = k_ref[at, part]
            scores = dot(tripled(k, False), queries[head])
            weights = jnp.exp(scores - row_lse[head, 0:1])
            slopes = dot(tripled(v_ref[at, part], False), gradients[head])
            slopes = weights * (slopes - row_delta[head, 0:1])
            first, second = split(weights)
            both = dot(first, wide_g[head])
            dvs.append(both[:, :HEAD] + both[:, HEAD:] + dot(second, wide_g[head][:, :HEAD]))
            first, second = split(slopes)
            both = dot(first, wide_q[head])
            dks.append(both[:, :HEAD] + both[:, HEAD:] + dot(second, wide_q[head][:, :HEAD]))
            kt = jnp.concatenate(split(k * scale), axis=1).T
            both = dot(kt, first)
            dq[head] = dq[head] + both[:HEAD] + both[HEAD:] + dot(kt[:HEAD], second)
        dk_ref[at, :] = jnp.concatenate(dks, axis=1)
        dv_ref[at, :] = jnp.concatenate(dvs, axis=1)

    @pl.when(pl.program_id(1) == pl.num_programs(1) - 1)
    def _():
        for head in range(2):
            dq_ref[:, head * HEAD : (head + 1) * HEAD] = dq[head].T


def attend_backward(packed, mixture, lse, upstream, block=512, chunk=256):
    rows, breadth = mixture.shape
    pairs = breadth // 128
    if rows < block:
        block = chunk = rows
    whole = lambda h, i: (0, h)
    stretch = lambda h, i: (i, h)
    parts = pl.pallas_call(
        partial(attend_back_kernel, chunk),
        grid=(pairs, rows // block),
        in_specs=[
            pl.BlockSpec((rows, 128), whole),
            pl.BlockSpec((block, 128), lambda h, i: (i, pairs + h)),
            pl.BlockSpec((block, 128), lambda h, i: (i, 2 * pairs + h)),
            pl.BlockSpec((rows, 128), whole),
            pl.BlockSpec((rows, 128), whole),
            pl.BlockSpec((None, rows, 128), lambda h, i: (h, 0, 0)),
        ],
        out_specs=[
            pl.BlockSpec((rows, 128), whole),
            pl.BlockSpec((block, 128), stretch),
            pl.BlockSpec((block, 128), stretch),
        ],
        out_shape=[jax.ShapeDtypeStruct((rows, breadth), jnp.float32)] * 3,
        scratch_shapes=[
            VMEM((2, 3 * HEAD, rows), NARROW),
            VMEM((2, 3 * HEAD, rows), NARROW),
            VMEM((2, rows, 2 * HEAD), NARROW),
            VMEM((2, rows, 2 * HEAD), NARROW),
            VMEM((2, 8, rows), jnp.float32),
            VMEM((2, 8, rows), jnp.float32),
            VMEM((2, HEAD, rows), jnp.float32),
        ],
        compiler_params=pltpu.CompilerParams(vmem_limit_bytes=48 << 20),
        cost_estimate=pl.CostEstimate(
            flops=30 * rows * rows * breadth, bytes_accessed=32 * rows * breadth, transcendentals=0
        ),
        name="attend_backward",
    )(packed, packed, packed, mixture, upstream, lse)
    return jnp.concatenate(parts, axis=1)


def stacked(values):
    high, low = split(values)
    return jnp.concatenate([high, low, high], axis=0)


def normal_parts(values):
    center = values - jnp.mean(values, axis=1, keepdims=True)
    inverse = lax.rsqrt(jnp.mean(center * center, axis=1, keepdims=True) + 1e-06)
    return center * inverse, inverse


def pieces_of(rows, size, body):
    for start in range(0, rows, size):
        body(slice(start, min(start + size, rows)))


def normal_share(values):
    return 0.5 + 0.5 * lax.erf(values * math.sqrt(0.5))


def weight_specs(expand, reduce, block):
    if expand.ndim == 2:
        return [
            pl.BlockSpec((expand.shape[0], block), lambda j: (0, j)),
            pl.BlockSpec((block, reduce.shape[1]), lambda j: (j, 0)),
        ]
    columns, rows, height, width = expand.shape
    each, deep = width // block, block // (columns * height // 2)
    return [
        pl.BlockSpec(
            (None, rows, height // 2, block), lambda j: (lax.div(j, each), 0, 0, lax.rem(j, each))
        ),
        pl.BlockSpec((columns, deep, height // 2, width), lambda j: (0, j, 1, 0)),
    ]


def hidden_units(expand):
    return expand.shape[1] if expand.ndim == 2 else expand.shape[0] * expand.shape[3]


def expand_of(ref):
    if len(ref.shape) == 2:
        return ref[...]
    return ref[...].reshape(ref.shape[0] * ref.shape[1], ref.shape[2])


def reduce_of(ref):
    if len(ref.shape) == 2:
        return ref[...]
    columns, deep, _, width = ref.shape
    share = width // columns
    return jnp.concatenate(
        [
            jnp.concatenate(
                [ref[column, row, :, part * share : (part + 1) * share] for column in range(columns)],
                axis=1,
            )
            for row in range(deep)
            for part in range(columns)
        ],
        axis=0,
    )


def forward_kernel(piece, m_ref, gain_ref, expand_ref, reduce_ref, out_ref, hidden_ref, wide):
    rows = m_ref.shape[0]

    @pl.when(pl.program_id(0) == 0)
    def _():
        def begin(at):
            wide[at, :] = tripled(normal_parts(m_ref[at, :])[0] * gain_ref[...], True)
            out_ref[at, :] = m_ref[at, :]

        pieces_of(rows, piece, begin)

    expand, reduce = stacked(expand_of(expand_ref)), stacked(reduce_of(reduce_ref))

    def go(at):
        hidden = dot(wide[at, :], expand)
        hidden_ref[at, :] = hidden
        active = hidden * normal_share(hidden)
        out_ref[at, :] = out_ref[at, :] + dot(tripled(active, True), reduce)

    pieces_of(rows, piece, go)


def feed_forward(middle, gain, expand, reduce, block=512, piece=512):
    rows, width = middle.shape
    hidden = hidden_units(expand)
    whole = lambda j: (0, 0)
    return pl.pallas_call(
        partial(forward_kernel, min(piece, rows)),
        grid=(hidden // block,),
        in_specs=[
            pl.BlockSpec((rows, width), whole),
            pl.BlockSpec((1, width), whole),
            *weight_specs(expand, reduce, block),
        ],
        out_specs=[
            pl.BlockSpec((rows, width), whole),
            pl.BlockSpec((rows, block), lambda j: (0, j)),
        ],
        out_shape=[
            jax.ShapeDtypeStruct((rows, width), jnp.float32),
            jax.ShapeDtypeStruct((rows, hidden), jnp.float32),
        ],
        scratch_shapes=[VMEM((rows, 3 * width), NARROW)],
        compiler_params=pltpu.CompilerParams(vmem_limit_bytes=56 << 20),
        cost_estimate=pl.CostEstimate(
            flops=12 * rows * width * hidden, bytes_accessed=4 * rows * hidden, transcendentals=0
        ),
        name="feed_forward",
    )(middle, gain.reshape(1, width), expand, reduce)


def backward_kernel(
    piece, g_ref, m_ref, gain_ref, hidden_ref, expand_ref, reduce_ref,
    dm_ref, dgain_ref, dexpand_ref, dreduce_ref,
    wide, g_high, g_low, b_high, b_low, r_high, r_low, u_high, u_low, back,
):
    rows = g_ref.shape[0]

    @pl.when(pl.program_id(0) == 0)
    def _():
        def begin(at):
            g = g_ref[at, :]
            wide[at, :] = tripled(g, True)
            g_high[:, at], g_low[:, at] = split(g.T)
            normal = normal_parts(m_ref[at, :])[0] * gain_ref[...]
            b_high[:, at], b_low[:, at] = split(normal.T)
            back[at, :] = jnp.zeros_like(g)

        pieces_of(rows, piece, begin)

    expand = tripled(expand_of(expand_ref), False)
    reduce = tripled(reduce_of(reduce_ref), False)

    def go(at):
        hidden = hidden_ref[at, :]
        share = normal_share(hidden)
        r_high[at, :], r_low[at, :] = split(hidden * share)
        bell = jnp.exp(hidden * hidden * -0.5) * (1.0 / math.sqrt(2.0 * math.pi))
        slope = share + hidden * bell
        hidden_grad = slope * dot(wide[at, :], reduce, (1, 1))
        u_high[at, :], u_low[at, :] = split(hidden_grad)
        back[at, :] = back[at, :] + dot(tripled(hidden_grad, True), expand, (1, 1))

    pieces_of(rows, piece, go)
    grad = dot(g_high[...], r_high[...]) + dot(g_high[...], r_low[...])
    dreduce_ref[...] = (grad + dot(g_low[...], r_high[...])).T
    grad = dot(b_high[...], u_high[...]) + dot(b_high[...], u_low[...])
    dexpand_ref[...] = grad + dot(b_low[...], u_high[...])

    @pl.when(pl.program_id(0) == pl.num_programs(0) - 1)
    def _():
        dgain_ref[...] = jnp.zeros_like(dgain_ref)

        def finish(at):
            normal, inverse = normal_parts(m_ref[at, :])
            grad = back[at, :]
            dgain_ref[...] = dgain_ref[...] + jnp.sum(grad * normal, axis=0, keepdims=True)
            grad = grad * gain_ref[...]
            mean = jnp.mean(grad, axis=1, keepdims=True)
            along = jnp.mean(grad * normal, axis=1, keepdims=True)
            dm_ref[at, :] = g_ref[at, :] + inverse * (grad - mean - normal * along)

        pieces_of(rows, piece, finish)


def feed_backward(upstream, middle, gain, hidden_values, expand, reduce):
    rows, width = middle.shape
    hidden = hidden_units(expand)
    block, piece = (512, rows) if rows <= 512 else (256, 256)
    whole = lambda j: (0, 0)
    once = pl.Buffered(1)
    dm, dgain, dexpand, dreduce = pl.pallas_call(
        partial(backward_kernel, min(piece, rows)),
        grid=(hidden // block,),
        in_specs=[
            pl.BlockSpec((rows, width), whole, pipeline_mode=once),
            pl.BlockSpec((rows, width), whole, pipeline_mode=once),
            pl.BlockSpec((1, width), whole),
            pl.BlockSpec((rows, block), lambda j: (0, j)),
            *weight_specs(expand, reduce, block),
        ],
        out_specs=[
            pl.BlockSpec((rows, width), whole, pipeline_mode=once),
            pl.BlockSpec((1, width), whole),
            pl.BlockSpec((width, block), lambda j: (0, j)),
            pl.BlockSpec((block, width), lambda j: (j, 0)),
        ],
        out_shape=[
            jax.ShapeDtypeStruct((rows, width), jnp.float32),
            jax.ShapeDtypeStruct((1, width), jnp.float32),
            jax.ShapeDtypeStruct((width, hidden), jnp.float32),
            jax.ShapeDtypeStruct((hidden, width), jnp.float32),
        ],
        scratch_shapes=[
            VMEM((rows, 3 * width), NARROW),
            VMEM((width, rows), NARROW),
            VMEM((width, rows), NARROW),
            VMEM((width, rows), NARROW),
            VMEM((width, rows), NARROW),
            VMEM((rows, block), NARROW),
            VMEM((rows, block), NARROW),
            VMEM((rows, block), NARROW),
            VMEM((rows, block), NARROW),
            VMEM((rows, width), jnp.float32),
        ],
        compiler_params=pltpu.CompilerParams(vmem_limit_bytes=56 << 20),
        cost_estimate=pl.CostEstimate(
            flops=24 * rows * width * hidden, bytes_accessed=4 * rows * hidden, transcendentals=0
        ),
        name="feed_backward",
    )(upstream, middle, gain.reshape(1, width), hidden_values, expand, reduce)
    return dm, dgain[0], dexpand, dreduce


GATHER_TARGET = 60000
SCATTER_TARGET = 26000


precise = lax.Precision.HIGH
everywhere = ("dp", "fsdp")


def product(operand, factor):
    return jnp.dot(operand, factor, precision=precise, preferred_element_type=jnp.float32)


def transposed_left(operand, factor):
    return lax.dot_general(
        operand,
        factor,
        (((0,), (0,)), ((), ())),
        precision=precise,
        preferred_element_type=jnp.float32,
    )


def against(operand, factor):
    return lax.dot_general(
        operand,
        factor,
        (((1,), (1,)), ((), ())),
        precision=precise,
        preferred_element_type=jnp.float32,
    )


def normalize(values, gain_row):
    center = values - jnp.mean(values, axis=-1, keepdims=True)
    inverse = lax.rsqrt(jnp.mean(center * center, axis=-1, keepdims=True) + 1e-06)
    return center * inverse * gain_row


def position_table(length, breadth):
    half_width = breadth // 2
    indices = jnp.arange(length, dtype=jnp.float32)[:, None]
    frequency = jnp.exp(
        jnp.arange(half_width, dtype=jnp.float32) * (-math.log(10000.0) / half_width)
    )[None, :]
    angles = indices * frequency
    return jnp.concatenate([jnp.sin(angles), jnp.cos(angles)], axis=1)


def block_forward(states, gain_pair, matrices):
    first_norm, first_back = jax.vjp(normalize, states, gain_pair[0])
    packed = product(first_norm, matrices[0])
    mixture, logsum = attend_forward(packed)
    middle = states + product(mixture, matrices[1])
    result, hidden = feed_forward(middle, gain_pair[1], matrices[2], matrices[3])
    return result, (first_norm, first_back, packed, mixture, logsum, middle, hidden)


def block_backward(upstream, gain_pair, matrices, stored, beside, begins):
    first_norm, first_back, packed, mixture, logsum, middle, hidden = stored
    middle_grad, second_gain, expand_grad, reduce_grad = feed_backward(
        upstream, middle, gain_pair[1], hidden, matrices[2], matrices[3]
    )
    if begins:
        beside.begin([expand_grad, reduce_grad])
    middle_grad = beside.advance(middle_grad)
    merge_grad = transposed_left(mixture, middle_grad)
    mixture_grad = against(middle_grad, matrices[1])
    if begins:
        mixture_grad = beside.advance(mixture_grad)
    packed_grad = attend_backward(packed, mixture, logsum, mixture_grad)
    packed_grad = beside.advance(packed_grad)
    attend_grad = transposed_left(first_norm, packed_grad)
    states_part, first_gain = first_back(against(packed_grad, matrices[0]))
    gain_grads = jnp.stack([first_gain, second_gain])
    return (
        middle_grad + states_part,
        gain_grads,
        (attend_grad, merge_grad, expand_grad, reduce_grad),
    )


def collect(weights, collective_id):
    columns, rows = lax.axis_size("dp"), lax.axis_size("fsdp")
    if all(weight.shape[0] % 16 == 0 for weight in weights):
        wholes = gather(weights, columns, rows, collective_id, GATHER_TARGET)
        return [whole.reshape(-1, whole.shape[3]) for whole in wholes]
    return [
        lax.all_gather(
            lax.all_gather(weight, "dp", axis=1, tiled=True), "fsdp", axis=0, tiled=True
        )
        for weight in weights
    ]


def spread(gradients, small, collective_id):
    columns, rows = lax.axis_size("dp"), lax.axis_size("fsdp")
    if all(gradient.shape[0] % (rows * 16) == 0 for gradient in gradients):
        wholes = [
            gradient.reshape(4, rows // 4, gradient.shape[0] // rows, gradient.shape[1])
            for gradient in gradients
        ]
        return scatter(wholes, small, columns, rows, collective_id, SCATTER_TARGET)
    parts = [
        lax.psum_scatter(
            lax.psum_scatter(gradient, "fsdp", scatter_dimension=0, tiled=True),
            "dp",
            scatter_dimension=1,
            tiled=True,
        )
        for gradient in gradients
    ]
    return parts, (None if small is None else lax.psum(small, everywhere))


def exchange_steps(columns, rows, near_first):
    def bits(size):
        return [1 << place for place in reversed(range(size.bit_length() - 1))]

    across = [("dp", bit, 0) for bit in bits(columns) if bit > 1]
    far = [("fsdp", bit, 2) for bit in bits(rows) if bit >= rows // 4]
    near = [("fsdp", bit, 3) for bit in bits(rows) if bit < rows // 4]
    return near + across + far if near_first else across + near + far


class Beside:
    def __init__(self):
        self.views, self.steps = [], []

    def begin(self, gradients):
        columns, rows = lax.axis_size("dp"), lax.axis_size("fsdp")
        for place, gradient in enumerate(gradients):
            height, width = gradient.shape
            share = width // columns
            panels = jnp.stack(
                [gradient[:, start : start + share] for start in range(0, width, share)]
            )
            self.views.append(
                panels.reshape(columns // 2, 2, 4, rows // 4, height // rows, share)
            )
            self.steps.append([("dp", 1, 1)] + exchange_steps(columns, rows, place % 2 == 0))

    def divided(self, place, upper, axis):
        view = self.views[place]
        half = view.shape[axis] // 2
        keep = lax.dynamic_slice_in_dim(view, upper * half, half, axis=axis)
        return keep, lax.dynamic_slice_in_dim(view, (1 - upper) * half, half, axis=axis)

    def advance(self, main):
        if not self.steps[0]:
            return main
        sent, kept, steps = [], [], [steps.pop(0) for steps in self.steps]
        for place, (name, bit, axis) in enumerate(steps):
            upper = jnp.bitwise_and(lax.axis_index(name) // bit, 1)
            keep, send = self.divided(place, upper, axis)
            sent.append(send)
            kept.append(keep)
        main, sent = lax.optimization_barrier((main, sent))
        self.views = [
            keep
            + lax.ppermute(
                send, name, [(place, place ^ bit) for place in range(lax.axis_size(name))]
            )
            for send, keep, (name, bit, _) in zip(sent, kept, steps)
        ]
        return main

    def finish(self):
        while self.steps[0]:
            self.advance(jnp.zeros((), jnp.float32))
        return [view.reshape(view.shape[4:]) for view in self.views]


def collect_beside(weights):
    columns, rows = lax.axis_size("dp"), lax.axis_size("fsdp")
    attend, merge, expand, reduce = weights
    padded = jnp.pad(merge, ((0, 0), (0, attend.shape[1] - merge.shape[1])))
    both = lax.all_gather(jnp.concatenate([attend, padded], axis=0), everywhere, axis=0)

    def panels(blocks):
        return blocks.reshape(columns, rows * blocks.shape[1], blocks.shape[2])

    def whole(blocks):
        return jnp.concatenate(list(panels(blocks)), axis=1)

    height = expand.shape[0]
    beside = [reduce[start : start + height] for start in range(0, reduce.shape[0], height)]
    stretches = jnp.concatenate(beside, axis=1)
    if reduce.shape[1] % 128 == 0 and stretches.shape == expand.shape and len(beside) == columns:
        rest = lax.all_gather(jnp.concatenate([expand, stretches], axis=0), everywhere, axis=0)
        expand = reduce = rest.reshape(columns, rows, 2 * height, expand.shape[1])
    else:
        expand, reduce = (
            whole(lax.all_gather(weight, everywhere, axis=0)) for weight in (expand, reduce)
        )
    return [
        whole(both[:, : attend.shape[0]]),
        whole(both[:, attend.shape[0] :, : merge.shape[1]]),
        expand,
        reduce,
    ]


def pack_small(arrays):
    flat = jnp.concatenate([array.reshape(-1) for array in arrays])
    size = -(-flat.shape[0] // 1024) * 1024
    return jnp.pad(flat, (0, size - flat.shape[0])).reshape(-1, 128)


def unpack_small(packed, arrays):
    flat, start, out = packed.reshape(-1), 0, []
    for array in arrays:
        out.append(flat[start : start + array.size].reshape(array.shape))
        start += array.size
    return out


def place(choice, values):
    high = lax.reduce_precision(values, 8, 7)
    low = values - high
    wide = choice.astype(jnp.bfloat16)
    return jnp.dot(
        wide, high.astype(jnp.bfloat16), preferred_element_type=jnp.float32
    ) + jnp.dot(wide, low.astype(jnp.bfloat16), preferred_element_type=jnp.float32)


def local(
    tokens,
    sensor_tag,
    block_dest,
    block_order,
    sensor_table,
    encoder_gains,
    encoder_attend,
    encoder_merge,
    encoder_expand,
    encoder_reduce,
    bridge,
    mask_token,
    decoder_gains,
    decoder_attend,
    decoder_merge,
    decoder_expand,
    decoder_reduce,
    cotangent,
):
    groups = lax.axis_size("fsdp")
    visible = tokens.shape[0]
    capacity = 2 * visible // groups
    length = block_order.shape[1]
    breadth = mask_token.shape[0]
    destination = block_dest[:, 0]
    chooser = (destination[:, None] == jnp.arange(groups, dtype=jnp.int32)[None, :]).astype(
        jnp.int32
    )
    tallies = jnp.zeros((16, 128), jnp.float32)
    tallies = tallies.at[0, :groups].set(jnp.sum(chooser, axis=0).astype(jnp.float32))
    expand, attend, reduce, merge, to_decoder, all_tallies = collect(
        [encoder_expand, encoder_attend, encoder_reduce, encoder_merge, bridge, tallies], 1
    )
    encoder_set = [attend, merge, expand, reduce, to_decoder]
    mine = all_tallies.reshape(groups, 16, -1, 128)[:, 0]
    mine = lax.dynamic_index_in_dim(mine, lax.axis_index("dp"), axis=1, keepdims=False)
    arrived_tallies = lax.dynamic_slice_in_dim(mine, lax.axis_index("fsdp"), 1, axis=1)
    decoder_set = collect_beside(
        lax.optimization_barrier(
            (decoder_attend, decoder_merge, decoder_expand, decoder_reduce, encoder_set[4])
        )[:4]
    )
    tag_row = (
        sensor_tag[:, None] == jnp.arange(sensor_table.shape[0], dtype=jnp.int32)[None, :]
    ).astype(jnp.float32)
    initial = tokens + product(tag_row, sensor_table)
    encoded, encoder_kept = block_forward(initial, encoder_gains, encoder_set)
    projected = product(encoded, encoder_set[4])
    ranking = jnp.sum((jnp.cumsum(chooser, axis=0) - chooser) * chooser, axis=1)
    slot_index = destination * capacity + ranking
    select = (
        slot_index[None, :] == jnp.arange(groups * capacity, dtype=jnp.int32)[:, None]
    ).astype(jnp.float32)
    outgoing = place(select, projected).reshape(groups, capacity, breadth)
    arrived = lax.all_to_all(outgoing, "fsdp", split_axis=0, concat_axis=0, tiled=True)
    present = (jnp.arange(capacity, dtype=jnp.float32)[None, :] < arrived_tallies).reshape(-1)
    ordering = block_order[0, : groups * capacity]
    placing = (
        (ordering[None, :] == jnp.arange(length, dtype=jnp.int32)[:, None]) & present[None, :]
    ).astype(jnp.float32)
    covered = jnp.sum(placing, axis=1, keepdims=True)
    filled = (
        place(placing, arrived.reshape(groups * capacity, breadth))
        + (1.0 - covered) * mask_token
        + position_table(length, breadth)
    )
    decoded, decoder_kept = block_forward(filled, decoder_gains, decoder_set)
    beside = Beside()
    filled_grad, decoder_gain_grad, decoder_grads = block_backward(
        cotangent, decoder_gains, decoder_set, decoder_kept, beside, True
    )
    mask_grad = jnp.sum((1.0 - covered) * filled_grad, axis=0)
    arrived_grad = place(placing.T, filled_grad).reshape(groups, capacity, breadth)
    returned = lax.all_to_all(arrived_grad, "fsdp", split_axis=0, concat_axis=0, tiled=True)
    projected_grad = place(select.T, returned.reshape(groups * capacity, breadth))
    bridge_grad = transposed_left(encoded, projected_grad)
    encoded_grad = against(projected_grad, encoder_set[4])
    tokens_grad, encoder_gain_grad, encoder_grads = block_backward(
        encoded_grad, encoder_gains, encoder_set, encoder_kept, beside, False
    )
    table_grad = transposed_left(tag_row, jnp.sum(tokens_grad, axis=0, keepdims=True))
    small = (table_grad, encoder_gain_grad, mask_grad, decoder_gain_grad)
    packed_small = pack_small(small)
    spreads, total = spread(
        [
            decoder_grads[1],
            encoder_grads[1],
            decoder_grads[0],
            bridge_grad,
            encoder_grads[0],
            encoder_grads[2],
            encoder_grads[3],
        ],
        packed_small,
        3,
    )
    encoder_spread = [spreads[4], spreads[1], spreads[5], spreads[6], spreads[3]]
    expand_sum, reduce_sum = beside.finish()
    decoder_spread = [spreads[2], spreads[0], expand_sum, reduce_sum]
    summed = unpack_small(total, small)
    return (
        decoded,
        tokens_grad,
        summed[0],
        summed[1],
        encoder_spread[0],
        encoder_spread[1],
        encoder_spread[2],
        encoder_spread[3],
        encoder_spread[4],
        summed[2],
        summed[3],
        decoder_spread[0],
        decoder_spread[1],
        decoder_spread[2],
        decoder_spread[3],
    )


def solution(mesh):
    in_specs = (
        P(("dp", "fsdp"), None),
        P(("dp", "fsdp")),
        P(("dp", "fsdp"), None),
        P(("dp", "fsdp"), None),
        P(),
        P(),
        P("fsdp", "dp"),
        P("fsdp", "dp"),
        P("fsdp", "dp"),
        P("fsdp", "dp"),
        P("fsdp", "dp"),
        P(),
        P(),
        P("fsdp", "dp"),
        P("fsdp", "dp"),
        P("fsdp", "dp"),
        P("fsdp", "dp"),
        P(("dp", "fsdp"), None),
    )
    out_specs = (
        P(("dp", "fsdp"), None),
        P(("dp", "fsdp"), None),
        P(),
        P(),
        P("fsdp", "dp"),
        P("fsdp", "dp"),
        P("fsdp", "dp"),
        P("fsdp", "dp"),
        P("fsdp", "dp"),
        P(),
        P(),
        P("fsdp", "dp"),
        P("fsdp", "dp"),
        P("fsdp", "dp"),
        P("fsdp", "dp"),
    )
    return jax.shard_map(local, mesh=mesh, in_specs=in_specs, out_specs=out_specs, check_vma=False)
```

```python
from functools import partial
import math

import jax
import jax.numpy as jnp
from jax import lax
from jax.experimental import pallas as pl
from jax.experimental.pallas import tpu as pltpu
from jax.sharding import PartitionSpec as P

MESH = pl.DeviceIdType.MESH
VMEM = pltpu.VMEM
NARROW = jnp.bfloat16
LONG = (("b", "a", "x"), ("x", "a", "b"))
SHORT = (("a", "x", "b"), ("a", "b", "x"))
GATHER_TURNS = (SHORT, LONG, LONG)
SCATTER_TURNS = (LONG, LONG, SHORT)
AHEAD = 2
SLACK = 2


class Grid:
    def __init__(self, dp, fsdp):
        self.size = {"x": dp // 2, "a": 4, "b": fsdp // 4}
        column, row = lax.axis_index("dp"), lax.axis_index("fsdp")
        self.core = lax.rem(column, 2)
        self.at = {
            "x": lax.div(column, 2),
            "a": lax.div(row, self.size["b"]),
            "b": lax.rem(row, self.size["b"]),
        }

    def device(self, core=None, **moved):
        at = {**self.at, **moved}
        core = self.core if core is None else core
        return (at["x"] * 2 + core, at["a"] * self.size["b"] + at["b"])

    def greet(self, reach):
        barrier = pltpu.get_barrier_semaphore()
        pl.semaphore_signal(
            barrier, inc=1, device_id=self.device(1 - self.core), device_id_type=MESH
        )
        count = 1
        for axis, size in self.size.items():
            here = self.at[axis]
            for move in range(-min(reach, size - 1), min(reach, size - 1) + 1):
                if move:
                    exists = together(here + move >= 0, here + move < size)
                    count = count + jnp.where(exists, 1, 0)

                    @pl.when(exists)
                    def _(axis=axis, here=here, move=move):
                        pl.semaphore_signal(
                            barrier,
                            inc=1,
                            device_id=self.device(**{axis: here + move}),
                            device_id_type=MESH,
                        )

        pl.semaphore_wait(barrier, count)


def plan_rounds(shapes, target, turns):
    plan, turn = [], 0
    for rows, columns in shapes:
        units = rows // 16
        pairs = max(1, min(units // 2, round(units * 8 * columns * 2 / target)))
        parts, start = [], 0
        for pair in range(pairs):
            orders = turns[turn % len(turns)]
            for place, order in enumerate(orders):
                take = -(-(units - start) // (2 * (pairs - pair) - place))
                if take:
                    parts.append((order, start * 8, take * 8, turn))
                start += take
            turn += 1
        plan.append(parts)
    return plan


def together(*conditions):
    joined = conditions[0]
    for condition in conditions[1:]:
        joined = jnp.logical_and(joined, condition)
    return joined


class Traffic:
    def __init__(self, grid, send, receive):
        self.grid, self.send, self.receive = grid, send, receive
        self.count, self.open = 0, []

    def copy(self, source, target, device, starts, arrives):
        place = self.count
        self.count += 1

        def made():
            return pltpu.make_async_remote_copy(
                src_ref=source,
                dst_ref=target,
                send_sem=self.send.at[place],
                recv_sem=self.receive.at[place],
                device_id=device,
                device_id_type=MESH,
            )

        if starts is None:
            made().start()
        else:

            @pl.when(starts)
            def _():
                made().start()

        self.open.append((made, starts))
        return (made, arrives)

    def arrive(self, handle):
        made, arrives = handle
        if arrives is None:
            made().wait_recv()
        else:

            @pl.when(arrives)
            def _():
                made().wait_recv()

    def take(self, handle):
        handle[0]().wait_recv()

    def drain(self, handle):
        handle[0]().wait_send()
        self.open = [entry for entry in self.open if entry[0] is not handle[0]]

    def close(self):
        for made, starts in self.open:
            if starts is None:
                made().wait_send()
            else:

                @pl.when(starts)
                def _():
                    made().wait_send()


def block_of(full, chosen, offset, rows, width):
    view = []
    for axis in ("a", "b"):
        place = chosen[axis]
        view.append(slice(None) if place is None else pl.ds(place, 1))
    columns = (
        slice(None)
        if chosen["x"] is None
        else pl.ds(pl.multiple_of(chosen["x"] * width, 128), width)
    )
    return full.at[(*view, pl.ds(pl.multiple_of(offset, 8), rows), columns)]


def pause():
    for _ in range(SLACK):
        yield


def gather_line(traffic, axis, chosen, view, exists, arrived):
    grid = traffic.grid
    here, size = grid.at[axis], grid.size[axis]

    def both(condition):
        return condition if exists is None else together(exists, condition)

    arrived({**chosen, axis: here}, exists)
    for step in range(1, size):
        ahead, behind = {**chosen, axis: here - (step - 1)}, {**chosen, axis: here + (step - 1)}
        rightward = traffic.copy(
            view(ahead),
            view(ahead),
            grid.device(**{axis: here + 1}),
            both(together(here + 1 < size, here - (step - 1) >= 0)),
            both(here - step >= 0),
        )
        leftward = traffic.copy(
            view(behind),
            view(behind),
            grid.device(**{axis: here - 1}),
            both(together(here - 1 >= 0, here + (step - 1) < size)),
            both(here + step < size),
        )
        yield from pause()
        traffic.arrive(rightward)
        arrived({**chosen, axis: here - step}, both(here - step >= 0))
        traffic.arrive(leftward)
        arrived({**chosen, axis: here + step}, both(here + step < size))


def gather_part(traffic, order, view, spawn, share):
    first, second, third = order
    grid = traffic.grid
    own = dict(grid.at)

    def last(chosen, exists):
        def finish():
            yield from gather_line(traffic, third, chosen, view, exists, lambda *_: None)
            share(view({**chosen, third: None}), exists)

        spawn(finish())

    def begin():
        if grid.size[first] == 2:
            yield from gather_line(traffic, first, own, view, None, lambda *_: None)
            yield from gather_line(traffic, second, {**own, first: None}, view, None, last)
        else:

            def middle(chosen, exists):
                def go():
                    yield from gather_line(traffic, second, chosen, view, exists, lambda *_: None)
                    last({**chosen, second: None}, exists)

                spawn(go())

            yield from gather_line(traffic, first, own, view, None, middle)

    spawn(begin())


def run_rounds(starts):
    active = []

    def spawn(generator):
        try:
            next(generator)
            active.append(generator)
        except StopIteration:
            pass

    for start in starts:
        for begin in start:
            begin(spawn)
        advance_all(active)
    while active:
        advance_all(active)


def advance_all(active):
    for generator in list(active):
        try:
            next(generator)
        except StopIteration:
            active.remove(generator)


def gather_kernel(dp, fsdp, shapes, plan, *refs):
    number = len(shapes)
    shards, wholes = refs[:number], refs[number : 2 * number]
    raws, blocks = refs[2 * number : 3 * number], refs[3 * number : 4 * number]
    send, receive, pair_send, pair_receive, local = refs[4 * number :]
    grid = Grid(dp, fsdp)
    traffic = Traffic(grid, send, receive)
    pair = Traffic(grid, pair_send, pair_receive)
    core, other = grid.core, 1 - grid.core
    sibling = grid.device(other)
    grid.greet(1)
    handles = []
    for index, (rows, columns) in enumerate(shapes):
        half = rows // 2
        theirs = shards[index].at[pl.ds(pl.multiple_of(other * half, 8), half)]
        handles.append(pair.copy(theirs, raws[index], sibling, None, None))
    stores = []
    for index, (rows, columns) in enumerate(shapes):
        half = rows // 2
        pair.arrive(handles[index])
        mine = shards[index][pl.ds(pl.multiple_of(core * half, 8), half), :]
        came = raws[index][...]
        blocks[index][0, 0] = jnp.where(
            core == 0,
            jnp.concatenate([mine, came], axis=1),
            jnp.concatenate([came, mine], axis=1),
        )
        store = pltpu.make_async_copy(
            blocks[index],
            block_of(wholes[index], grid.at, core * half, half, 2 * columns),
            local.at[index],
        )
        store.start()
        stores.append(store)
    for store in stores:
        store.wait()
    pending = []

    def share(piece, exists):
        pending.append(pair.copy(piece, piece, sibling, exists, exists))

    starts = [[] for _ in range(1 + max(part[3] for parts in plan for part in parts))]
    for index, (rows, columns) in enumerate(shapes):
        half = rows // 2
        for order, offset, count, turn in plan[index]:

            def view(chosen, index=index, offset=offset, count=count, half=half, columns=columns):
                return block_of(wholes[index], chosen, core * half + offset, count, 2 * columns)

            starts[turn].append(
                lambda spawn, order=order, view=view: gather_part(
                    traffic, order, view, spawn, share
                )
            )
    run_rounds(starts)
    for handle in pending:
        pair.arrive(handle)
    traffic.close()
    pair.close()


def gather(weights, dp, fsdp, collective_id, target):
    shapes = [weight.shape for weight in weights]
    a, b = 4, fsdp // 4
    plan = plan_rounds(shapes, target, GATHER_TURNS)
    total = sum(len(parts) for parts in plan)
    out = [jax.ShapeDtypeStruct((a, b, r, dp * c), jnp.float32) for r, c in shapes]
    vmem = pl.BlockSpec(memory_space=VMEM)
    return pl.pallas_call(
        partial(gather_kernel, dp, fsdp, shapes, plan),
        out_shape=out,
        in_specs=[vmem] * len(shapes),
        out_specs=[pl.BlockSpec(memory_space=pl.ANY)] * len(shapes),
        scratch_shapes=[VMEM((r // 2, c), jnp.float32) for r, c in shapes]
        + [VMEM((1, 1, r // 2, 2 * c), jnp.float32) for r, c in shapes]
        + [
            pltpu.SemaphoreType.DMA((34 * total,)),
            pltpu.SemaphoreType.DMA((34 * total,)),
            pltpu.SemaphoreType.DMA((8 * total + len(shapes),)),
            pltpu.SemaphoreType.DMA((8 * total + len(shapes),)),
            pltpu.SemaphoreType.DMA((len(shapes),)),
        ],
        compiler_params=pltpu.CompilerParams(
            collective_id=collective_id, has_side_effects=True, vmem_limit_bytes=32 << 20
        ),
        name="gather_weights",
    )(*weights)


def landing_shapes(size, order, rows, width):
    chosen, shapes = {"x": size["x"], "a": size["a"], "b": size["b"]}, []
    for axis in reversed(order):
        chosen[axis] = 1
        slots = 1 if size[axis] == 2 else 2 * (size[axis] - 1)
        shapes.append((slots, chosen["a"], chosen["b"], rows, chosen["x"] * width))
    return shapes


def sum_line(traffic, axis, chosen, view, landing):
    grid = traffic.grid
    here, size = grid.at[axis], grid.size[axis]
    ends = size - 1

    def slot(rightward, place):
        if size == 2:
            return 0
        return place - 1 if rightward else ends + place

    def blocks(place):
        return view({**chosen, axis: place})

    def add(rightward, place):
        target = blocks(place)
        target[...] += landing[slot(rightward, place)]

    def send(rightward, place, starts, arrives):
        return traffic.copy(
            blocks(place),
            landing.at[slot(rightward, place)],
            grid.device(**{axis: here + (1 if rightward else -1)}),
            starts,
            arrives,
        )

    first = {}
    for place in range(ends, 0, -1):
        first[True, place] = send(
            True, place, here == 0, here == 1
        )
    for place in range(ends):
        first[False, place] = send(False, place, here == ends, here == ends - 1)
    later = {}
    for step in range(ends - 1):
        yield from pause()
        for come in range(1, ends):
            place = ends - step + come - 1
            if come < place <= ends:
                @pl.when(here == come)
                def _(come=come, place=place):
                    traffic.take(first[True, place] if come == 1 else later[True, come - 1, place])
                    add(True, place)

                later[True, come, place] = send(True, place, here == come, here == come + 1)
            come, place = ends - come, ends - place
            if come > place >= 0:

                @pl.when(here == come)
                def _(come=come, place=place):
                    traffic.take(
                        first[False, place] if come == ends - 1 else later[False, come + 1, place]
                    )
                    add(False, place)

                later[False, come, place] = send(False, place, here == come, here == come - 1)
    yield from pause()
    for place in range(size):

        @pl.when(here == place)
        def _(place=place):
            if place > 0:
                traffic.take(first[True, place] if place == 1 else later[True, place - 1, place])
                add(True, place)
            if place < ends:
                traffic.take(
                    first[False, place] if place == ends - 1 else later[False, place + 1, place]
                )
                add(False, place)


def sum_part(traffic, order, view, landings):
    chosen = {"x": None, "a": None, "b": None}
    for axis, landing in zip(reversed(order), landings):
        yield from sum_line(traffic, axis, chosen, view, landing)
        chosen[axis] = traffic.grid.at[axis]


def total_everywhere(traffic, pair, value, pair_landing, landings):
    grid = traffic.grid
    came = pair.copy(value, pair_landing, grid.device(1 - grid.core), None, None)
    yield
    pair.arrive(came)
    pair.drain(came)
    value[...] += pair_landing[...]
    for axis, landing in zip(("x", "b", "a"), landings):
        here, size = grid.at[axis], grid.size[axis]
        handles = []
        for move in range(1, size):
            target = lax.rem(here + move, size)
            source = lax.rem(here + size - move, size)
            handles.append(
                (
                    traffic.copy(
                        value, landing.at[here], grid.device(**{axis: target}), None, None
                    ),
                    source,
                )
            )
        landing[here] = value[...]
        yield
        for handle, _ in handles:
            traffic.arrive(handle)
            traffic.drain(handle)
        total = landing[0]
        for place in range(1, size):
            total = total + landing[place]
        value[...] = total


def scatter_kernel(dp, fsdp, shapes, pieces, has_small, *refs):
    number = len(shapes)
    refs = list(refs)

    def take(count):
        taken = refs[:count]
        del refs[:count]
        return taken

    wholes, small = take(number), (take(1)[0] if has_small else None)
    outs, small_out = take(number), (take(1)[0] if has_small else None)
    sums, others, finals = take(number), take(number), take(number)
    landings = [[take(3) for _ in parts] for parts in pieces]
    if has_small:
        small_pair, *small_landings = take(4)
    send, receive, pair_send, pair_receive, local = refs
    grid = Grid(dp, fsdp)
    traffic = Traffic(grid, send, receive)
    pair = Traffic(grid, pair_send, pair_receive)
    core, other = grid.core, 1 - grid.core
    sibling = grid.device(other)
    grid.greet(max(grid.size.values()) if small is not None else 1)
    starts = [[] for _ in range(1 + max(part[3] for parts in pieces for part in parts))]
    if has_small:
        small_out[...] = small[...]
        starts[0].append(
            lambda spawn: spawn(
                total_everywhere(traffic, pair, small_out, small_pair, small_landings)
            )
        )
    place, runs = 0, []
    for index, (rows, columns) in enumerate(shapes):
        half = rows // 2
        for part, (order, offset, count, turn) in enumerate(pieces[index]):
            window = (slice(None), slice(None), slice(offset, offset + count))
            fetched = []

            def fetch(index=index, half=half, offset=offset, count=count, window=window,
                      fetched=fetched, place=place):
                def stretch(at):
                    start = pl.multiple_of(at * half + offset, 8)
                    return wholes[index].at[:, :, pl.ds(start, count), :]

                came = pair.copy(stretch(other), others[index].at[window], sibling, None, None)
                load = pltpu.make_async_copy(
                    stretch(core), sums[index].at[window], local.at[place]
                )
                load.start()
                fetched.extend((came, load))

            ahead = max(0, turn - AHEAD)
            starts[ahead].append(lambda spawn, fetch=fetch: fetch())
            place += 1

            def run(index=index, order=order, offset=offset, count=count, window=window,
                    fetched=fetched, columns=columns, part=part):
                fetched[1].wait()
                pair.arrive(fetched[0])
                sums[index][window] += others[index][window]

                def view(chosen):
                    return block_of(sums[index], chosen, offset, count, 2 * columns)

                yield from sum_part(traffic, order, view, landings[index][part])

            runs.append((turn, lambda spawn, run=run: spawn(run())))
    for turn, run in runs:
        starts[turn].append(run)
    run_rounds(starts)
    handles = []
    for index, (rows, columns) in enumerate(shapes):
        half = rows // 2
        block = block_of(sums[index], grid.at, 0, half, 2 * columns)
        handles.append(pair.copy(block, finals[index], sibling, None, None))
    for index, (rows, columns) in enumerate(shapes):
        half = rows // 2
        block = block_of(sums[index], grid.at, 0, half, 2 * columns)[0, 0]
        pair.arrive(handles[index])
        came = finals[index][0, 0]
        for value, at in ((block, core), (came, other)):
            outs[index][pl.ds(pl.multiple_of(at * half, 8), half), :] = jnp.where(
                core == 0, value[:, :columns], value[:, columns:]
            )
    traffic.close()
    pair.close()


def scatter(wholes, small, dp, fsdp, collective_id, target):
    size = {"x": dp // 2, "a": 4, "b": fsdp // 4}
    shapes = [(whole.shape[2], whole.shape[3] // dp) for whole in wholes]
    pieces = plan_rounds(shapes, target, SCATTER_TURNS)
    number = len(shapes)
    total = sum(len(parts) for parts in pieces)
    scratch = []
    for _ in range(2):
        scratch += [VMEM((size["a"], size["b"], r // 2, dp * c), jnp.float32) for r, c in shapes]
    scratch += [VMEM((1, 1, r // 2, 2 * c), jnp.float32) for r, c in shapes]
    for (rows, columns), parts in zip(shapes, pieces):
        for order, _, count, _ in parts:
            for shape in landing_shapes(size, order, count, 2 * columns):
                scratch.append(VMEM(shape, jnp.float32))
    smalls = [] if small is None else [small]
    for array in smalls:
        scratch.append(VMEM(array.shape, jnp.float32))
        for axis in ("x", "b", "a"):
            scratch.append(VMEM((size[axis], *array.shape), jnp.float32))
    hops = 2 * sum(size.values()) + sum((length - 1) * length for length in size.values())
    scratch += [
        pltpu.SemaphoreType.DMA((total * hops + 40,)),
        pltpu.SemaphoreType.DMA((total * hops + 40,)),
        pltpu.SemaphoreType.DMA((total + number + 1,)),
        pltpu.SemaphoreType.DMA((total + number + 1,)),
        pltpu.SemaphoreType.DMA((total,)),
    ]
    vmem = pl.BlockSpec(memory_space=VMEM)
    results = pl.pallas_call(
        partial(scatter_kernel, dp, fsdp, shapes, pieces, small is not None),
        out_shape=[jax.ShapeDtypeStruct(shape, jnp.float32) for shape in shapes]
        + [jax.ShapeDtypeStruct(array.shape, jnp.float32) for array in smalls],
        in_specs=[pl.BlockSpec(memory_space=pl.ANY)] * number + [vmem] * len(smalls),
        out_specs=[vmem] * (number + len(smalls)),
        scratch_shapes=scratch,
        compiler_params=pltpu.CompilerParams(
            collective_id=collective_id, has_side_effects=True, vmem_limit_bytes=60 << 20
        ),
        name="scatter_sums",
    )(*wholes, *smalls)
    return results[:number], (results[number] if smalls else None)


HEAD = 64


def split(values):
    high = values.astype(NARROW)
    return high, (values - high.astype(jnp.float32)).astype(NARROW)


def tripled(values, leading):
    high, low = split(values)
    return jnp.concatenate([high, high, low] if leading else [high, low, high], axis=1)


def dot(left, right, contract=(1, 0)):
    return lax.dot_general(
        left,
        right,
        (((contract[0],), (contract[1],)), ((), ())),
        preferred_element_type=jnp.float32,
    )


def attend_kernel(chunk, q_ref, k_ref, v_ref, out_ref, lse_ref, keys, values):
    rows = q_ref.shape[0]

    @pl.when(pl.program_id(1) == 0)
    def _():
        for head in range(2):
            part = slice(head * HEAD, (head + 1) * HEAD)
            keys[head] = tripled(k_ref[:, part], False)
            values[head] = jnp.concatenate(split(v_ref[:, part]), axis=1)

    for start in range(0, rows, chunk):
        at = slice(start, start + chunk)
        outs = []
        for head in range(2):
            part = slice(head * HEAD, (head + 1) * HEAD)
            queries = tripled(q_ref[at, part] * (1.0 / math.sqrt(HEAD)), True)
            scores = dot(queries, keys[head], (1, 1))
            top = jnp.max(scores, axis=1, keepdims=True)
            weights = jnp.exp(scores - top)
            total = jnp.sum(weights, axis=1, keepdims=True)
            first, second = split(weights)
            both = dot(first, values[head])
            mixed = both[:, :HEAD] + both[:, HEAD:] + dot(second, values[head][:, :HEAD])
            outs.append(mixed * (1.0 / total))
            lse_ref[at, head : head + 1] = top + jnp.log(total)
        out_ref[at, :] = jnp.concatenate(outs, axis=1)


def attend_forward(packed, block=768, chunk=768):
    rows, breadth = packed.shape[0], packed.shape[1] // 3
    pairs = breadth // 128
    block = min(block, rows)
    chunk = min(chunk, block)
    return pl.pallas_call(
        partial(attend_kernel, chunk),
        grid=(pairs, rows // block),
        in_specs=[
            pl.BlockSpec((block, 128), lambda h, i: (i, h)),
            pl.BlockSpec((rows, 128), lambda h, i: (0, pairs + h)),
            pl.BlockSpec((rows, 128), lambda h, i: (0, 2 * pairs + h)),
        ],
        out_specs=[
            pl.BlockSpec((block, 128), lambda h, i: (i, h)),
            pl.BlockSpec((None, block, 128), lambda h, i: (h, i, 0)),
        ],
        out_shape=[
            jax.ShapeDtypeStruct((rows, breadth), jnp.float32),
            jax.ShapeDtypeStruct((pairs, rows, 128), jnp.float32),
        ],
        scratch_shapes=[
            VMEM((2, rows, 3 * HEAD), NARROW),
            VMEM((2, rows, 2 * HEAD), NARROW),
        ],
        compiler_params=pltpu.CompilerParams(vmem_limit_bytes=48 << 20),
        cost_estimate=pl.CostEstimate(
            flops=12 * rows * rows * breadth, bytes_accessed=20 * rows * breadth, transcendentals=0
        ),
        name="attend_forward",
    )(packed, packed, packed)


def attend_back_kernel(
    chunk, q_ref, k_ref, v_ref, o_ref, g_ref, lse_ref, dq_ref, dk_ref, dv_ref,
    queries, gradients, wide_q, wide_g, row_lse, row_delta, dq,
):
    rows, block = q_ref.shape[0], k_ref.shape[0]
    scale = 1.0 / math.sqrt(HEAD)

    @pl.when(pl.program_id(1) == 0)
    def _():
        for head in range(2):
            part = slice(head * HEAD, (head + 1) * HEAD)
            q = q_ref[:, part] * scale
            g = g_ref[:, part]
            queries[head] = tripled(q, True).T
            gradients[head] = tripled(g, True).T
            wide_q[head] = jnp.concatenate(split(q), axis=1)
            wide_g[head] = jnp.concatenate(split(g), axis=1)
            delta = jnp.sum(g * o_ref[:, part], axis=1, keepdims=True)
            row_delta[head] = jnp.broadcast_to(delta, (rows, 128)).T[:8]
            row_lse[head] = jnp.broadcast_to(lse_ref[:, head : head + 1], (rows, 128)).T[:8]
        dq[...] = jnp.zeros_like(dq)

    for start in range(0, block, chunk):
        at = slice(start, start + chunk)
        dks, dvs = [], []
        for head in range(2):
            part = slice(head * HEAD, (head + 1) * HEAD)
            k = k_ref[at, part]
            scores = dot(tripled(k, False), queries[head])
            weights = jnp.exp(scores - row_lse[head, 0:1])
            slopes = dot(tripled(v_ref[at, part], False), gradients[head])
            slopes = weights * (slopes - row_delta[head, 0:1])
            first, second = split(weights)
            both = dot(first, wide_g[head])
            dvs.append(both[:, :HEAD] + both[:, HEAD:] + dot(second, wide_g[head][:, :HEAD]))
            first, second = split(slopes)
            both = dot(first, wide_q[head])
            dks.append(both[:, :HEAD] + both[:, HEAD:] + dot(second, wide_q[head][:, :HEAD]))
            kt = jnp.concatenate(split(k * scale), axis=1).T
            both = dot(kt, first)
            dq[head] = dq[head] + both[:HEAD] + both[HEAD:] + dot(kt[:HEAD], second)
        dk_ref[at, :] = jnp.concatenate(dks, axis=1)
        dv_ref[at, :] = jnp.concatenate(dvs, axis=1)

    @pl.when(pl.program_id(1) == pl.num_programs(1) - 1)
    def _():
        for head in range(2):
            dq_ref[:, head * HEAD : (head + 1) * HEAD] = dq[head].T


def attend_backward(packed, mixture, lse, upstream, block=512, chunk=256):
    rows, breadth = mixture.shape
    pairs = breadth // 128
    if rows < block:
        block = chunk = rows
    whole = lambda h, i: (0, h)
    stretch = lambda h, i: (i, h)
    parts = pl.pallas_call(
        partial(attend_back_kernel, chunk),
        grid=(pairs, rows // block),
        in_specs=[
            pl.BlockSpec((rows, 128), whole),
            pl.BlockSpec((block, 128), lambda h, i: (i, pairs + h)),
            pl.BlockSpec((block, 128), lambda h, i: (i, 2 * pairs + h)),
            pl.BlockSpec((rows, 128), whole),
            pl.BlockSpec((rows, 128), whole),
            pl.BlockSpec((None, rows, 128), lambda h, i: (h, 0, 0)),
        ],
        out_specs=[
            pl.BlockSpec((rows, 128), whole),
            pl.BlockSpec((block, 128), stretch),
            pl.BlockSpec((block, 128), stretch),
        ],
        out_shape=[jax.ShapeDtypeStruct((rows, breadth), jnp.float32)] * 3,
        scratch_shapes=[
            VMEM((2, 3 * HEAD, rows), NARROW),
            VMEM((2, 3 * HEAD, rows), NARROW),
            VMEM((2, rows, 2 * HEAD), NARROW),
            VMEM((2, rows, 2 * HEAD), NARROW),
            VMEM((2, 8, rows), jnp.float32),
            VMEM((2, 8, rows), jnp.float32),
            VMEM((2, HEAD, rows), jnp.float32),
        ],
        compiler_params=pltpu.CompilerParams(vmem_limit_bytes=48 << 20),
        cost_estimate=pl.CostEstimate(
            flops=30 * rows * rows * breadth, bytes_accessed=32 * rows * breadth, transcendentals=0
        ),
        name="attend_backward",
    )(packed, packed, packed, mixture, upstream, lse)
    return jnp.concatenate(parts, axis=1)


def stacked(values):
    high, low = split(values)
    return jnp.concatenate([high, low, high], axis=0)


def normal_parts(values):
    center = values - jnp.mean(values, axis=1, keepdims=True)
    inverse = lax.rsqrt(jnp.mean(center * center, axis=1, keepdims=True) + 1e-06)
    return center * inverse, inverse


def pieces_of(rows, size, body):
    for start in range(0, rows, size):
        body(slice(start, min(start + size, rows)))


def normal_share(values):
    return 0.5 + 0.5 * lax.erf(values * math.sqrt(0.5))


def weight_specs(expand, reduce, block):
    if expand.ndim == 2:
        return [
            pl.BlockSpec((expand.shape[0], block), lambda j: (0, j)),
            pl.BlockSpec((block, reduce.shape[1]), lambda j: (j, 0)),
        ]
    columns, rows, height, width = expand.shape
    each, deep = width // block, block // (columns * height // 2)
    return [
        pl.BlockSpec(
            (None, rows, height // 2, block), lambda j: (lax.div(j, each), 0, 0, lax.rem(j, each))
        ),
        pl.BlockSpec((columns, deep, height // 2, width), lambda j: (0, j, 1, 0)),
    ]


def hidden_units(expand):
    return expand.shape[1] if expand.ndim == 2 else expand.shape[0] * expand.shape[3]


def expand_of(ref):
    if len(ref.shape) == 2:
        return ref[...]
    return ref[...].reshape(ref.shape[0] * ref.shape[1], ref.shape[2])


def reduce_of(ref):
    if len(ref.shape) == 2:
        return ref[...]
    columns, deep, _, width = ref.shape
    share = width // columns
    return jnp.concatenate(
        [
            jnp.concatenate(
                [ref[column, row, :, part * share : (part + 1) * share] for column in range(columns)],
                axis=1,
            )
            for row in range(deep)
            for part in range(columns)
        ],
        axis=0,
    )


def forward_kernel(piece, m_ref, gain_ref, expand_ref, reduce_ref, out_ref, hidden_ref, wide):
    rows = m_ref.shape[0]

    @pl.when(pl.program_id(0) == 0)
    def _():
        def begin(at):
            wide[at, :] = tripled(normal_parts(m_ref[at, :])[0] * gain_ref[...], True)
            out_ref[at, :] = m_ref[at, :]

        pieces_of(rows, piece, begin)

    expand, reduce = stacked(expand_of(expand_ref)), stacked(reduce_of(reduce_ref))

    def go(at):
        hidden = dot(wide[at, :], expand)
        hidden_ref[at, :] = hidden
        active = hidden * normal_share(hidden)
        out_ref[at, :] = out_ref[at, :] + dot(tripled(active, True), reduce)

    pieces_of(rows, piece, go)


def feed_forward(middle, gain, expand, reduce, block=512, piece=512):
    rows, width = middle.shape
    hidden = hidden_units(expand)
    whole = lambda j: (0, 0)
    return pl.pallas_call(
        partial(forward_kernel, min(piece, rows)),
        grid=(hidden // block,),
        in_specs=[
            pl.BlockSpec((rows, width), whole),
            pl.BlockSpec((1, width), whole),
            *weight_specs(expand, reduce, block),
        ],
        out_specs=[
            pl.BlockSpec((rows, width), whole),
            pl.BlockSpec((rows, block), lambda j: (0, j)),
        ],
        out_shape=[
            jax.ShapeDtypeStruct((rows, width), jnp.float32),
            jax.ShapeDtypeStruct((rows, hidden), jnp.float32),
        ],
        scratch_shapes=[VMEM((rows, 3 * width), NARROW)],
        compiler_params=pltpu.CompilerParams(vmem_limit_bytes=56 << 20),
        cost_estimate=pl.CostEstimate(
            flops=12 * rows * width * hidden, bytes_accessed=4 * rows * hidden, transcendentals=0
        ),
        name="feed_forward",
    )(middle, gain.reshape(1, width), expand, reduce)


def backward_kernel(
    piece, g_ref, m_ref, gain_ref, hidden_ref, expand_ref, reduce_ref,
    dm_ref, dgain_ref, dexpand_ref, dreduce_ref,
    wide, g_high, g_low, b_high, b_low, r_high, r_low, u_high, u_low, back,
):
    rows = g_ref.shape[0]

    @pl.when(pl.program_id(0) == 0)
    def _():
        def begin(at):
            g = g_ref[at, :]
            wide[at, :] = tripled(g, True)
            g_high[:, at], g_low[:, at] = split(g.T)
            normal = normal_parts(m_ref[at, :])[0] * gain_ref[...]
            b_high[:, at], b_low[:, at] = split(normal.T)
            back[at, :] = jnp.zeros_like(g)

        pieces_of(rows, piece, begin)

    expand = tripled(expand_of(expand_ref), False)
    reduce = tripled(reduce_of(reduce_ref), False)

    def go(at):
        hidden = hidden_ref[at, :]
        share = normal_share(hidden)
        r_high[at, :], r_low[at, :] = split(hidden * share)
        bell = jnp.exp(hidden * hidden * -0.5) * (1.0 / math.sqrt(2.0 * math.pi))
        slope = share + hidden * bell
        hidden_grad = slope * dot(wide[at, :], reduce, (1, 1))
        u_high[at, :], u_low[at, :] = split(hidden_grad)
        back[at, :] = back[at, :] + dot(tripled(hidden_grad, True), expand, (1, 1))

    pieces_of(rows, piece, go)
    grad = dot(g_high[...], r_high[...]) + dot(g_high[...], r_low[...])
    dreduce_ref[...] = (grad + dot(g_low[...], r_high[...])).T
    grad = dot(b_high[...], u_high[...]) + dot(b_high[...], u_low[...])
    dexpand_ref[...] = grad + dot(b_low[...], u_high[...])

    @pl.when(pl.program_id(0) == pl.num_programs(0) - 1)
    def _():
        dgain_ref[...] = jnp.zeros_like(dgain_ref)

        def finish(at):
            normal, inverse = normal_parts(m_ref[at, :])
            grad = back[at, :]
            dgain_ref[...] = dgain_ref[...] + jnp.sum(grad * normal, axis=0, keepdims=True)
            grad = grad * gain_ref[...]
            mean = jnp.mean(grad, axis=1, keepdims=True)
            along = jnp.mean(grad * normal, axis=1, keepdims=True)
            dm_ref[at, :] = g_ref[at, :] + inverse * (grad - mean - normal * along)

        pieces_of(rows, piece, finish)


def feed_backward(upstream, middle, gain, hidden_values, expand, reduce):
    rows, width = middle.shape
    hidden = hidden_units(expand)
    block, piece = (512, rows) if rows <= 512 else (256, 256)
    whole = lambda j: (0, 0)
    once = pl.Buffered(1)
    dm, dgain, dexpand, dreduce = pl.pallas_call(
        partial(backward_kernel, min(piece, rows)),
        grid=(hidden // block,),
        in_specs=[
            pl.BlockSpec((rows, width), whole, pipeline_mode=once),
            pl.BlockSpec((rows, width), whole, pipeline_mode=once),
            pl.BlockSpec((1, width), whole),
            pl.BlockSpec((rows, block), lambda j: (0, j)),
            *weight_specs(expand, reduce, block),
        ],
        out_specs=[
            pl.BlockSpec((rows, width), whole, pipeline_mode=once),
            pl.BlockSpec((1, width), whole),
            pl.BlockSpec((width, block), lambda j: (0, j)),
            pl.BlockSpec((block, width), lambda j: (j, 0)),
        ],
        out_shape=[
            jax.ShapeDtypeStruct((rows, width), jnp.float32),
            jax.ShapeDtypeStruct((1, width), jnp.float32),
            jax.ShapeDtypeStruct((width, hidden), jnp.float32),
            jax.ShapeDtypeStruct((hidden, width), jnp.float32),
        ],
        scratch_shapes=[
            VMEM((rows, 3 * width), NARROW),
            VMEM((width, rows), NARROW),
            VMEM((width, rows), NARROW),
            VMEM((width, rows), NARROW),
            VMEM((width, rows), NARROW),
            VMEM((rows, block), NARROW),
            VMEM((rows, block), NARROW),
            VMEM((rows, block), NARROW),
            VMEM((rows, block), NARROW),
            VMEM((rows, width), jnp.float32),
        ],
        compiler_params=pltpu.CompilerParams(vmem_limit_bytes=56 << 20),
        cost_estimate=pl.CostEstimate(
            flops=24 * rows * width * hidden, bytes_accessed=4 * rows * hidden, transcendentals=0
        ),
        name="feed_backward",
    )(upstream, middle, gain.reshape(1, width), hidden_values, expand, reduce)
    return dm, dgain[0], dexpand, dreduce


GATHER_TARGET = 60000
SCATTER_TARGET = 26000


precise = lax.Precision.HIGH
everywhere = ("dp", "fsdp")


def product(operand, factor):
    return jnp.dot(operand, factor, precision=precise, preferred_element_type=jnp.float32)


def transposed_left(operand, factor):
    return lax.dot_general(
        operand,
        factor,
        (((0,), (0,)), ((), ())),
        precision=precise,
        preferred_element_type=jnp.float32,
    )


def against(operand, factor):
    return lax.dot_general(
        operand,
        factor,
        (((1,), (1,)), ((), ())),
        precision=precise,
        preferred_element_type=jnp.float32,
    )


def normalize(values, gain_row):
    center = values - jnp.mean(values, axis=-1, keepdims=True)
    inverse = lax.rsqrt(jnp.mean(center * center, axis=-1, keepdims=True) + 1e-06)
    return center * inverse * gain_row


def position_table(length, breadth):
    half_width = breadth // 2
    indices = jnp.arange(length, dtype=jnp.float32)[:, None]
    frequency = jnp.exp(
        jnp.arange(half_width, dtype=jnp.float32) * (-math.log(10000.0) / half_width)
    )[None, :]
    angles = indices * frequency
    return jnp.concatenate([jnp.sin(angles), jnp.cos(angles)], axis=1)


def block_forward(states, gain_pair, matrices):
    first_norm, first_back = jax.vjp(normalize, states, gain_pair[0])
    packed = product(first_norm, matrices[0])
    mixture, logsum = attend_forward(packed)
    middle = states + product(mixture, matrices[1])
    result, hidden = feed_forward(middle, gain_pair[1], matrices[2], matrices[3])
    return result, (first_norm, first_back, packed, mixture, logsum, middle, hidden)


def block_backward(upstream, gain_pair, matrices, stored, beside, begins):
    first_norm, first_back, packed, mixture, logsum, middle, hidden = stored
    middle_grad, second_gain, expand_grad, reduce_grad = feed_backward(
        upstream, middle, gain_pair[1], hidden, matrices[2], matrices[3]
    )
    if begins:
        beside.begin([expand_grad, reduce_grad])
    middle_grad = beside.advance(middle_grad)
    merge_grad = transposed_left(mixture, middle_grad)
    mixture_grad = against(middle_grad, matrices[1])
    if begins:
        mixture_grad = beside.advance(mixture_grad)
    packed_grad = attend_backward(packed, mixture, logsum, mixture_grad)
    packed_grad = beside.advance(packed_grad)
    attend_grad = transposed_left(first_norm, packed_grad)
    states_part, first_gain = first_back(against(packed_grad, matrices[0]))
    gain_grads = jnp.stack([first_gain, second_gain])
    return (
        middle_grad + states_part,
        gain_grads,
        (attend_grad, merge_grad, expand_grad, reduce_grad),
    )


def collect(weights, collective_id):
    columns, rows = lax.axis_size("dp"), lax.axis_size("fsdp")
    if all(weight.shape[0] % 16 == 0 for weight in weights):
        wholes = gather(weights, columns, rows, collective_id, GATHER_TARGET)
        return [whole.reshape(-1, whole.shape[3]) for whole in wholes]
    return [
        lax.all_gather(
            lax.all_gather(weight, "dp", axis=1, tiled=True), "fsdp", axis=0, tiled=True
        )
        for weight in weights
    ]


def spread(gradients, small, collective_id):
    columns, rows = lax.axis_size("dp"), lax.axis_size("fsdp")
    if all(gradient.shape[0] % (rows * 16) == 0 for gradient in gradients):
        wholes = [
            gradient.reshape(4, rows // 4, gradient.shape[0] // rows, gradient.shape[1])
            for gradient in gradients
        ]
        return scatter(wholes, small, columns, rows, collective_id, SCATTER_TARGET)
    parts = [
        lax.psum_scatter(
            lax.psum_scatter(gradient, "fsdp", scatter_dimension=0, tiled=True),
            "dp",
            scatter_dimension=1,
            tiled=True,
        )
        for gradient in gradients
    ]
    return parts, (None if small is None else lax.psum(small, everywhere))


def exchange_steps(columns, rows, near_first):
    def bits(size):
        return [1 << place for place in reversed(range(size.bit_length() - 1))]

    across = [("dp", bit, 0) for bit in bits(columns) if bit > 1]
    far = [("fsdp", bit, 2) for bit in bits(rows) if bit >= rows // 4]
    near = [("fsdp", bit, 3) for bit in bits(rows) if bit < rows // 4]
    return near + across + far if near_first else across + near + far


class Beside:
    def __init__(self):
        self.views, self.steps = [], []

    def begin(self, gradients):
        columns, rows = lax.axis_size("dp"), lax.axis_size("fsdp")
        for place, gradient in enumerate(gradients):
            height, width = gradient.shape
            share = width // columns
            panels = jnp.stack(
                [gradient[:, start : start + share] for start in range(0, width, share)]
            )
            self.views.append(
                panels.reshape(columns // 2, 2, 4, rows // 4, height // rows, share)
            )
            self.steps.append([("dp", 1, 1)] + exchange_steps(columns, rows, place % 2 == 0))

    def divided(self, place, upper, axis):
        view = self.views[place]
        half = view.shape[axis] // 2
        keep = lax.dynamic_slice_in_dim(view, upper * half, half, axis=axis)
        return keep, lax.dynamic_slice_in_dim(view, (1 - upper) * half, half, axis=axis)

    def advance(self, main):
        if not self.steps[0]:
            return main
        sent, kept, steps = [], [], [steps.pop(0) for steps in self.steps]
        for place, (name, bit, axis) in enumerate(steps):
            upper = jnp.bitwise_and(lax.axis_index(name) // bit, 1)
            keep, send = self.divided(place, upper, axis)
            sent.append(send)
            kept.append(keep)
        main, sent = lax.optimization_barrier((main, sent))
        self.views = [
            keep
            + lax.ppermute(
                send, name, [(place, place ^ bit) for place in range(lax.axis_size(name))]
            )
            for send, keep, (name, bit, _) in zip(sent, kept, steps)
        ]
        return main

    def finish(self):
        while self.steps[0]:
            self.advance(jnp.zeros((), jnp.float32))
        return [view.reshape(view.shape[4:]) for view in self.views]


def collect_beside(weights):
    columns, rows = lax.axis_size("dp"), lax.axis_size("fsdp")
    attend, merge, expand, reduce = weights
    padded = jnp.pad(merge, ((0, 0), (0, attend.shape[1] - merge.shape[1])))
    both = lax.all_gather(jnp.concatenate([attend, padded], axis=0), everywhere, axis=0)

    def panels(blocks):
        return blocks.reshape(columns, rows * blocks.shape[1], blocks.shape[2])

    def whole(blocks):
        return jnp.concatenate(list(panels(blocks)), axis=1)

    height = expand.shape[0]
    beside = [reduce[start : start + height] for start in range(0, reduce.shape[0], height)]
    stretches = jnp.concatenate(beside, axis=1)
    if reduce.shape[1] % 128 == 0 and stretches.shape == expand.shape and len(beside) == columns:
        rest = lax.all_gather(jnp.concatenate([expand, stretches], axis=0), everywhere, axis=0)
        expand = reduce = rest.reshape(columns, rows, 2 * height, expand.shape[1])
    else:
        expand, reduce = (
            whole(lax.all_gather(weight, everywhere, axis=0)) for weight in (expand, reduce)
        )
    return [
        whole(both[:, : attend.shape[0]]),
        whole(both[:, attend.shape[0] :, : merge.shape[1]]),
        expand,
        reduce,
    ]


def pack_small(arrays):
    flat = jnp.concatenate([array.reshape(-1) for array in arrays])
    size = -(-flat.shape[0] // 1024) * 1024
    return jnp.pad(flat, (0, size - flat.shape[0])).reshape(-1, 128)


def unpack_small(packed, arrays):
    flat, start, out = packed.reshape(-1), 0, []
    for array in arrays:
        out.append(flat[start : start + array.size].reshape(array.shape))
        start += array.size
    return out


def place(choice, values):
    high = lax.reduce_precision(values, 8, 7)
    low = values - high
    wide = choice.astype(jnp.bfloat16)
    return jnp.dot(
        wide, high.astype(jnp.bfloat16), preferred_element_type=jnp.float32
    ) + jnp.dot(wide, low.astype(jnp.bfloat16), preferred_element_type=jnp.float32)


def local(
    tokens,
    sensor_tag,
    block_dest,
    block_order,
    sensor_table,
    encoder_gains,
    encoder_attend,
    encoder_merge,
    encoder_expand,
    encoder_reduce,
    bridge,
    mask_token,
    decoder_gains,
    decoder_attend,
    decoder_merge,
    decoder_expand,
    decoder_reduce,
    cotangent,
):
    groups = lax.axis_size("fsdp")
    visible = tokens.shape[0]
    capacity = 2 * visible // groups
    length = block_order.shape[1]
    breadth = mask_token.shape[0]
    destination = block_dest[:, 0]
    chooser = (destination[:, None] == jnp.arange(groups, dtype=jnp.int32)[None, :]).astype(
        jnp.int32
    )
    tallies = jnp.zeros((16, 128), jnp.float32)
    tallies = tallies.at[0, :groups].set(jnp.sum(chooser, axis=0).astype(jnp.float32))
    expand, attend, reduce, merge, to_decoder, all_tallies = collect(
        [encoder_expand, encoder_attend, encoder_reduce, encoder_merge, bridge, tallies], 1
    )
    encoder_set = [attend, merge, expand, reduce, to_decoder]
    mine = all_tallies.reshape(groups, 16, -1, 128)[:, 0]
    mine = lax.dynamic_index_in_dim(mine, lax.axis_index("dp"), axis=1, keepdims=False)
    arrived_tallies = lax.dynamic_slice_in_dim(mine, lax.axis_index("fsdp"), 1, axis=1)
    later = lax.optimization_barrier((decoder_expand, decoder_reduce, encoder_set[4]))
    decoder_set = collect_beside([decoder_attend, decoder_merge, later[0], later[1]])
    tag_row = (
        sensor_tag[:, None] == jnp.arange(sensor_table.shape[0], dtype=jnp.int32)[None, :]
    ).astype(jnp.float32)
    initial = tokens + product(tag_row, sensor_table)
    encoded, encoder_kept = block_forward(initial, encoder_gains, encoder_set)
    projected = product(encoded, encoder_set[4])
    ranking = jnp.sum((jnp.cumsum(chooser, axis=0) - chooser) * chooser, axis=1)
    slot_index = destination * capacity + ranking
    select = (
        slot_index[None, :] == jnp.arange(groups * capacity, dtype=jnp.int32)[:, None]
    ).astype(jnp.float32)
    outgoing = place(select, projected).reshape(groups, capacity, breadth)
    arrived = lax.all_to_all(outgoing, "fsdp", split_axis=0, concat_axis=0, tiled=True)
    present = (jnp.arange(capacity, dtype=jnp.float32)[None, :] < arrived_tallies).reshape(-1)
    ordering = block_order[0, : groups * capacity]
    placing = (
        (ordering[None, :] == jnp.arange(length, dtype=jnp.int32)[:, None]) & present[None, :]
    ).astype(jnp.float32)
    covered = jnp.sum(placing, axis=1, keepdims=True)
    filled = (
        place(placing, arrived.reshape(groups * capacity, breadth))
        + (1.0 - covered) * mask_token
        + position_table(length, breadth)
    )
    decoded, decoder_kept = block_forward(filled, decoder_gains, decoder_set)
    beside = Beside()
    filled_grad, decoder_gain_grad, decoder_grads = block_backward(
        cotangent, decoder_gains, decoder_set, decoder_kept, beside, True
    )
    mask_grad = jnp.sum((1.0 - covered) * filled_grad, axis=0)
    arrived_grad = place(placing.T, filled_grad).reshape(groups, capacity, breadth)
    returned = lax.all_to_all(arrived_grad, "fsdp", split_axis=0, concat_axis=0, tiled=True)
    projected_grad = place(select.T, returned.reshape(groups * capacity, breadth))
    bridge_grad = transposed_left(encoded, projected_grad)
    encoded_grad = against(projected_grad, encoder_set[4])
    tokens_grad, encoder_gain_grad, encoder_grads = block_backward(
        encoded_grad, encoder_gains, encoder_set, encoder_kept, beside, False
    )
    table_grad = transposed_left(tag_row, jnp.sum(tokens_grad, axis=0, keepdims=True))
    small = (table_grad, encoder_gain_grad, mask_grad, decoder_gain_grad)
    packed_small = pack_small(small)
    spreads, total = spread(
        [
            decoder_grads[1],
            encoder_grads[1],
            decoder_grads[0],
            bridge_grad,
            encoder_grads[0],
            encoder_grads[2],
            encoder_grads[3],
        ],
        packed_small,
        3,
    )
    encoder_spread = [spreads[4], spreads[1], spreads[5], spreads[6], spreads[3]]
    expand_sum, reduce_sum = beside.finish()
    decoder_spread = [spreads[2], spreads[0], expand_sum, reduce_sum]
    summed = unpack_small(total, small)
    return (
        decoded,
        tokens_grad,
        summed[0],
        summed[1],
        encoder_spread[0],
        encoder_spread[1],
        encoder_spread[2],
        encoder_spread[3],
        encoder_spread[4],
        summed[2],
        summed[3],
        decoder_spread[0],
        decoder_spread[1],
        decoder_spread[2],
        decoder_spread[3],
    )


def solution(mesh):
    in_specs = (
        P(("dp", "fsdp"), None),
        P(("dp", "fsdp")),
        P(("dp", "fsdp"), None),
        P(("dp", "fsdp"), None),
        P(),
        P(),
        P("fsdp", "dp"),
        P("fsdp", "dp"),
        P("fsdp", "dp"),
        P("fsdp", "dp"),
        P("fsdp", "dp"),
        P(),
        P(),
        P("fsdp", "dp"),
        P("fsdp", "dp"),
        P("fsdp", "dp"),
        P("fsdp", "dp"),
        P(("dp", "fsdp"), None),
    )
    out_specs = (
        P(("dp", "fsdp"), None),
        P(("dp", "fsdp"), None),
        P(),
        P(),
        P("fsdp", "dp"),
        P("fsdp", "dp"),
        P("fsdp", "dp"),
        P("fsdp", "dp"),
        P("fsdp", "dp"),
        P(),
        P(),
        P("fsdp", "dp"),
        P("fsdp", "dp"),
        P("fsdp", "dp"),
        P("fsdp", "dp"),
    )
    return jax.shard_map(local, mesh=mesh, in_specs=in_specs, out_specs=out_specs, check_vma=False)
```
